32 devices in a mesh: wide: 8 (over y, x, core), narrow: 4 (over z).
Axes of the slice: x: 2, y: 2, z: 4, core: 2. Of those that a mesh axis runs over, the one named last changes fastest.
Arguments:
- tokens: bfloat16 [2, 4, 2048, 960], P(None, 'narrow', 'wide'), may hold values from -6 to 6
- lengths: int32 [2, 4, 4], P(None, 'narrow'), may hold values from 1 to 1024, 2048 in all within a row
- block_plan: int32 [2, 4, 16], P(None, 'narrow'), may hold values from 0 to 15, each once within a row
- attn_gain: float32 [960], replicated, may hold values from 0.1 to 1.9
- w_query: bfloat16 [960, 960], P('wide'), may hold values from -0.25 to 0.25
- w_key: bfloat16 [960, 320], P('wide'), may hold values from -0.25 to 0.25
- w_value: bfloat16 [960, 320], P('wide'), may hold values from -0.1875 to 0.1875
- w_out: bfloat16 [960, 960], P('wide'), may hold values from -1 to 1
- ffn_gain: float32 [960], replicated, may hold values from 0.1 to 1.9
- w_gate: bfloat16 [960, 2560], P('wide'), may hold values from -0.1875 to 0.1875
- w_up: bfloat16 [960, 2560], P('wide'), may hold values from -0.1875 to 0.1875
- w_down: bfloat16 [2560, 960], P('wide'), may hold values from -0.125 to 0.125
- cotangent: bfloat16 [2, 4, 2048, 960], P(None, 'narrow', 'wide'), may hold values from -6 to 6
Outputs:
- layer_out: bfloat16 [2, 4, 2048, 960], P(None, 'narrow', 'wide')
- grad_tokens: float32 [2, 4, 2048, 960], P(None, 'narrow', 'wide')
- grad_attn_gain: float32 [960], replicated
- grad_query: float32 [960, 960], P('wide')
- grad_key: float32 [960, 320], P('wide')
- grad_value: float32 [960, 320], P('wide')
- grad_out: float32 [960, 960], P('wide')
- grad_ffn_gain: float32 [960], replicated
- grad_gate: float32 [960, 2560], P('wide')
- grad_up: float32 [960, 2560], P('wide')
- grad_down: float32 [2560, 960], P('wide')
The draws below stay inside these ranges and needn't reach their ends.
Inputs may be any that keep to these rules, and one draw needn't show every extreme that they name: In each row the 4 lengths add up to 2048, the documents follow one another from position 0, and the longest is exactly 1024 tokens. For each micro-batch and row the plan names every block of the row once: slots j * 128 to j * 128 + 127 hold the tokens from position block_plan[j] * 128 on.
All inputs are finite; a program needn't handle non-finite values.
Results may differ from the reference program's by a relative error of at most 0.023.
Values may be sent and summed in bfloat16 or wider, within the bound.
A program may use at most 256 MiB of HBM per device.

```python
import math
import jax
import jax.numpy as jnp
import numpy as np
from jax import lax

D = 960
HEADS = 15
KVHEADS = 5
HDIM = 64
FF = 2560
BLOCK = 128
DOCS = 4
MB = 2
KD = 320
ROW = 2048
BLOCKS = 16
ROWS = 4
LONGEST = 1024


def shard_levels(rng, extent, shards, least, high):
    def one(dim, shards_of):
        heights = jax.random.uniform(jax.random.fold_in(jax.random.fold_in(rng, 6), dim), (shards_of,), jnp.float32, least / len(shards), high / len(shards))
        return jnp.repeat(jnp.exp(heights), extent[dim] // shards_of).reshape((-1,) + (1,) * (len(extent) - dim - 1))

    loudness = one(*shards[0])
    for cut in shards[1:]:
        loudness = loudness * one(*cut)
    return loudness


def length_profile(number_of, total, reach, slope):
    loads = [(1 << 20) // math.isqrt(grade ** slope) + 1 for grade in range(2, number_of + 1)]
    rest, counts = total - reach - (number_of - 1), [1] * (number_of - 1)
    while rest > 0:
        movable = [i for i in range(number_of - 1) if counts[i] < reach]
        whole, remaining = sum([loads[i] for i in movable]), rest
        for i in movable:
            addition = min(reach - counts[i], max(1, remaining * loads[i] // whole), rest)
            counts[i] = counts[i] + addition
            rest = rest - addition
    return np.array([reach] + counts)


def uneven_parts(own_key, number_of, total, most, skew):
    if number_of == 2:
        one = jax.random.randint(own_key, (), max(1, total - most), min(most, total - 1) + 1)
        return jnp.stack([one, total - one])
    sizes = jnp.asarray(length_profile(number_of, total, most, skew), jnp.int32)
    couples = (number_of - 1) // 2
    source_of, taker = sizes[1:1 + 2 * couples:2], sizes[2:2 + 2 * couples:2]
    room = jnp.minimum(source_of - 1, most - taker)
    moved = jax.random.randint(jax.random.fold_in(own_key, 1), (couples,), 0, 1 << 20) % (room + 1)
    sizes = sizes.at[1:1 + 2 * couples:2].set(source_of - moved).at[2:2 + 2 * couples:2].set(taker + moved)
    return sizes[jax.random.permutation(jax.random.fold_in(own_key, 2), number_of)]


def normal_values(stream_key, extent, scale, limit, pieces=(), kind=jnp.bfloat16):
    level = shard_levels(stream_key, extent, pieces, -0.22, 0.18) if pieces else 1.0
    drawn = jax.random.normal(stream_key, extent, jnp.float32) * scale * level
    return jnp.minimum(jnp.maximum(drawn, -limit), limit).astype(kind)


def setup_inputs(seed: int = 0) -> dict:
    key_list = jax.random.split(jax.random.key(seed), 14)
    return {
        "tokens": normal_values(key_list[0], (MB, ROWS, ROW, D), 1.0, 6.0, ((1, 4), (2, 8))),
        "lengths": jax.vmap(lambda own: uneven_parts(own, DOCS, ROW, LONGEST, 2))(jax.random.split(key_list[1], MB * ROWS)).reshape((MB, ROWS, DOCS)).astype(jnp.int32),
        "block_plan": jax.vmap(lambda own: jax.random.permutation(own, BLOCKS))(jax.random.split(key_list[2], MB * ROWS)).reshape((MB, ROWS, BLOCKS)).astype(jnp.int32),
        "attn_gain": jnp.clip(1.0 + 0.18 * jax.random.normal(key_list[3], (D,), jnp.float32), 0.1, 1.9),
        "w_query": normal_values(key_list[4], (D, D), (D // 2) ** -0.5, 0.25, ((0, 8),)),
        "w_key": normal_values(key_list[5], (D, KD), (D // 2) ** -0.5, 0.25, ((0, 8),)),
        "w_value": normal_values(key_list[6], (D, KD), D ** -0.5, 0.1875, ((0, 8),)),
        "w_out": normal_values(key_list[7], (D, D), (D // 32) ** -0.5, 1.0, ((0, 8),)),
        "ffn_gain": jnp.clip(1.0 + 0.18 * jax.random.normal(key_list[8], (D,), jnp.float32), 0.1, 1.9),
        "w_gate": normal_values(key_list[9], (D, FF), D ** -0.5, 0.1875, ((0, 8),)),
        "w_up": normal_values(key_list[10], (D, FF), D ** -0.5, 0.1875, ((0, 8),)),
        "w_down": normal_values(key_list[11], (FF, D), FF ** -0.5, 0.125, ((0, 8),)),
        "cotangent": normal_values(key_list[12], (MB, ROWS, ROW, D), 1.0, 6.0, ((1, 4), (2, 8))),
    }


EPS = 1e-05
ROPE_BASE = 100000.0
NEG_FILL = -1e+30

@jax.custom_vjp
def low(v):
    return lax.optimization_barrier(v.astype(jnp.bfloat16)).astype(jnp.float32)

@jax.custom_vjp
def low_back(v):
    return v

def low_keep(v):
    return (low(v), None)

def low_pass(kept, grad):
    return (grad,)

def back_keep(v):
    return (v, None)

def back_low(kept, grad):
    return (low(grad),)
low.defvjp(low_keep, low_pass)
low_back.defvjp(back_keep, back_low)

def precise(source, target):
    return jnp.dot(source, target, precision=lax.Precision.HIGHEST, preferred_element_type=jnp.float32)

def places(block_plan_row, length_row, block_size):
    in_block = jnp.arange(block_size, dtype=jnp.int32)
    position = (block_plan_row.astype(jnp.int32)[:, None] * block_size + in_block[None, :]).reshape(-1)
    sizes_int = length_row.astype(jnp.int32)
    doc_ends = jnp.cumsum(sizes_int).astype(jnp.int32)
    is_after = position[:, None] >= doc_ends[None, :]
    document = lax.optimization_barrier(jnp.sum(is_after.astype(jnp.int32), axis=1)).astype(jnp.int32)
    doc_begin = lax.optimization_barrier(jnp.sum(jnp.where(is_after, sizes_int[None, :], 0), axis=1)).astype(jnp.int32)
    return (position, document, (position - doc_begin).astype(jnp.int32))

def rotary_tables(in_document):
    half_dim = HDIM // 2
    frequency = ROPE_BASE ** (-2.0 * jnp.arange(half_dim, dtype=jnp.float32) / HDIM)
    angles = in_document.astype(jnp.float32)[:, None] * frequency[None, :]
    angles = jnp.concatenate([angles, angles], axis=1)
    return (jnp.cos(angles), jnp.sin(angles))

def rotate(operand, cosine_table, sine_table):
    row_total = operand.shape[0]
    per_head = operand.reshape(row_total, -1, HDIM)
    half_dim = HDIM // 2
    turned = jnp.concatenate([-per_head[..., half_dim:], per_head[..., :half_dim]], axis=-1)
    return (per_head * cosine_table[:, None, :] + turned * sine_table[:, None, :]).reshape(row_total, -1)

def rms_norm(operand, gain_vec):
    return operand * lax.rsqrt(lax.optimization_barrier(jnp.mean(operand * operand, axis=-1, keepdims=True)) + EPS) * gain_vec

def swiglu(gate_lin, up_lin):
    return gate_lin / (1.0 + jnp.exp(-gate_lin)) * up_lin

def attention_row(query, key_rows, value_rows, position, document):
    row_total = query.shape[0]
    query_block = min(512, row_total)
    score_scale = HDIM ** (-0.5)
    group_size = HEADS // KVHEADS
    queries = query.reshape(row_total // query_block, query_block, KVHEADS, group_size, HDIM)
    keys_all = key_rows.reshape(row_total, KVHEADS, HDIM)
    values_all = value_rows.reshape(row_total, KVHEADS, HDIM)

    def one_block(element):
        block_query, block_position, block_document = element
        scores = low_back(jnp.einsum('qkgd,tkd->kgqt', block_query, keys_all, precision=lax.Precision.HIGHEST) * score_scale)
        allowed = (block_document[:, None] == document[None, :]) & (position[None, :] <= block_position[:, None])
        masked = jnp.where(allowed[None, None], scores, NEG_FILL)
        row_top = lax.optimization_barrier(jnp.max(masked, axis=-1, keepdims=True))
        raw_weights = jnp.where(allowed[None, None], jnp.exp(masked - row_top), 0.0)
        soft_weights = low(raw_weights / lax.optimization_barrier(jnp.sum(raw_weights, axis=-1, keepdims=True)))
        return jnp.einsum('kgqt,tkd->qkgd', soft_weights, values_all, precision=lax.Precision.HIGHEST)
    blocks_out = lax.map(jax.checkpoint(one_block), (queries, position.reshape(-1, query_block), document.reshape(-1, query_block)))
    return blocks_out.reshape(row_total, -1)

def layer_row(inputs, position, document, in_document, params):
    attn_gain, w_query, w_key, w_value, w_out, ffn_gain, w_gate, w_up, w_down = params
    cosine_table, sine_table = rotary_tables(in_document)
    normed = low(rms_norm(inputs, attn_gain))
    query = low(rotate(low_back(precise(normed, w_query)), cosine_table, sine_table))
    key_rot = low(rotate(low_back(precise(normed, w_key)), cosine_table, sine_table))
    value_rows = low(low_back(precise(normed, w_value)))
    attended = low(low_back(attention_row(query, key_rot, value_rows, position, document)))
    residual = inputs + low_back(precise(attended, w_out))
    normed_two = low(rms_norm(residual, ffn_gain))
    gate_lin = low_back(precise(normed_two, w_gate))
    up_lin = low_back(precise(normed_two, w_up))
    hidden = low(swiglu(gate_lin, up_lin))
    return residual + low_back(precise(hidden, w_down))

def reference(tokens, lengths, block_plan, attn_gain, w_query, w_key, w_value, w_out, ffn_gain, w_gate, w_up, w_down, cotangent):
    row_count = MB * ROWS
    row_inputs = tokens.reshape(row_count, ROW, D).astype(jnp.float32)
    position, document, in_document = jax.vmap(lambda plan_row, length_row: places(plan_row, length_row, BLOCK))(block_plan.reshape(row_count, BLOCKS), lengths.reshape(row_count, DOCS))
    params = tuple((weight.astype(jnp.float32) for weight in (attn_gain, w_query, w_key, w_value, w_out, ffn_gain, w_gate, w_up, w_down)))

    def whole(row_values, param_values):

        def advance(carry, element):
            inputs, place_row, doc_row, local_row = element
            return (carry, layer_row(inputs, place_row, doc_row, local_row, param_values))
        return lax.scan(advance, jnp.zeros((), jnp.float32), (row_values, position, document, in_document))[1]
    results, pull = jax.vjp(whole, row_inputs, params)
    grad_rows, grad_params = pull(cotangent.reshape(row_count, ROW, D).astype(jnp.float32))
    return (results.reshape(MB, ROWS, ROW, D).astype(jnp.bfloat16), grad_rows.reshape(MB, ROWS, ROW, D), grad_params[0], grad_params[1], grad_params[2], grad_params[3], grad_params[4], grad_params[5], grad_params[6], grad_params[7], grad_params[8])
```

```python
import functools

import jax
import jax.numpy as jnp
from jax import lax
from jax.experimental import pallas as pl
from jax.experimental.pallas import tpu as pltpu
from jax.sharding import PartitionSpec as P

HDIM = 64
BLOCK = 128
EPS = 1e-05
ROPE_BASE = 100000.0
NEG_FILL = -1e30
F32 = jnp.float32
BF16 = jnp.bfloat16
VMEM_LIMIT = 56 * 1024 * 1024


def dot(a, b, ca, cb):
    return lax.dot_general(a, b, (((ca,), (cb,)), ((), ())), preferred_element_type=F32)


def live_mask(qpos, start, p):
    kpos = p * BLOCK + lax.broadcasted_iota(jnp.int32, (BLOCK, BLOCK), 0)
    return (kpos <= qpos) & (kpos >= start)


def fwd_kernel(groups, share, info, kvat, q_ref, start_ref, kv_ref, o_ref, lse_ref, qs, m_s, l_s, acc):
    i = pl.program_id(0)
    lo, b = info[0, i], info[1, i]
    lanes = share * BLOCK
    for g in range(groups):
        for h in range(share):
            at = (g * share + h) * HDIM
            qs[g, :, h * BLOCK : (h + 1) * BLOCK] = q_ref[at : at + HDIM, :]
    m_s[...] = jnp.full_like(m_s, NEG_FILL)
    l_s[...] = jnp.zeros_like(l_s)
    acc[...] = jnp.zeros_like(acc)
    qpos = b * BLOCK + lax.broadcasted_iota(jnp.int32, (1, BLOCK), 1)
    start = start_ref[...]

    def step(t, carry):
        p = b - t
        at = kvat[p]
        ok = live_mask(qpos, start, p)
        ok = jnp.concatenate([ok] * share, axis=1)
        for g in range(groups):
            k_t = kv_ref[at, g * HDIM : (g + 1) * HDIM, :]
            v_t = kv_ref[at, (groups + g) * HDIM : (groups + g + 1) * HDIM, :]
            s = jnp.where(ok, dot(k_t, qs[g], 0, 0), NEG_FILL)
            m_old = m_s[g]
            m_new = jnp.maximum(m_old, jnp.max(s, axis=0, keepdims=True))
            w = jnp.exp(s - m_new)
            alpha = jnp.exp(m_old - m_new)
            l_s[g] = l_s[g] * alpha + jnp.sum(w, axis=0, keepdims=True)
            acc[g] = acc[g] * alpha + dot(v_t, w.astype(BF16), 1, 0)
            m_s[g] = m_new
        return carry

    lax.fori_loop(0, b - lo + 1, step, 0)
    for g in range(groups):
        total = l_s[g]
        out = (acc[g] / total).astype(BF16)
        for h in range(share):
            at = (g * share + h) * HDIM
            o_ref[at : at + HDIM, :] = out[:, h * BLOCK : (h + 1) * BLOCK]
        lse_ref[0, g : g + 1, :] = m_s[g] + jnp.log(total)


def attention_fwd(info, kvat, q_t, start, kv, mb):
    width, tokens = q_t.shape
    nb, kvw, _ = kv.shape
    groups = kvw // HDIM // 2
    share = width // HDIM // groups
    nq = info.shape[1]
    lanes = share * BLOCK
    return pl.pallas_call(
        functools.partial(fwd_kernel, groups, share),
        grid_spec=pltpu.PrefetchScalarGridSpec(
            num_scalar_prefetch=2,
            grid=(nq,),
            in_specs=[
                pl.BlockSpec((width, BLOCK), lambda i, *_: (0, mb * nq + i)),
                pl.BlockSpec((1, BLOCK), lambda i, *_: (0, mb * nq + i)),
                pl.BlockSpec((nb, kvw, BLOCK), lambda i, *_: (0, 0, 0)),
            ],
            out_specs=[
                pl.BlockSpec((width, BLOCK), lambda i, *_: (0, i)),
                pl.BlockSpec((1, groups, lanes), lambda i, *_: (i, 0, 0)),
            ],
            scratch_shapes=[
                pltpu.VMEM((groups, HDIM, lanes), BF16),
                pltpu.VMEM((groups, 1, lanes), F32),
                pltpu.VMEM((groups, 1, lanes), F32),
                pltpu.VMEM((groups, HDIM, lanes), F32),
            ],
        ),
        out_shape=[
            jax.ShapeDtypeStruct((width, nq * BLOCK), BF16),
            jax.ShapeDtypeStruct((nq, groups, lanes), F32),
        ],
        compiler_params=pltpu.CompilerParams(vmem_limit_bytes=VMEM_LIMIT),
        cost_estimate=pl.CostEstimate(
            flops=int(5e9), bytes_accessed=int(4e6), transcendentals=int(4e6)
        ),
        name="attention_fwd",
    )(info, kvat, q_t, start, kv)


def bwd_kernel(
    groups, share, info, kvat, q_ref, do_ref, o_ref, lse_ref, start_ref, cos_ref, sin_ref, kv_ref,
    dq_ref, own_ref, send_ref, qs, dos, delta, dq, dkv,
):
    i = pl.program_id(0)
    lo, b = info[0, i], info[1, i]

    @pl.when(i == 0)
    def _():
        dkv[...] = jnp.zeros_like(dkv)

    for g in range(groups):
        for h in range(share):
            at = (g * share + h) * HDIM
            cols = slice(h * BLOCK, (h + 1) * BLOCK)
            d_out = do_ref[at : at + HDIM, :]
            qs[g, :, cols] = q_ref[at : at + HDIM, :]
            dos[g, :, cols] = d_out
            delta[g, :, cols] = jnp.sum(
                d_out.astype(F32) * o_ref[at : at + HDIM, :].astype(F32), axis=0, keepdims=True
            )
    dq[...] = jnp.zeros_like(dq)
    qpos = b * BLOCK + lax.broadcasted_iota(jnp.int32, (1, BLOCK), 1)
    start = start_ref[...]

    def step(t, carry):
        p = b - t
        at = kvat[p]
        ok = live_mask(qpos, start, p)
        ok = jnp.concatenate([ok] * share, axis=1)
        for g in range(groups):
            krows = slice(g * HDIM, (g + 1) * HDIM)
            vrows = slice((groups + g) * HDIM, (groups + g + 1) * HDIM)
            k_t = kv_ref[at, krows, :]
            v_t = kv_ref[at, vrows, :]
            s = jnp.where(ok, dot(k_t, qs[g], 0, 0), NEG_FILL)
            w = jnp.exp(s - lse_ref[0, g : g + 1, :])
            dw = dot(v_t, dos[g], 0, 0)
            ds = (w * (dw - delta[g])).astype(BF16)
            dq[g] += dot(k_t, ds, 1, 0)
            dkv[at, krows, :] += dot(qs[g], ds, 1, 1)
            dkv[at, vrows, :] += dot(dos[g], w.astype(BF16), 1, 1)
        return carry

    lax.fori_loop(0, b - lo + 1, step, 0)
    cos, sin = cos_ref[...], sin_ref[...]
    half = HDIM // 2
    for g in range(groups):
        for h in range(share):
            at = (g * share + h) * HDIM
            one = dq[g, :half, h * BLOCK : (h + 1) * BLOCK] * HDIM**-0.5
            two = dq[g, half:, h * BLOCK : (h + 1) * BLOCK] * HDIM**-0.5
            dq_ref[at : at + half, :] = (one * cos + two * sin).astype(BF16)
            dq_ref[at + half : at + HDIM, :] = (two * cos - one * sin).astype(BF16)

    @pl.when(i == pl.num_programs(0) - 1)
    def _():
        n = own_ref.shape[0]
        own_ref[...] = dkv[:n].astype(BF16)
        send_ref[...] = dkv[n:].astype(BF16)


def attention_bwd(info, kvat, q_t, do_t, o_t, lse, start, cos_t, sin_t, kv, mb):
    width = q_t.shape[0]
    nb, kvw, _ = kv.shape
    groups = kvw // HDIM // 2
    share = width // HDIM // groups
    nq = info.shape[1]
    lanes = share * BLOCK
    tok = lambda rows: pl.BlockSpec((rows, BLOCK), lambda i, *_: (0, mb * nq + i))
    return pl.pallas_call(
        functools.partial(bwd_kernel, groups, share),
        grid_spec=pltpu.PrefetchScalarGridSpec(
            num_scalar_prefetch=2,
            grid=(nq,),
            in_specs=[
                tok(width),
                tok(width),
                tok(width),
                pl.BlockSpec((1, groups, lanes), lambda i, *_: (i, 0, 0)),
                tok(1),
                tok(HDIM // 2),
                tok(HDIM // 2),
                pl.BlockSpec((nb, kvw, BLOCK), lambda i, *_: (0, 0, 0)),
            ],
            out_specs=[
                pl.BlockSpec((width, BLOCK), lambda i, *_: (0, i)),
                pl.BlockSpec((nb // 2, kvw, BLOCK), lambda i, *_: (0, 0, 0)),
                pl.BlockSpec((nb // 2, kvw, BLOCK), lambda i, *_: (0, 0, 0)),
            ],
            scratch_shapes=[
                pltpu.VMEM((groups, HDIM, lanes), BF16),
                pltpu.VMEM((groups, HDIM, lanes), BF16),
                pltpu.VMEM((groups, 1, lanes), F32),
                pltpu.VMEM((groups, HDIM, lanes), F32),
                pltpu.VMEM((nb, kvw, BLOCK), F32),
            ],
        ),
        out_shape=[
            jax.ShapeDtypeStruct((width, nq * BLOCK), BF16),
            jax.ShapeDtypeStruct((nb // 2, kvw, BLOCK), BF16),
            jax.ShapeDtypeStruct((nb // 2, kvw, BLOCK), BF16),
        ],
        compiler_params=pltpu.CompilerParams(vmem_limit_bytes=VMEM_LIMIT),
        cost_estimate=pl.CostEstimate(
            flops=int(1e10), bytes_accessed=int(8e6), transcendentals=int(4e6)
        ),
        name="attention_bwd",
    )(info, kvat, q_t, do_t, o_t, lse, start, cos_t, sin_t, kv)


CORE, ALONG_X, ALONG_Y = 1, 2, 4


class Wide:
    def __init__(self, size):
        self.size = size
        self.at = lax.axis_index("wide")
        self.cube = size == 8

    def swap(self, a, bit):
        return lax.ppermute(a, "wide", [(i, i ^ bit) for i in range(self.size)])

    def pieces(self, own, first):
        other = ALONG_X + ALONG_Y - first
        got = {0: own, ALONG_X: self.swap(own, ALONG_X), ALONG_Y: self.swap(own, ALONG_Y)}
        got[ALONG_X + ALONG_Y] = self.swap(got[other], first)
        for m in list(got):
            got[m + CORE] = self.swap(got[m], CORE)
        return got

    def rows(self, own, first):
        if not self.cube:
            return lax.all_gather(own, "wide", axis=0, tiled=True)
        rows, cols = own.shape
        whole = jnp.zeros((self.size, rows, cols), own.dtype)
        for m, piece in self.pieces(own, first).items():
            whole = lax.dynamic_update_slice(whole, piece[None], (self.at ^ m, 0, 0))
        return whole.reshape(self.size * rows, cols)

    def order(self, first):
        other = ALONG_X + ALONG_Y - first
        return [
            c * CORE + a * first + b * other for c in range(2) for a in range(2) for b in range(2)
        ]

    def ordered_rows(self, src_t, first):
        if not self.cube:
            return src_t
        each = src_t.shape[0] // self.size
        return jnp.concatenate(
            [
                lax.dynamic_slice_in_dim(src_t, (self.at ^ m) * each, each)
                for m in self.order(first)
            ]
        )

    def halve(self, own, bit):
        half = own.shape[0] // 2
        got = self.swap(own[half:], bit)
        return (own[:half].astype(F32) + got.astype(F32)).astype(BF16)

    def scatter_chips(self, own, first):
        return self.halve(self.halve(own, first), ALONG_X + ALONG_Y - first)

    def weight_sum(self, src_ord, target, target_dim, first):
        if not self.cube:
            return lax.psum_scatter(
                dot(src_ord, target, 1, target_dim).astype(BF16), "wide", scatter_dimension=0, tiled=True
            )
        half = src_ord.shape[0] // 2
        got = self.swap(dot(src_ord[half:], target, 1, target_dim).astype(BF16), CORE)
        own = (dot(src_ord[:half], target, 1, target_dim) + got.astype(F32)).astype(BF16)
        return self.scatter_chips(own, first)


def row_sum(part, size):
    if size != 4:
        return lax.psum(part, "narrow").astype(F32)
    add = lambda a, b: (a.astype(F32) + b.astype(F32)).astype(BF16)
    part = add(part, lax.ppermute(part, "narrow", [(0, 1), (3, 2)]))
    part = add(part, lax.ppermute(part, "narrow", [(1, 2), (2, 1)]))
    back = lax.ppermute(part, "narrow", [(1, 0), (2, 3)])
    at = lax.axis_index("narrow")
    return jnp.where((at == 1) | (at == 2), part, back).astype(F32)


def turn(v, cos, sin):
    heads = v.reshape(-1, 2, HDIM // 2, v.shape[1])
    one, two = heads[:, 0], heads[:, 1]
    return jnp.stack([one * cos - two * sin, two * cos + one * sin], axis=1).reshape(v.shape)


def turn_back(v, cos, sin):
    return turn(v, cos, -sin)


def shards(sizes, tokens, lengths, block_plan, attn_gain, w_query, w_key, w_value, w_out, ffn_gain,
           w_gate, w_up, w_down, cotangent):
    wide = Wide(sizes["wide"])
    n = wide.size
    micro, _, slots, width = tokens.shape
    total = micro * slots
    kd = w_key.shape[1]
    ff = w_gate.shape[1]
    nq = slots // BLOCK
    nb = nq * n

    plan = block_plan[:, 0]
    sizes_of = lengths[:, 0]
    docs = sizes_of.shape[1]
    upto = jnp.arange(docs)[:, None] >= jnp.arange(docs)[None, :]
    ends = jnp.sum(jnp.where(upto[None], sizes_of[:, None, :], 0), axis=2)
    own_plan = lax.dynamic_slice_in_dim(plan, wide.at * nq, nq, axis=1)
    position = own_plan[:, :, None] * BLOCK + jnp.arange(BLOCK, dtype=jnp.int32)
    start = jnp.sum(
        jnp.where(position[..., None] >= ends[:, None, None, :], sizes_of[:, None, None, :], 0), axis=3
    )
    info = jnp.stack([start[:, :, 0] // BLOCK, own_plan], axis=1)
    slot_block = jnp.arange(nb, dtype=jnp.int32)
    where_is = jnp.sum(
        jnp.where(plan[:, None, :] == slot_block[None, :, None], slot_block[None, None, :], 0), axis=2
    )
    start = start.reshape(1, total)
    local = position.reshape(1, total) - start
    frequency = ROPE_BASE ** (-2.0 * jnp.arange(HDIM // 2, dtype=F32) / HDIM)
    angles = frequency[:, None] * local.astype(F32)
    cos, sin = jnp.cos(angles), jnp.sin(angles)

    if wide.cube:
        kv_order = wide.order(ALONG_X)
        rank = sum(
            jnp.where((where_is // nq) ^ wide.at == m, r, 0) for r, m in enumerate(kv_order)
        )
        kvat = rank * nq + where_is % nq
    else:
        kvat = where_is

    x = tokens.reshape(total, width).astype(F32)
    ct = cotangent.reshape(total, width)

    g_query = wide.rows(w_query, ALONG_X)
    g_kv = wide.rows(jnp.concatenate([w_key, w_value], axis=1), ALONG_Y)
    g_out = wide.rows(w_out, ALONG_Y)
    g_gate = wide.rows(w_gate, ALONG_X)
    g_up = wide.rows(w_up, ALONG_Y)
    g_down = wide.rows(w_down, ALONG_X)

    rr1 = lax.rsqrt(jnp.mean(x * x, axis=1, keepdims=True) + EPS)
    xn = (x * rr1 * attn_gain).astype(BF16)
    kv_t = dot(g_kv, xn, 0, 1)
    key_t = turn(kv_t[:kd], cos, sin).astype(BF16)
    value_t = kv_t[kd:].astype(BF16)
    own_kv = jnp.concatenate([key_t, value_t]).reshape(2 * kd, micro, nq, BLOCK).transpose(1, 2, 0, 3)
    q_t = (turn(dot(g_query, xn, 0, 1), cos, sin).astype(BF16) * HDIM**-0.5).astype(BF16)

    kvs, outs, lses = [], [], []
    for mb in range(micro):
        if wide.cube:
            got = wide.pieces(own_kv[mb], ALONG_X)
            kv = jnp.concatenate([got[m] for m in kv_order])
        else:
            kv = lax.all_gather(own_kv[mb], "wide", axis=0, tiled=True)
        o_t, lse = attention_fwd(info[mb], kvat[mb], q_t, start, kv, mb)
        kvs.append(kv)
        outs.append(o_t)
        lses.append(lse)
    att_t = jnp.concatenate(outs, axis=1)

    res = x + dot(att_t, g_out, 0, 0)
    rr2 = lax.rsqrt(jnp.mean(res * res, axis=1, keepdims=True) + EPS)
    hn = (res * rr2 * ffn_gain).astype(BF16)
    gate = dot(g_gate, hn, 0, 1)
    up = dot(g_up, hn, 0, 1)
    sg = 1.0 / (1.0 + jnp.exp(-gate))
    hidden = (gate * sg * up).astype(BF16)
    out = (res + dot(hidden, g_down, 0, 0)).astype(BF16)

    first_down, first_out, first_q, first_kv = ALONG_X, ALONG_Y, ALONG_X, ALONG_Y
    s_down = wide.weight_sum(wide.ordered_rows(hidden, first_down), ct, 0, first_down)

    d_hidden = dot(g_down, ct, 1, 1)
    d_gate = (d_hidden * up * sg * (1.0 + gate * (1.0 - sg))).astype(BF16)
    d_up = (d_hidden * gate * sg).astype(BF16)
    hn_t = hn.T
    s_gate = wide.weight_sum(wide.ordered_rows(hn_t, ALONG_X), d_gate, 1, ALONG_X)
    s_up = wide.weight_sum(wide.ordered_rows(hn_t, ALONG_Y), d_up, 1, ALONG_Y)
    d_hn = dot(d_gate, g_gate, 0, 1) + dot(d_up, g_up, 0, 1)
    u = d_hn * ffn_gain
    d_res = (
        ct.astype(F32) + rr2 * u - res * rr2**3 * jnp.mean(u * res, axis=1, keepdims=True)
    )
    gain_two = jnp.sum(d_hn * res * rr2, axis=0)
    d_attn = d_res.astype(BF16)
    do_t = dot(g_out, d_attn, 1, 1).astype(BF16)
    s_out = wide.weight_sum(wide.ordered_rows(att_t, first_out), d_attn, 0, first_out)

    dqs, dkvs = [], []
    for mb in range(micro):
        dq_t, own, send = attention_bwd(
            info[mb], kvat[mb], q_t, do_t, outs[mb] if micro == 1 else att_t, lses[mb], start, cos, sin,
            kvs[mb], mb,
        )
        dqs.append(dq_t)
        if wide.cube:
            got = wide.swap(send, CORE)
            dkv = wide.scatter_chips((own.astype(F32) + got.astype(F32)).astype(BF16), ALONG_X)
        else:
            dkv = lax.psum_scatter(
                jnp.concatenate([own, send]), "wide", scatter_dimension=0, tiled=True
            )
        dkvs.append(dkv.transpose(1, 0, 2).reshape(2 * kd, slots))
    dq = jnp.concatenate(dqs, axis=1)
    dkv = jnp.concatenate(dkvs, axis=1)
    dk = turn_back(dkv[:kd].astype(F32), cos, sin).astype(BF16)
    dkv = jnp.concatenate([dk, dkv[kd:]])

    xn_t = xn.T
    s_query = wide.weight_sum(wide.ordered_rows(xn_t, first_q), dq, 1, first_q)
    s_kv = wide.weight_sum(wide.ordered_rows(xn_t, first_kv), dkv, 1, first_kv)

    d_xn = dot(dq, g_query, 0, 1) + dot(dkv, g_kv, 0, 1)
    u = d_xn * attn_gain
    grad_x = d_res + rr1 * u - x * rr1**3 * jnp.mean(u * x, axis=1, keepdims=True)
    gain_one = jnp.sum(d_xn * x * rr1, axis=0)
    gains = lax.psum(jnp.stack([gain_one, gain_two]), ("wide", "narrow"))

    over = functools.partial(row_sum, size=sizes["narrow"])
    s_down, s_gate, s_up, s_out = over(s_down), over(s_gate), over(s_up), over(s_out)
    s_query, s_kv = over(s_query), over(s_kv)
    shape = (micro, 1, slots, width)
    return (
        out.reshape(shape),
        grad_x.reshape(shape),
        gains[0],
        s_query,
        s_kv[:, :kd],
        s_kv[:, kd:],
        s_out,
        gains[1],
        s_gate,
        s_up,
        s_down,
    )


def solution(mesh):
    by_slot = P(None, "narrow", "wide", None)
    by_row = P(None, "narrow", None)
    split = P("wide", None)
    in_specs = (
        by_slot, by_row, by_row, P(), split, split, split, split, P(), split, split, split, by_slot,
    )
    out_specs = (
        by_slot, by_slot, P(), split, split, split, split, P(), split, split, split,
    )
    return jax.shard_map(
        functools.partial(shards, dict(mesh.shape)),
        mesh=mesh,
        in_specs=in_specs,
        out_specs=out_specs,
        check_vma=False,
    )
```

```python
import functools

import jax
import jax.numpy as jnp
from jax import lax
from jax.experimental import pallas as pl
from jax.experimental.pallas import tpu as pltpu
from jax.sharding import PartitionSpec as P

HDIM = 64
BLOCK = 128
EPS = 1e-05
ROPE_BASE = 100000.0
NEG_FILL = -1e30
F32 = jnp.float32
BF16 = jnp.bfloat16
VMEM_LIMIT = 56 * 1024 * 1024


def dot(a, b, ca, cb):
    return lax.dot_general(a, b, (((ca,), (cb,)), ((), ())), preferred_element_type=F32)


def live_mask(qpos, start, p):
    kpos = p * BLOCK + lax.broadcasted_iota(jnp.int32, (BLOCK, BLOCK), 0)
    return (kpos <= qpos) & (kpos >= start)


def fwd_kernel(groups, share, info, kvat, q_ref, start_ref, kv_ref, o_ref, lse_ref, qs, m_s, l_s, acc):
    i = pl.program_id(0)
    lo, b = info[0, i], info[1, i]
    lanes = share * BLOCK
    for g in range(groups):
        for h in range(share):
            at = (g * share + h) * HDIM
            qs[g, :, h * BLOCK : (h + 1) * BLOCK] = q_ref[at : at + HDIM, :]
    m_s[...] = jnp.full_like(m_s, NEG_FILL)
    l_s[...] = jnp.zeros_like(l_s)
    acc[...] = jnp.zeros_like(acc)
    qpos = b * BLOCK + lax.broadcasted_iota(jnp.int32, (1, BLOCK), 1)
    start = start_ref[...]

    def step(t, carry):
        p = b - t
        at = kvat[p]
        ok = live_mask(qpos, start, p)
        ok = jnp.concatenate([ok] * share, axis=1)
        for g in range(groups):
            k_t = kv_ref[at, g * HDIM : (g + 1) * HDIM, :]
            v_t = kv_ref[at, (groups + g) * HDIM : (groups + g + 1) * HDIM, :]
            s = jnp.where(ok, dot(k_t, qs[g], 0, 0), NEG_FILL)
            m_old = m_s[g]
            m_new = jnp.maximum(m_old, jnp.max(s, axis=0, keepdims=True))
            w = jnp.exp(s - m_new)
            alpha = jnp.exp(m_old - m_new)
            l_s[g] = l_s[g] * alpha + jnp.sum(w, axis=0, keepdims=True)
            acc[g] = acc[g] * alpha + dot(v_t, w.astype(BF16), 1, 0)
            m_s[g] = m_new
        return carry

    lax.fori_loop(0, b - lo + 1, step, 0)
    for g in range(groups):
        total = l_s[g]
        out = (acc[g] / total).astype(BF16)
        for h in range(share):
            at = (g * share + h) * HDIM
            o_ref[at : at + HDIM, :] = out[:, h * BLOCK : (h + 1) * BLOCK]
        lse_ref[0, g : g + 1, :] = m_s[g] + jnp.log(total)


def attention_fwd(info, kvat, q_t, start, kv, mb):
    width, tokens = q_t.shape
    nb, kvw, _ = kv.shape
    groups = kvw // HDIM // 2
    share = width // HDIM // groups
    nq = info.shape[1]
    lanes = share * BLOCK
    return pl.pallas_call(
        functools.partial(fwd_kernel, groups, share),
        grid_spec=pltpu.PrefetchScalarGridSpec(
            num_scalar_prefetch=2,
            grid=(nq,),
            in_specs=[
                pl.BlockSpec((width, BLOCK), lambda i, *_: (0, mb * nq + i)),
                pl.BlockSpec((1, BLOCK), lambda i, *_: (0, mb * nq + i)),
                pl.BlockSpec((nb, kvw, BLOCK), lambda i, *_: (0, 0, 0)),
            ],
            out_specs=[
                pl.BlockSpec((width, BLOCK), lambda i, *_: (0, i)),
                pl.BlockSpec((1, groups, lanes), lambda i, *_: (i, 0, 0)),
            ],
            scratch_shapes=[
                pltpu.VMEM((groups, HDIM, lanes), BF16),
                pltpu.VMEM((groups, 1, lanes), F32),
                pltpu.VMEM((groups, 1, lanes), F32),
                pltpu.VMEM((groups, HDIM, lanes), F32),
            ],
        ),
        out_shape=[
            jax.ShapeDtypeStruct((width, nq * BLOCK), BF16),
            jax.ShapeDtypeStruct((nq, groups, lanes), F32),
        ],
        compiler_params=pltpu.CompilerParams(vmem_limit_bytes=VMEM_LIMIT),
        cost_estimate=pl.CostEstimate(
            flops=int(5e9), bytes_accessed=int(4e6), transcendentals=int(4e6)
        ),
        name="attention_fwd",
    )(info, kvat, q_t, start, kv)


def bwd_kernel(
    groups, share, info, kvat, q_ref, do_ref, o_ref, lse_ref, start_ref, cos_ref, sin_ref, kv_ref,
    dq_ref, dkv_ref, qs, dos, delta, dq, dkv,
):
    i = pl.program_id(0)
    lo, b = info[0, i], info[1, i]

    @pl.when(i == 0)
    def _():
        dkv[...] = jnp.zeros_like(dkv)

    for g in range(groups):
        for h in range(share):
            at = (g * share + h) * HDIM
            cols = slice(h * BLOCK, (h + 1) * BLOCK)
            d_out = do_ref[at : at + HDIM, :]
            qs[g, :, cols] = q_ref[at : at + HDIM, :]
            dos[g, :, cols] = d_out
            delta[g, :, cols] = jnp.sum(
                d_out.astype(F32) * o_ref[at : at + HDIM, :].astype(F32), axis=0, keepdims=True
            )
    dq[...] = jnp.zeros_like(dq)
    qpos = b * BLOCK + lax.broadcasted_iota(jnp.int32, (1, BLOCK), 1)
    start = start_ref[...]

    def step(t, carry):
        p = b - t
        at = kvat[p]
        ok = live_mask(qpos, start, p)
        ok = jnp.concatenate([ok] * share, axis=1)
        for g in range(groups):
            krows = slice(g * HDIM, (g + 1) * HDIM)
            vrows = slice((groups + g) * HDIM, (groups + g + 1) * HDIM)
            k_t = kv_ref[at, krows, :]
            v_t = kv_ref[at, vrows, :]
            s = jnp.where(ok, dot(k_t, qs[g], 0, 0), NEG_FILL)
            w = jnp.exp(s - lse_ref[0, g : g + 1, :])
            dw = dot(v_t, dos[g], 0, 0)
            ds = (w * (dw - delta[g])).astype(BF16)
            dq[g] += dot(k_t, ds, 1, 0)
            dkv[at, krows, :] += dot(qs[g], ds, 1, 1)
            dkv[at, vrows, :] += dot(dos[g], w.astype(BF16), 1, 1)
        return carry

    lax.fori_loop(0, b - lo + 1, step, 0)
    cos, sin = cos_ref[...], sin_ref[...]
    half = HDIM // 2
    for g in range(groups):
        for h in range(share):
            at = (g * share + h) * HDIM
            one = dq[g, :half, h * BLOCK : (h + 1) * BLOCK] * HDIM**-0.5
            two = dq[g, half:, h * BLOCK : (h + 1) * BLOCK] * HDIM**-0.5
            dq_ref[at : at + half, :] = (one * cos + two * sin).astype(BF16)
            dq_ref[at + half : at + HDIM, :] = (two * cos - one * sin).astype(BF16)

    @pl.when(i == pl.num_programs(0) - 1)
    def _():
        dkv_ref[...] = dkv[...].astype(BF16)


def attention_bwd(info, kvat, q_t, do_t, o_t, lse, start, cos_t, sin_t, kv, mb):
    width = q_t.shape[0]
    nb, kvw, _ = kv.shape
    groups = kvw // HDIM // 2
    share = width // HDIM // groups
    nq = info.shape[1]
    lanes = share * BLOCK
    tok = lambda rows: pl.BlockSpec((rows, BLOCK), lambda i, *_: (0, mb * nq + i))
    return pl.pallas_call(
        functools.partial(bwd_kernel, groups, share),
        grid_spec=pltpu.PrefetchScalarGridSpec(
            num_scalar_prefetch=2,
            grid=(nq,),
            in_specs=[
                tok(width),
                tok(width),
                tok(width),
                pl.BlockSpec((1, groups, lanes), lambda i, *_: (i, 0, 0)),
                tok(1),
                tok(HDIM // 2),
                tok(HDIM // 2),
                pl.BlockSpec((nb, kvw, BLOCK), lambda i, *_: (0, 0, 0)),
            ],
            out_specs=[
                pl.BlockSpec((width, BLOCK), lambda i, *_: (0, i)),
                pl.BlockSpec((nb, kvw, BLOCK), lambda i, *_: (0, 0, 0)),
            ],
            scratch_shapes=[
                pltpu.VMEM((groups, HDIM, lanes), BF16),
                pltpu.VMEM((groups, HDIM, lanes), BF16),
                pltpu.VMEM((groups, 1, lanes), F32),
                pltpu.VMEM((groups, HDIM, lanes), F32),
                pltpu.VMEM((nb, kvw, BLOCK), F32),
            ],
        ),
        out_shape=[
            jax.ShapeDtypeStruct((width, nq * BLOCK), BF16),
            jax.ShapeDtypeStruct((nb, kvw, BLOCK), BF16),
        ],
        compiler_params=pltpu.CompilerParams(vmem_limit_bytes=VMEM_LIMIT),
        cost_estimate=pl.CostEstimate(
            flops=int(1e10), bytes_accessed=int(8e6), transcendentals=int(4e6)
        ),
        name="attention_bwd",
    )(info, kvat, q_t, do_t, o_t, lse, start, cos_t, sin_t, kv)


CORE, ALONG_X, ALONG_Y = 1, 2, 4
FAR = ALONG_X + ALONG_Y
CUBE = 8
LAG = 2
LAGS = 1
SEM = pltpu.SemaphoreType.DMA


def meet(peers):
    barrier = pltpu.get_barrier_semaphore()
    for peer in peers:
        pl.semaphore_signal(barrier, inc=1, device_id=peer, device_id_type=pl.DeviceIdType.MESH)
    pl.semaphore_wait(barrier, len(peers))


def gather_kernel(count, chunks, planes, *refs):
    ins, outs = refs[:count], refs[count : 2 * count]
    sent, came = refs[2 * count :]
    at, row = lax.axis_index("wide"), lax.axis_index("narrow")
    peer = {bit: (at ^ bit, row) for bit in (CORE, ALONG_X, ALONG_Y)}
    if planes:
        peer["row"] = (at, row ^ 1)

    def part(ref, c, half):
        return ref.at[chunks[c][1 + half]]

    def copy(c, m, half, way, slot):
        a = chunks[c][0]
        there = part(outs[a].at[at ^ m], c, half)
        return pltpu.make_async_remote_copy(
            src_ref=there if m else part(ins[a], c, half),
            dst_ref=there,
            send_sem=sent.at[c, slot],
            recv_sem=came.at[c, m if way == "row" else m ^ way, half],
            device_id=peer[way],
            device_id_type=pl.DeviceIdType.MESH,
        )

    def run(mine):
        other = 1 - mine
        used = [0] * len(chunks)
        begun = []

        def push(c, m, half, way):
            r = copy(c, m, half, way, used[c])
            used[c] += 1
            r.start()
            begun.append(r)

        def take(c, m, half, *ways):
            copy(c, m ^ CORE, half, CORE, 0).wait_recv()
            for way in ways:
                push(c, m, half, way)

        def first(c):
            push(c, 0, mine, ALONG_X)
            push(c, 0, mine, ALONG_Y)
            if not planes:
                push(c, 0, other, ALONG_X)
                push(c, 0, other, ALONG_Y)

        def second(c):
            if planes:
                take(c, ALONG_Y, mine, ALONG_X, CORE)
                push(c, 0, other, ALONG_Y)
                take(c, ALONG_X, mine, "row", CORE)
            else:
                take(c, ALONG_X, mine, ALONG_Y, CORE)
                take(c, ALONG_Y, other, ALONG_X, CORE)
                take(c, ALONG_Y, mine, CORE)
                take(c, ALONG_X, other, CORE)
            push(c, 0, 0, CORE)
            push(c, 0, 1, CORE)

        def third(c):
            take(c, FAR, mine, *(("row", CORE) if planes else (CORE,)))
            if planes:
                take(c, ALONG_Y, other, CORE)
                take(c, ALONG_X, other, CORE)
            else:
                take(c, FAR, other, CORE)

        def fourth(c):
            if planes:
                take(c, FAR, other, CORE)

        def fifth(c):
            for half in range(2):
                take(c, CORE, half, CORE)
            for m in (ALONG_X, ALONG_Y, FAR):
                for half in range(2):
                    take(c, m + CORE, half)

        def sixth(c):
            for half in range(2):
                take(c, 0, half)

        steps = (first, second, third, fourth, fifth, sixth)
        for t in range(len(chunks) + LAG * (len(steps) - 1)):
            for s, step in enumerate(steps):
                if 0 <= t - LAG * s < len(chunks):
                    step(t - LAG * s)
        for r in begun:
            r.wait_send()

    meet(list(peer.values()))
    if planes:
        for mine in range(2):
            pl.when(row % 2 == mine)(functools.partial(run, mine))
    else:
        run(0)


def gather(arrays, chunks, planes, collective_id):
    count = len(arrays)
    return pl.pallas_call(
        functools.partial(gather_kernel, count, chunks, planes),
        in_specs=[pl.BlockSpec(memory_space=pl.ANY)] * count,
        out_specs=[pl.BlockSpec(memory_space=pl.ANY)] * count,
        out_shape=[jax.ShapeDtypeStruct((8,) + a.shape, a.dtype) for a in arrays],
        scratch_shapes=[
            SEM((len(chunks), 16)),
            SEM((len(chunks), 8, 2)),
        ],
        compiler_params=pltpu.CompilerParams(collective_id=collective_id, has_side_effects=True),
        name="gather_rows" if planes else "gather_keys",
    )(*arrays)


def weight_chunks(shapes, most=160 * 1024):
    chunks = []
    for a, (rows, cols) in enumerate(shapes):
        n = 1
        while rows * cols // n > most and rows % (32 * n) == 0:
            n *= 2
        k = 1
        while rows // n * cols // k > most and cols % (256 * k) == 0:
            k *= 2
        for i in range(n):
            lo, hi = rows // n * i, rows // n * (i + 1)
            mid = lo + -(-(hi - lo) // 32) * 16
            for j in range(k):
                c = pl.ds(cols // k * j, cols // k)
                chunks.append((a, (pl.ds(lo, mid - lo), c), (pl.ds(mid, hi - mid), c)))
    return chunks


def key_chunks(count, blocks, rows, parts=2):
    return [
        (a, (pl.ds(0, blocks // 2), pl.ds(rows // parts * i, rows // parts)),
         (pl.ds(blocks // 2, blocks // 2), pl.ds(rows // parts * i, rows // parts)))
        for a in range(count) for i in range(parts)
    ]


def sum_kernel(count, chunks, rows_too, *refs):
    refs = list(refs)
    take = lambda n: [refs.pop(0) for _ in range(n)]
    ins = take(count)
    gain = take(1)[0] if rows_too else None
    outs = take(count)
    total = take(1)[0] if rows_too else None
    n = len(chunks)
    held, core_in, one_in, two_in, line_in, last = (take(n) for _ in range(6))
    load, sent, came, stored = take(4)
    if rows_too:
        gain_buf, gain_sent, gain_came = take(3)
    at, row = lax.axis_index("wide"), lax.axis_index("narrow")
    way = {bit: (at ^ bit, row) for bit in (CORE, ALONG_X, ALONG_Y)}
    peers = [way[CORE], way[ALONG_X], way[ALONG_Y]]
    if rows_too:
        near, across = (at, row ^ 1), (at, row ^ 3)
        peers += [near, across]
    middle = (row == 1) | (row == 2)

    def send(c, slot, src, dst, to):
        return pltpu.make_async_remote_copy(
            src_ref=src, dst_ref=dst, send_sem=sent.at[c, slot], recv_sem=came.at[c, slot],
            device_id=to, device_id_type=pl.DeviceIdType.MESH,
        )

    def add(dst, src):
        rows = dst.shape[-2]
        most = rows // 16
        step = 16 * max(k for k in (1, 2, 3, 4) if most % k == 0)

        def body(i, carry):
            cut = pl.ds(pl.multiple_of(i * step, 16), step)
            dst[cut, :] = dst[cut, :] + src[cut, :]
            return carry

        lax.fori_loop(0, most * 16 // step, body, 0)
        if rows % 16:
            cut = slice(most * 16, rows)
            dst[cut, :] = dst[cut, :] + src[cut, :]

    def orders(c):
        first = chunks[c][2]
        other = FAR - first
        return first, other, (0, other, first, FAR)

    def core_copies(c):
        a, cut, _ = chunks[c]
        return [
            send(c, i, ins[a].at[(at ^ CORE ^ m,) + cut], core_in[c].at[i], way[CORE])
            for i, m in enumerate(orders(c)[2])
        ]

    def loads(c):
        a, cut, _ = chunks[c]
        return [
            pltpu.make_async_copy(ins[a].at[(at ^ m,) + cut], held[c].at[i], load.at[c, i])
            for i, m in enumerate(orders(c)[2])
        ]

    def first_copy(c):
        return send(c, 4, held[c].at[pl.ds(2, 2)], one_in[c], way[orders(c)[0]])

    def second_copy(c):
        return send(c, 5, held[c].at[1], two_in[c], way[orders(c)[1]])

    def inward(c):
        return send(c, 6, held[c].at[0], line_in[c].at[0], near)

    def over(c):
        return send(c, 7, held[c].at[0], line_in[c].at[1], across)

    def outward(c):
        return send(c, 6, line_in[c].at[1], line_in[c].at[0], near)

    def store(c):
        a, cut, _ = chunks[c]
        return pltpu.make_async_copy(last[c], outs[a].at[cut], stored.at[c])

    def s0(c):
        for r in core_copies(c) + loads(c):
            r.start()

    def s1(c):
        for r in loads(c):
            r.wait()
        for r in core_copies(c):
            r.wait_recv()
        for i in (2, 3, 0, 1):
            add(held[c].at[i], core_in[c].at[i])
            if i == 3:
                first_copy(c).start()

    def s2(c):
        first_copy(c).wait_recv()
        add(held[c].at[1], one_in[c].at[1])
        second_copy(c).start()
        add(held[c].at[0], one_in[c].at[0])

    def s3(c):
        second_copy(c).wait_recv()
        add(held[c].at[0], two_in[c])
        if rows_too:
            pl.when(~middle)(lambda: inward(c).start())
        else:
            last[c][...] = held[c][0].astype(last[c].dtype)
            store(c).start()

    def s4(c):
        @pl.when(middle)
        def _():
            inward(c).wait_recv()
            add(held[c].at[0], line_in[c].at[0])
            over(c).start()

    def s5(c):
        @pl.when(middle)
        def _():
            over(c).wait_recv()
            add(line_in[c].at[1], held[c].at[0])
            outward(c).start()
            last[c][...] = line_in[c][1].astype(last[c].dtype)
            store(c).start()

    def s6(c):
        @pl.when(~middle)
        def _():
            outward(c).wait_recv()
            last[c][...] = line_in[c][0].astype(last[c].dtype)
            store(c).start()

    meet(peers)
    gain_ways = []
    if rows_too:
        gain_ways = [way[CORE], way[ALONG_X], way[ALONG_Y], near, across]
        gain_buf[0] = gain[...]

    def gain_copy(i):
        return pltpu.make_async_remote_copy(
            src_ref=gain_buf.at[2 * i], dst_ref=gain_buf.at[2 * i + 1], send_sem=gain_sent.at[i],
            recv_sem=gain_came.at[i], device_id=gain_ways[i], device_id_type=pl.DeviceIdType.MESH,
        )

    steps = (s0, s1, s2, s3) + ((s4, s5, s6) if rows_too else ())
    for t in range(n + LAGS * (len(steps) - 1)):
        for s, step in enumerate(steps):
            if 0 <= t - LAGS * s < n:
                step(t - LAGS * s)
        if 1 <= t <= len(gain_ways):
            gain_copy(t - 1).wait_recv()
            gain_buf[2 * t] = gain_buf[2 * t - 2] + gain_buf[2 * t - 1]
        if t < len(gain_ways):
            gain_copy(t).start()
    for c in range(n):
        for r in core_copies(c):
            r.wait_send()
        first_copy(c).wait_send()
        second_copy(c).wait_send()
        if rows_too:
            inward(c).wait_send()
            pl.when(middle)(lambda: over(c).wait_send())
        store(c).wait()
    for i in range(len(gain_ways)):
        gain_copy(i).wait_send()
    if rows_too:
        total[...] = gain_buf[2 * len(gain_ways)]


def sums(arrays, chunks, collective_id, gain=None):
    count, n = len(arrays), len(chunks)
    rows_too = gain is not None
    kind = F32 if rows_too else arrays[0].dtype
    anywhere = pl.BlockSpec(memory_space=pl.ANY)
    vmem = pl.BlockSpec(memory_space=pltpu.VMEM)
    size = [(c[1][0].size, c[1][1].size) for c in chunks]
    dtype = arrays[0].dtype
    room = lambda *lead: [pltpu.VMEM(lead + s, dtype) for s in size]
    line = room(2) if rows_too else [pltpu.VMEM((8, 128), dtype)] * n
    scratch = room(4) + room(4) + room(2) + room() + line + [pltpu.VMEM(s, kind) for s in size]
    scratch += [SEM((n, 4)), SEM((n, 8)), SEM((n, 8)), SEM((n,))]
    outs = [jax.ShapeDtypeStruct(a.shape[1:], kind) for a in arrays]
    if rows_too:
        scratch += [pltpu.VMEM((11,) + gain.shape, F32), SEM((5,)), SEM((5,))]
        outs.append(jax.ShapeDtypeStruct(gain.shape, F32))
    return pl.pallas_call(
        functools.partial(sum_kernel, count, chunks, rows_too),
        in_specs=[anywhere] * count + [vmem] * rows_too,
        out_specs=[anywhere] * count + [vmem] * rows_too,
        out_shape=outs,
        scratch_shapes=scratch,
        compiler_params=pltpu.CompilerParams(
            collective_id=collective_id, has_side_effects=True, vmem_limit_bytes=62 * 1024 * 1024
        ),
        name="sum_weights" if rows_too else "sum_keys",
    )(*arrays, *([gain] if rows_too else []))


def sum_chunks(shapes, most=180 * 1024):
    chunks = []
    for a, (rows, cols) in enumerate(shapes):
        n = k = 1
        while rows // n * cols > most and rows % (32 * n) == 0:
            n *= 2
        while rows // n * cols // k > most and cols % (256 * k) == 0:
            k *= 2
        for i in range(n):
            for j in range(k):
                first = (ALONG_X, ALONG_Y)[len(chunks) % 2]
                chunks.append((a, (pl.ds(rows // n * i, rows // n), pl.ds(cols // k * j, cols // k)), first))
    return chunks


def row_sum(part, size):
    if size != 4:
        return lax.psum(part, "narrow").astype(F32)
    add = lambda a, b: (a.astype(F32) + b.astype(F32)).astype(BF16)
    part = add(part, lax.ppermute(part, "narrow", [(0, 1), (3, 2)]))
    part = add(part, lax.ppermute(part, "narrow", [(1, 2), (2, 1)]))
    back = lax.ppermute(part, "narrow", [(1, 0), (2, 3)])
    at = lax.axis_index("narrow")
    return jnp.where((at == 1) | (at == 2), part, back).astype(F32)


def turn(v, cos, sin):
    heads = v.reshape(-1, 2, HDIM // 2, v.shape[1])
    one, two = heads[:, 0], heads[:, 1]
    return jnp.stack([one * cos - two * sin, two * cos + one * sin], axis=1).reshape(v.shape)


def turn_back(v, cos, sin):
    return turn(v, cos, -sin)


def shards(sizes, tokens, lengths, block_plan, attn_gain, w_query, w_key, w_value, w_out, ffn_gain,
           w_gate, w_up, w_down, cotangent):
    n = sizes["wide"]
    at = lax.axis_index("wide")
    micro, _, slots, width = tokens.shape
    total = micro * slots
    kd = w_key.shape[1]
    ff = w_gate.shape[1]
    nq = slots // BLOCK
    nb = nq * n

    plan = block_plan[:, 0]
    sizes_of = lengths[:, 0]
    docs = sizes_of.shape[1]
    upto = jnp.arange(docs)[:, None] >= jnp.arange(docs)[None, :]
    ends = jnp.sum(jnp.where(upto[None], sizes_of[:, None, :], 0), axis=2)
    own_plan = lax.dynamic_slice_in_dim(plan, at * nq, nq, axis=1)
    position = own_plan[:, :, None] * BLOCK + jnp.arange(BLOCK, dtype=jnp.int32)
    start = jnp.sum(
        jnp.where(position[..., None] >= ends[:, None, None, :], sizes_of[:, None, None, :], 0), axis=3
    )
    info = jnp.stack([start[:, :, 0] // BLOCK, own_plan], axis=1)
    slot_block = jnp.arange(nb, dtype=jnp.int32)
    where_is = jnp.sum(
        jnp.where(plan[:, None, :] == slot_block[None, :, None], slot_block[None, None, :], 0), axis=2
    )
    start = start.reshape(1, total)
    local = position.reshape(1, total) - start
    frequency = ROPE_BASE ** (-2.0 * jnp.arange(HDIM // 2, dtype=F32) / HDIM)
    angles = frequency[:, None] * local.astype(F32)
    cos, sin = jnp.cos(angles), jnp.sin(angles)

    cube = n == CUBE and sizes["narrow"] == 4 and nq % 2 == 0

    def whole_rows(*shards_of):
        if cube:
            got = gather(shards_of, weight_chunks([a.shape for a in shards_of]), True, 1)
        else:
            got = [lax.all_gather(a, "wide", axis=0) for a in shards_of]
        return [a.reshape(-1, a.shape[2]) for a in got]

    def whole_keys(*own):
        if cube:
            got = gather(own, key_chunks(len(own), nq, own[0].shape[1]), False, 2)
        else:
            got = [lax.all_gather(a, "wide", axis=0) for a in own]
        return [a.reshape((nb,) + a.shape[2:]) for a in got]

    def key_sums(*parts):
        shaped = [a.reshape(n, -1, BLOCK) for a in parts]
        if cube:
            got = sums(shaped, sum_chunks([a.shape[1:] for a in shaped], 100 * 1024), 3)
        else:
            got = [lax.psum_scatter(a, "wide", scatter_dimension=0) for a in shaped]
        return [a.reshape((nq,) + p.shape[1:]) for a, p in zip(got, parts)]

    def weight_sums(gain, *parts):
        shaped = [a.reshape(n, -1, a.shape[1]) for a in parts]
        if cube:
            *got, gain = sums(shaped, sum_chunks([a.shape[1:] for a in shaped]), 4, gain)
            return got, gain
        got = [lax.psum_scatter(a, "wide", scatter_dimension=0) for a in shaped]
        return [row_sum(a, sizes["narrow"]) for a in got], lax.psum(gain, ("wide", "narrow"))

    x = tokens.reshape(total, width).astype(F32)
    ct = cotangent.reshape(total, width)

    g_query, g_key, g_value, g_out, g_gate, g_up, g_down = whole_rows(
        w_query, w_key, w_value, w_out, w_gate, w_up, w_down
    )
    rr1 = lax.rsqrt(jnp.mean(x * x, axis=1, keepdims=True) + EPS)
    xn = (x * rr1 * attn_gain).astype(BF16)
    key_t = turn(dot(g_key, xn, 0, 1), cos, sin).astype(BF16)
    value_t = dot(g_value, xn, 0, 1).astype(BF16)
    own_kv = jnp.concatenate([key_t, value_t]).reshape(2 * kd, micro, nq, BLOCK).transpose(1, 2, 0, 3)
    q_t = (turn(dot(g_query, xn, 0, 1), cos, sin).astype(BF16) * HDIM**-0.5).astype(BF16)

    kvs = whole_keys(*[own_kv[mb] for mb in range(micro)])
    outs, lses = [], []
    for mb in range(micro):
        o_t, lse = attention_fwd(info[mb], where_is[mb], q_t, start, kvs[mb], mb)
        outs.append(o_t)
        lses.append(lse)
    att_t = jnp.concatenate(outs, axis=1)

    res = x + dot(att_t, g_out, 0, 0)
    rr2 = lax.rsqrt(jnp.mean(res * res, axis=1, keepdims=True) + EPS)
    hn = (res * rr2 * ffn_gain).astype(BF16)
    gate = dot(g_gate, hn, 0, 1)
    up = dot(g_up, hn, 0, 1)
    sg = 1.0 / (1.0 + jnp.exp(-gate))
    hidden = (gate * sg * up).astype(BF16)
    out = (res + dot(hidden, g_down, 0, 0)).astype(BF16)

    d_hidden = dot(g_down, ct, 1, 1)
    d_gate = (d_hidden * up * sg * (1.0 + gate * (1.0 - sg))).astype(BF16)
    d_up = (d_hidden * gate * sg).astype(BF16)
    d_hn = dot(d_gate, g_gate, 0, 1) + dot(d_up, g_up, 0, 1)
    u = d_hn * ffn_gain
    d_res = (
        ct.astype(F32) + rr2 * u - res * rr2**3 * jnp.mean(u * res, axis=1, keepdims=True)
    )
    gain_two = jnp.sum(d_hn * res * rr2, axis=0)
    d_attn = d_res.astype(BF16)
    do_t = dot(g_out, d_attn, 1, 1).astype(BF16)

    dqs, dkvs = [], []
    for mb in range(micro):
        dq_t, dkv = attention_bwd(
            info[mb], where_is[mb], q_t, do_t, att_t, lses[mb], start, cos, sin, kvs[mb], mb
        )
        dqs.append(dq_t)
        dkvs.append(dkv)
    dq = jnp.concatenate(dqs, axis=1)
    dkv = jnp.concatenate([a.transpose(1, 0, 2).reshape(2 * kd, slots) for a in key_sums(*dkvs)], axis=1)
    dk = turn_back(dkv[:kd].astype(F32), cos, sin).astype(BF16)
    dv = dkv[kd:]

    d_xn = dot(dq, g_query, 0, 1) + dot(dk, g_key, 0, 1) + dot(dv, g_value, 0, 1)
    u = d_xn * attn_gain
    grad_x = d_res + rr1 * u - x * rr1**3 * jnp.mean(u * x, axis=1, keepdims=True)
    gain_one = jnp.sum(d_xn * x * rr1, axis=0)

    part = lambda a, b, ca, cb: dot(a, b, ca, cb).astype(BF16)
    (s_down, s_gate, s_up, s_out, s_query, s_key, s_value), gains = weight_sums(
        jnp.stack([gain_one, gain_two]),
        part(hidden, ct, 1, 0),
        part(hn, d_gate, 0, 1),
        part(hn, d_up, 0, 1),
        part(att_t, d_attn, 1, 0),
        part(xn, dq, 0, 1),
        part(xn, dk, 0, 1),
        part(xn, dv, 0, 1),
    )
    shape = (micro, 1, slots, width)
    return (
        out.reshape(shape),
        grad_x.reshape(shape),
        gains[0],
        s_query,
        s_key,
        s_value,
        s_out,
        gains[1],
        s_gate,
        s_up,
        s_down,
    )


def solution(mesh):
    by_slot = P(None, "narrow", "wide", None)
    by_row = P(None, "narrow", None)
    split = P("wide", None)
    in_specs = (
        by_slot, by_row, by_row, P(), split, split, split, split, P(), split, split, split, by_slot,
    )
    out_specs = (
        by_slot, by_slot, P(), split, split, split, split, P(), split, split, split,
    )
    return jax.shard_map(
        functools.partial(shards, dict(mesh.shape)),
        mesh=mesh,
        in_specs=in_specs,
        out_specs=out_specs,
        check_vma=False,
    )
```

```python
import functools

import jax
import jax.numpy as jnp
from jax import lax
from jax.experimental import pallas as pl
from jax.experimental.pallas import tpu as pltpu
from jax.sharding import PartitionSpec as P

HDIM = 64
BLOCK = 128
EPS = 1e-05
ROPE_BASE = 100000.0
NEG_FILL = -1e30
F32 = jnp.float32
BF16 = jnp.bfloat16
VMEM_LIMIT = 56 * 1024 * 1024


def dot(a, b, ca, cb):
    return lax.dot_general(a, b, (((ca,), (cb,)), ((), ())), preferred_element_type=F32)


def live_mask(qpos, start, p):
    kpos = p * BLOCK + lax.broadcasted_iota(jnp.int32, (BLOCK, BLOCK), 0)
    return (kpos <= qpos) & (kpos >= start)


STEP = 2


def pick(kv_ref, kvat, mb, qpos, start, b, t, share):
    nq = kv_ref.shape[2]
    blocks = [b - STEP * t - i for i in range(STEP)]
    slots = [kvat[mb, jnp.maximum(p, 0)] for p in blocks]
    at = [(lax.div(s, nq), lax.rem(s, nq)) for s in slots]
    ok = jnp.concatenate([live_mask(qpos, start, p) for p in blocks], axis=0)

    def keys(g):
        rows = slice(g * HDIM, (g + 1) * HDIM)
        return jnp.concatenate([kv_ref[d, 0, s, rows, :] for d, s in at], axis=1)

    return keys, at, jnp.concatenate([ok] * share, axis=1)


def fwd_kernel(groups, share, info, kvat, q_ref, start_ref, kv_ref, o_ref, lse_ref, qs, m_s, l_s, acc, s_s, w_s):
    mb, i = pl.program_id(0), pl.program_id(1)
    lo, b = info[mb, 0, i], info[mb, 1, i]
    nq = kv_ref.shape[2]
    lanes = share * BLOCK
    for g in range(groups):
        for h in range(share):
            at = (g * share + h) * HDIM
            qs[g, :, h * BLOCK : (h + 1) * BLOCK] = q_ref[at : at + HDIM, :]
    m_s[...] = jnp.full_like(m_s, NEG_FILL)
    l_s[...] = jnp.zeros_like(l_s)
    acc[...] = jnp.zeros_like(acc)
    qpos = b * BLOCK + lax.broadcasted_iota(jnp.int32, (1, BLOCK), 1)
    start = start_ref[...]

    def step(t, carry):
        keys, at, ok = pick(kv_ref, kvat, mb, qpos, start, b, t, share)
        for g in range(groups):
            s_s[g] = jnp.where(ok, dot(keys(g), qs[g], 0, 0), NEG_FILL)
        alphas = []
        for g in range(groups):
            s = s_s[g]
            m_old = m_s[g]
            m_new = jnp.maximum(m_old, jnp.max(s, axis=0, keepdims=True))
            w = jnp.exp(s - m_new)
            alpha = jnp.exp(m_old - m_new)
            l_s[g] = l_s[g] * alpha + jnp.sum(w, axis=0, keepdims=True)
            m_s[g] = m_new
            w_s[g] = w.astype(BF16)
            alphas.append(alpha)
        for g in range(groups):
            acc[g] = acc[g] * alphas[g] + dot(keys(groups + g), w_s[g], 1, 0)
        return carry

    lax.fori_loop(0, (b - lo + STEP) // STEP, step, 0)
    for g in range(groups):
        total = l_s[g]
        out = (acc[g] / total).astype(BF16)
        for h in range(share):
            at = (g * share + h) * HDIM
            o_ref[at : at + HDIM, :] = out[:, h * BLOCK : (h + 1) * BLOCK]
        lse_ref[0, g : g + 1, :] = m_s[g] + jnp.log(total)


def attention_fwd(info, kvat, q_t, start, kv):
    width = q_t.shape[0]
    n, micro, nq, kvw, _ = kv.shape
    groups = kvw // HDIM // 2
    share = width // HDIM // groups
    lanes = share * BLOCK
    tok = lambda rows: pl.BlockSpec((rows, BLOCK), lambda m, i, *_: (0, m * nq + i))
    return pl.pallas_call(
        functools.partial(fwd_kernel, groups, share),
        grid_spec=pltpu.PrefetchScalarGridSpec(
            num_scalar_prefetch=2,
            grid=(micro, nq),
            in_specs=[
                tok(width),
                tok(1),
                pl.BlockSpec((n, 1, nq, kvw, BLOCK), lambda m, i, *_: (0, m, 0, 0, 0)),
            ],
            out_specs=[
                tok(width),
                pl.BlockSpec((1, groups, lanes), lambda m, i, *_: (m * nq + i, 0, 0)),
            ],
            scratch_shapes=[
                pltpu.VMEM((groups, HDIM, lanes), BF16),
                pltpu.VMEM((groups, 1, lanes), F32),
                pltpu.VMEM((groups, 1, lanes), F32),
                pltpu.VMEM((groups, HDIM, lanes), F32),
                pltpu.VMEM((groups, STEP * BLOCK, lanes), F32),
                pltpu.VMEM((groups, STEP * BLOCK, lanes), BF16),
            ],
        ),
        out_shape=[
            jax.ShapeDtypeStruct(q_t.shape, BF16),
            jax.ShapeDtypeStruct((micro * nq, groups, lanes), F32),
        ],
        compiler_params=pltpu.CompilerParams(vmem_limit_bytes=VMEM_LIMIT),
        cost_estimate=pl.CostEstimate(
            flops=int(1e10), bytes_accessed=int(8e6), transcendentals=int(8e6)
        ),
        name="attention_fwd",
    )(info, kvat, q_t, start, kv)


def bwd_kernel(
    groups, share, info, kvat, q_ref, do_ref, o_ref, lse_ref, start_ref, cos_ref, sin_ref, kv_ref,
    dq_ref, dkv_ref, qs, dos, delta, dq, dkv, s_s, d_s, w_s, ds_s,
):
    mb, i = pl.program_id(0), pl.program_id(1)
    lo, b = info[mb, 0, i], info[mb, 1, i]
    nq = kv_ref.shape[2]

    @pl.when(i == 0)
    def _():
        dkv[...] = jnp.zeros_like(dkv)

    for g in range(groups):
        for h in range(share):
            at = (g * share + h) * HDIM
            cols = slice(h * BLOCK, (h + 1) * BLOCK)
            d_out = do_ref[at : at + HDIM, :]
            qs[g, :, cols] = q_ref[at : at + HDIM, :]
            dos[g, :, cols] = d_out
            delta[g, :, cols] = jnp.sum(
                d_out.astype(F32) * o_ref[at : at + HDIM, :].astype(F32), axis=0, keepdims=True
            )
    dq[...] = jnp.zeros_like(dq)
    qpos = b * BLOCK + lax.broadcasted_iota(jnp.int32, (1, BLOCK), 1)
    start = start_ref[...]

    def step(t, carry):
        keys, at, ok = pick(kv_ref, kvat, mb, qpos, start, b, t, share)
        for g in range(groups):
            s_s[g] = jnp.where(ok, dot(keys(g), qs[g], 0, 0), NEG_FILL)
            d_s[g] = dot(keys(groups + g), dos[g], 0, 0)
        for g in range(groups):
            w = jnp.exp(s_s[g] - lse_ref[0, g : g + 1, :])
            w_s[g] = w.astype(BF16)
            ds_s[g] = (w * (d_s[g] - delta[g])).astype(BF16)
        for g in range(groups):
            dq[g] += dot(keys(g), ds_s[g], 1, 0)
            dk = dot(qs[g], ds_s[g], 1, 1)
            dv = dot(dos[g], w_s[g], 1, 1)
            krows = slice(g * HDIM, (g + 1) * HDIM)
            vrows = slice((groups + g) * HDIM, (groups + g + 1) * HDIM)
            for i in range(STEP):
                cols = slice(i * BLOCK, (i + 1) * BLOCK)
                dkv[at[i][0], at[i][1], krows, :] += dk[:, cols]
                dkv[at[i][0], at[i][1], vrows, :] += dv[:, cols]
        return carry

    lax.fori_loop(0, (b - lo + STEP) // STEP, step, 0)
    cos, sin = cos_ref[...], sin_ref[...]
    half = HDIM // 2
    for g in range(groups):
        for h in range(share):
            at = (g * share + h) * HDIM
            one = dq[g, :half, h * BLOCK : (h + 1) * BLOCK] * HDIM**-0.5
            two = dq[g, half:, h * BLOCK : (h + 1) * BLOCK] * HDIM**-0.5
            dq_ref[at : at + half, :] = (one * cos + two * sin).astype(BF16)
            dq_ref[at + half : at + HDIM, :] = (two * cos - one * sin).astype(BF16)

    @pl.when(i == nq - 1)
    def _():
        dkv_ref[:, 0] = dkv[...].astype(BF16)


def attention_bwd(info, kvat, q_t, do_t, o_t, lse, start, cos_t, sin_t, kv):
    width = q_t.shape[0]
    n, micro, nq, kvw, _ = kv.shape
    groups = kvw // HDIM // 2
    share = width // HDIM // groups
    lanes = share * BLOCK
    tok = lambda rows: pl.BlockSpec((rows, BLOCK), lambda m, i, *_: (0, m * nq + i))
    keys = pl.BlockSpec((n, 1, nq, kvw, BLOCK), lambda m, i, *_: (0, m, 0, 0, 0))
    return pl.pallas_call(
        functools.partial(bwd_kernel, groups, share),
        grid_spec=pltpu.PrefetchScalarGridSpec(
            num_scalar_prefetch=2,
            grid=(micro, nq),
            in_specs=[
                tok(width),
                tok(width),
                tok(width),
                pl.BlockSpec((1, groups, lanes), lambda m, i, *_: (m * nq + i, 0, 0)),
                tok(1),
                tok(HDIM // 2),
                tok(HDIM // 2),
                keys,
            ],
            out_specs=[tok(width), keys],
            scratch_shapes=[
                pltpu.VMEM((groups, HDIM, lanes), BF16),
                pltpu.VMEM((groups, HDIM, lanes), BF16),
                pltpu.VMEM((groups, 1, lanes), F32),
                pltpu.VMEM((groups, HDIM, lanes), F32),
                pltpu.VMEM((n, nq, kvw, BLOCK), F32),
                pltpu.VMEM((groups, STEP * BLOCK, lanes), F32),
                pltpu.VMEM((groups, STEP * BLOCK, lanes), F32),
                pltpu.VMEM((groups, STEP * BLOCK, lanes), BF16),
                pltpu.VMEM((groups, STEP * BLOCK, lanes), BF16),
            ],
        ),
        out_shape=[
            jax.ShapeDtypeStruct(q_t.shape, BF16),
            jax.ShapeDtypeStruct(kv.shape, BF16),
        ],
        compiler_params=pltpu.CompilerParams(vmem_limit_bytes=VMEM_LIMIT),
        cost_estimate=pl.CostEstimate(
            flops=int(2e10), bytes_accessed=int(16e6), transcendentals=int(8e6)
        ),
        name="attention_bwd",
    )(info, kvat, q_t, do_t, o_t, lse, start, cos_t, sin_t, kv)


CORE, ALONG_X, ALONG_Y = 1, 2, 4
FAR = ALONG_X + ALONG_Y
CUBE = 8
LAG = 2
LAGS = 2
SEM = pltpu.SemaphoreType.DMA


def meet(peers):
    barrier = pltpu.get_barrier_semaphore()
    for peer in peers:
        pl.semaphore_signal(barrier, inc=1, device_id=peer, device_id_type=pl.DeviceIdType.MESH)
    pl.semaphore_wait(barrier, len(peers))


def gather_kernel(count, chunks, planes, *refs):
    ins, outs = refs[:count], refs[count : 2 * count]
    sent, came = refs[2 * count :]
    at, row = lax.axis_index("wide"), lax.axis_index("narrow")
    peer = {bit: (at ^ bit, row) for bit in (CORE, ALONG_X, ALONG_Y)}
    if planes:
        peer["row"] = (at, row ^ 1)

    def part(ref, c, half):
        return ref.at[chunks[c][1 + half]]

    def copy(c, m, half, way, slot):
        a = chunks[c][0]
        there = part(outs[a].at[at ^ m], c, half)
        return pltpu.make_async_remote_copy(
            src_ref=there if m else part(ins[a], c, half),
            dst_ref=there,
            send_sem=sent.at[c, slot],
            recv_sem=came.at[c, m if way == "row" else m ^ way, half],
            device_id=peer[way],
            device_id_type=pl.DeviceIdType.MESH,
        )

    def run(mine):
        other = 1 - mine
        used = [0] * len(chunks)
        begun = []

        def push(c, m, half, way):
            r = copy(c, m, half, way, used[c])
            used[c] += 1
            r.start()
            begun.append(r)

        def take(c, m, half, *ways):
            copy(c, m ^ CORE, half, CORE, 0).wait_recv()
            for way in ways:
                push(c, m, half, way)

        def first(c):
            push(c, 0, mine, ALONG_X)
            push(c, 0, mine, ALONG_Y)
            if not planes:
                push(c, 0, other, ALONG_X)
                push(c, 0, other, ALONG_Y)

        def second(c):
            if planes:
                take(c, ALONG_Y, mine, ALONG_X, CORE)
                push(c, 0, other, ALONG_Y)
                take(c, ALONG_X, mine, "row", CORE)
            else:
                take(c, ALONG_X, mine, ALONG_Y, CORE)
                take(c, ALONG_Y, other, ALONG_X, CORE)
                take(c, ALONG_Y, mine, CORE)
                take(c, ALONG_X, other, CORE)
            push(c, 0, 0, CORE)
            push(c, 0, 1, CORE)

        def third(c):
            take(c, FAR, mine, *(("row", CORE) if planes else (CORE,)))
            if planes:
                take(c, ALONG_Y, other, CORE)
                take(c, ALONG_X, other, CORE)
            else:
                take(c, FAR, other, CORE)

        def fourth(c):
            if planes:
                take(c, FAR, other, CORE)

        def fifth(c):
            for half in range(2):
                take(c, CORE, half, CORE)
            for m in (ALONG_X, ALONG_Y, FAR):
                for half in range(2):
                    take(c, m + CORE, half)

        def sixth(c):
            for half in range(2):
                take(c, 0, half)

        steps = (first, second, third, fourth, fifth, sixth)
        for t in range(len(chunks) + LAG * (len(steps) - 1)):
            for s, step in enumerate(steps):
                if 0 <= t - LAG * s < len(chunks):
                    step(t - LAG * s)
        for r in begun:
            r.wait_send()

    meet(list(peer.values()))
    if planes:
        for mine in range(2):
            pl.when(row % 2 == mine)(functools.partial(run, mine))
    else:
        run(0)


def gather(arrays, chunks, planes, collective_id):
    count = len(arrays)
    return pl.pallas_call(
        functools.partial(gather_kernel, count, chunks, planes),
        in_specs=[pl.BlockSpec(memory_space=pl.ANY)] * count,
        out_specs=[pl.BlockSpec(memory_space=pl.ANY)] * count,
        out_shape=[jax.ShapeDtypeStruct((8,) + a.shape, a.dtype) for a in arrays],
        scratch_shapes=[
            SEM((len(chunks), 16)),
            SEM((len(chunks), 8, 2)),
        ],
        compiler_params=pltpu.CompilerParams(collective_id=collective_id, has_side_effects=True),
        name="gather_rows" if planes else "gather_keys",
    )(*arrays)


def weight_chunks(shapes, most=160 * 1024):
    chunks = []
    for a, (rows, cols) in enumerate(shapes):
        n = 1
        while rows * cols // n > most and rows % (32 * n) == 0:
            n *= 2
        k = 1
        while rows // n * cols // k > most and cols % (256 * k) == 0:
            k *= 2
        for i in range(n):
            lo, hi = rows // n * i, rows // n * (i + 1)
            mid = lo + -(-(hi - lo) // 32) * 16
            for j in range(k):
                c = pl.ds(cols // k * j, cols // k)
                chunks.append((a, (pl.ds(lo, mid - lo), c), (pl.ds(mid, hi - mid), c)))
    return chunks


def key_chunks(micro, blocks, rows, parts=2):
    return [
        (0,) + tuple(
            (m, pl.ds(blocks // 2 * h, blocks // 2), pl.ds(rows // parts * i, rows // parts))
            for h in range(2)
        )
        for m in range(micro)
        for i in range(parts)
    ]


def pieces_of(total, size):
    return [(lo, min(size, total - lo)) for lo in range(0, total, size)]


class Unit:
    def __init__(self, source, target, out, rows, cols, first):
        self.source, self.target, self.out = source, target, out
        self.rows, self.cols, self.first = rows, cols, first

    @property
    def shape(self):
        return (self.rows[1], self.cols[1])


def weight_units(sizes, most):
    units = []
    for source, target, out, rows, cols in sizes:
        k = 1
        while cols % (256 * k) == 0 and rows * cols // k > most:
            k *= 2
        high = -(-rows // max(1, round(rows * cols / k / most)) // 16) * 16
        for rows_cut in pieces_of(rows, high):
            for cols_cut in pieces_of(cols, cols // k):
                first = (ALONG_X, ALONG_Y)[len(units) % 2]
                units.append(Unit(source, target, out, rows_cut, cols_cut, first))
    return units


RING = 3


def ring_sizes(units):
    shapes = [u.shape for u in units if u.source is not None]
    return {a: min(RING, shapes.count(a)) for a in shapes}


def sum_kernel(units, n_src, n_tgt, n_out, tail, *refs):
    refs = list(refs)
    take = lambda n: [refs.pop(0) for _ in range(n)]
    far_src, far_tgt = take(n_src), take(n_tgt)
    if tail:
        far_keys, far_w, far_x, far_res = take(1)[0], take(3), *take(2)
        cos_ref, sin_ref, rr_ref, gain_ref, gain_two = take(5)
    outs = take(n_out)
    if tail:
        far_grad, total = take(2)
    n = len(units)
    held, core_in, one_in, two_in, line_in = (take(n) for _ in range(5))
    src, tgt = take(n_src), take(n_tgt)
    lhs = take(1)[0]
    depth = ring_sizes(units)
    rings = dict(zip(depth, take(len(depth))))
    load_src, load_tgt, sent, came, stored = take(5)
    if tail:
        dkv, w, x, res, dx, grad, gain_buf, key_load, tail_load, key_sent, key_came, gain_sent, gain_came = (
            *take(1), take(3), *take(11)
        )
    at, row = lax.axis_index("wide"), lax.axis_index("narrow")
    way = {bit: (at ^ bit, row) for bit in (CORE, ALONG_X, ALONG_Y)}
    near, across = (at, row ^ 1), (at, row ^ 3)
    middle = (row == 1) | (row == 2)
    is_keys = [u.source is None for u in units]

    loads = [pltpu.make_async_copy(a, b, load_src.at[i]) for i, (a, b) in enumerate(zip(far_src, src))]
    loads_tgt = [pltpu.make_async_copy(a, b, load_tgt.at[i]) for i, (a, b) in enumerate(zip(far_tgt, tgt))]
    tail_loads = []
    if tail:
        tail_loads = [
            pltpu.make_async_copy(a, b, tail_load.at[i])
            for i, (a, b) in enumerate(zip([*far_w, far_x, far_res], [*w, x, res]))
        ]
    ready = set()

    def need(copies, i):
        if (id(copies), i) not in ready:
            ready.add((id(copies), i))
            copies[i].wait()

    def send(c, slot, a, b, to):
        return pltpu.make_async_remote_copy(
            src_ref=a, dst_ref=b, send_sem=sent.at[c, slot], recv_sem=came.at[c, slot],
            device_id=to, device_id_type=pl.DeviceIdType.MESH,
        )

    def add(dst, other):
        rows = dst.shape[-2]
        most = rows // 16
        step = 16 * max(k for k in (1, 2, 3, 4) if most % k == 0)

        def body(i, carry):
            cut = pl.ds(pl.multiple_of(i * step, 16), step)
            dst[cut, :] = dst[cut, :] + other[cut, :]
            return carry

        lax.fori_loop(0, most * 16 // step, body, 0)
        if rows % 16:
            cut = slice(most * 16, rows)
            dst[cut, :] = dst[cut, :] + other[cut, :]

    def order(c):
        first = units[c].first
        return (0, FAR - first, first, FAR)

    def slot_of(c):
        alike = [i for i in range(n) if not is_keys[i] and units[i].shape == units[c].shape]
        return alike.index(c) % depth[units[c].shape]

    def same_slot(i, c):
        alike = not is_keys[i] and not is_keys[c] and units[i].shape == units[c].shape
        return alike and slot_of(i) == slot_of(c)

    def core_copies(c):
        if is_keys[c]:
            rows = pl.ds(*units[c].rows)
            return [
                pltpu.make_async_remote_copy(
                    src_ref=far_keys.at[at ^ CORE ^ m, rows], dst_ref=core_in[c].at[i],
                    send_sem=key_sent.at[c, i], recv_sem=key_came.at[c, i],
                    device_id=way[CORE], device_id_type=pl.DeviceIdType.MESH,
                )
                for i, m in enumerate(order(c))
            ]
        return [send(c, 0, rings[units[c].shape].at[slot_of(c)], core_in[c], way[CORE])]

    def key_loads(c):
        rows = pl.ds(*units[c].rows)
        return [
            pltpu.make_async_copy(far_keys.at[at ^ m, rows], held[c].at[i], key_load.at[c, i])
            for i, m in enumerate(order(c))
        ]

    def first_copy(c):
        return send(c, 1, held[c].at[pl.ds(2, 2)], one_in[c], way[units[c].first])

    def second_copy(c):
        return send(c, 2, held[c].at[1], two_in[c], way[FAR - units[c].first])

    def inward(c):
        return send(c, 3, held[c].at[0], line_in[c].at[0], near)

    def over(c):
        return send(c, 4, held[c].at[0], line_in[c].at[1], across)

    def outward(c):
        return send(c, 3, line_in[c].at[1], line_in[c].at[0], near)

    def store(c, slot):
        cut = (pl.ds(*units[c].rows), pl.ds(*units[c].cols))
        return pltpu.make_async_copy(line_in[c].at[slot], outs[units[c].out].at[cut], stored.at[c])

    def products(c, mine):
        u = units[c]
        rows, cols = u.shape
        whole = pl.ds(*u.rows)
        if u.source is not None:
            need(loads, u.source)
        b = dkv if u.target is None else tgt[u.target]
        if u.target is not None:
            need(loads_tgt, u.target)
        for i, m in enumerate(order(c)):
            lhs[pl.ds(i * rows, rows), :] = src[u.source][at ^ m ^ mine, whole, :]
        a = lhs[pl.ds(0, 4 * rows), :]
        into = (lambda cut: held[c].at[:, :, cut]) if mine == 0 else (
            lambda cut: rings[u.shape].at[slot_of(c), :, :, cut]
        )

        def one(lo, size, start):
            got = dot(a, b[pl.ds(start, size), :], 1, 1).astype(BF16)
            into(lo)[...] = got.reshape(4, rows, size)

        for lo, size in pieces_of(cols, 256):
            one(pl.ds(lo, size), size, u.cols[0] + lo)

    def s0(c):
        if is_keys[c]:
            for r in core_copies(c) + key_loads(c):
                r.start()
            return
        before = [i for i in range(c) if same_slot(i, c)]
        if before:
            core_copies(before[-1])[0].wait_send()
        products(c, CORE)
        core_copies(c)[0].start()
        products(c, 0)

    def s1(c):
        if is_keys[c]:
            for r in key_loads(c):
                r.wait()
        for r in core_copies(c):
            r.wait_recv()
        for i in (2, 3, 0, 1):
            add(held[c].at[i], core_in[c].at[i])
            if i == 3:
                first_copy(c).start()

    def s2(c):
        first_copy(c).wait_recv()
        add(held[c].at[1], one_in[c].at[1])
        second_copy(c).start()
        add(held[c].at[0], one_in[c].at[0])

    def s3(c):
        second_copy(c).wait_recv()
        add(held[c].at[0], two_in[c])
        if is_keys[c]:
            keys_done(c)
        else:
            pl.when(~middle)(lambda: inward(c).start())

    def s4(c):
        @pl.when(middle)
        def _():
            inward(c).wait_recv()
            add(held[c].at[0], line_in[c].at[0])
            over(c).start()

    def s5(c):
        @pl.when(middle)
        def _():
            over(c).wait_recv()
            add(line_in[c].at[1], held[c].at[0])
            outward(c).start()
            store(c, 1).start()

    def s6(c):
        @pl.when(~middle)
        def _():
            outward(c).wait_recv()
            store(c, 0).start()

    def keys_done(c):
        lanes = slice(c * BLOCK, (c + 1) * BLOCK)
        cs, sn = cos_ref[:, lanes], sin_ref[:, lanes]
        half, kd = HDIM // 2, dkv.shape[0] // 2
        for h in range(0, kd, HDIM):
            one = held[c][0, h : h + half, :].astype(F32)
            two = held[c][0, h + half : h + HDIM, :].astype(F32)
            dkv[h : h + half, lanes] = (one * cs + two * sn).astype(BF16)
            dkv[h + half : h + HDIM, lanes] = (two * cs - one * sn).astype(BF16)
        dkv[kd:, lanes] = held[c][0, kd:, :]

    def input_grad():
        for i in range(len(tail_loads)):
            need(tail_loads, i)
        kd = dkv.shape[0] // 2
        width = x.shape[0]
        rr = rr_ref[...]
        mean = jnp.zeros_like(rr)
        for lo, size in pieces_of(width, 128):
            cut = slice(lo, lo + size)
            d = dot(w[0][cut, :], tgt[0][...], 1, 0)
            d += dot(w[1][cut, :], dkv[:kd, :], 1, 0)
            d += dot(w[2][cut, :], dkv[kd:, :], 1, 0)
            dx[cut, :] = d
            xf = x[cut, :].astype(F32)
            p = d * xf
            mean += jnp.sum(p * gain_ref[cut, :], axis=0, keepdims=True)
            g = jnp.sum(p * rr, axis=1, keepdims=True)
            gain_buf[0, 0:1, cut] = jnp.broadcast_to(g, (size, BLOCK)).T[0:1]
        gain_buf[0, 1:2, :] = gain_two[...]
        mean = mean * (rr * rr * rr / width)
        for lo, size in pieces_of(width, 128):
            cut = slice(lo, lo + size)
            g = res[cut, :] + rr * (dx[cut, :] * gain_ref[cut, :]) - x[cut, :].astype(F32) * mean
            grad[:, cut] = g.T
        pltpu.make_async_copy(grad, far_grad, tail_load.at[len(tail_loads)]).start()

    gain_ways = [way[CORE], way[ALONG_X], way[ALONG_Y], near, across]

    def gain_copy(i):
        return pltpu.make_async_remote_copy(
            src_ref=gain_buf.at[2 * i], dst_ref=gain_buf.at[2 * i + 1], send_sem=gain_sent.at[i],
            recv_sem=gain_came.at[i], device_id=gain_ways[i], device_id_type=pl.DeviceIdType.MESH,
        )

    def gain_step(i):
        if i:
            gain_copy(i - 1).wait_recv()
            gain_buf[2 * i] = gain_buf[2 * i - 2] + gain_buf[2 * i - 1]
        if i < len(gain_ways):
            gain_copy(i).start()

    for r in loads + loads_tgt + tail_loads:
        r.start()
    meet([*way.values(), near, across])
    steps = (s0, s1, s2, s3, s4, s5, s6)
    begins, after = [], 0
    for c in range(n):
        begins.append(c if not begins else begins[-1] + 1)
        if is_keys[c]:
            after = begins[-1] + 3 * LAGS + 1
        elif units[c].target is None:
            begins[-1] = max(begins[-1], after)
    gains_at = 0
    for t in range(begins[-1] + LAGS * (len(steps) - 1) + 1):
        for s, step in enumerate(steps):
            for c in range(n):
                if begins[c] + LAGS * s == t and not (is_keys[c] and s > 3):
                    step(c)
        if tail and t == after:
            input_grad()
        if tail and t >= after and gains_at <= len(gain_ways):
            gain_step(gains_at)
            gains_at += 1
    if tail:
        for i in range(gains_at, len(gain_ways) + 1):
            gain_step(i)
        total[...] = gain_buf[2 * len(gain_ways)]
    for c in range(n):
        if not any(same_slot(c, i) for i in range(c + 1, n)):
            for r in core_copies(c):
                r.wait_send()
        first_copy(c).wait_send()
        second_copy(c).wait_send()
        if not is_keys[c]:
            inward(c).wait_send()
            pl.when(middle)(lambda: over(c).wait_send())
            store(c, 0).wait()
    if tail:
        for i in range(len(gain_ways)):
            gain_copy(i).wait_send()
        pltpu.make_async_copy(grad, far_grad, tail_load.at[len(tail_loads)]).wait()


def sums(units, sources, targets, out_shapes, collective_id, tail=None):
    n = len(units)
    anywhere = pl.BlockSpec(memory_space=pl.ANY)
    vmem = pl.BlockSpec(memory_space=pltpu.VMEM)
    room = lambda *lead: [pltpu.VMEM(lead + u.shape, BF16) for u in units]
    line = [pltpu.VMEM((2,) + u.shape if u.source is not None else (8, BLOCK), BF16) for u in units]
    tokens = sources[0].shape[2]
    rows = max(u.shape[0] for u in units if u.source is not None)
    scratch = room(4) + room(4) + room(2) + room() + line
    scratch += [pltpu.VMEM(a.shape, BF16) for a in (*sources, *targets)]
    scratch += [pltpu.VMEM((4 * rows, tokens), BF16)]
    scratch += [pltpu.VMEM((d, 4) + a, BF16) for a, d in ring_sizes(units).items()]
    scratch += [SEM((len(sources),)), SEM((len(targets),)), SEM((n, 5)), SEM((n, 5)), SEM((n,))]
    args = [*sources, *targets]
    specs = [anywhere] * len(args)
    out_shape = [jax.ShapeDtypeStruct(s, BF16) for s in out_shapes]
    out_specs = [anywhere] * len(out_shapes)
    if tail:
        big, small = tail[:6], tail[6:]
        args += [*big, *small]
        specs += [anywhere] * len(big) + [vmem] * len(small)
        width = big[4].shape[0]
        out_shape += [jax.ShapeDtypeStruct((tokens, width), F32), jax.ShapeDtypeStruct((2, width), F32)]
        out_specs += [anywhere, vmem]
        scratch += [pltpu.VMEM((big[0].shape[1] * BLOCK // tokens, tokens), BF16)]
        scratch += [pltpu.VMEM(a.shape, a.dtype) for a in big[1:]]
        scratch += [pltpu.VMEM((width, tokens), F32), pltpu.VMEM((tokens, width), F32)]
        scratch += [pltpu.VMEM((11, 2, width), F32), SEM((n, 4)), SEM((6,)), SEM((n, 4)), SEM((n, 4))]
        scratch += [SEM((5,)), SEM((5,))]
    return pl.pallas_call(
        functools.partial(sum_kernel, units, len(sources), len(targets), len(out_shapes), bool(tail)),
        in_specs=specs,
        out_specs=out_specs,
        out_shape=out_shape,
        scratch_shapes=scratch,
        compiler_params=pltpu.CompilerParams(
            collective_id=collective_id, has_side_effects=True, vmem_limit_bytes=60 * 1024 * 1024
        ),
        name="sum_with_keys" if tail else "sum_weights",
    )(*args)


def row_sum(part, size):
    if size != 4:
        return lax.psum(part, "narrow")
    add = lambda a, b: (a.astype(F32) + b.astype(F32)).astype(BF16)
    part = add(part, lax.ppermute(part, "narrow", [(0, 1), (3, 2)]))
    part = add(part, lax.ppermute(part, "narrow", [(1, 2), (2, 1)]))
    back = lax.ppermute(part, "narrow", [(1, 0), (2, 3)])
    at = lax.axis_index("narrow")
    return jnp.where((at == 1) | (at == 2), part, back)


def turn(v, cos, sin):
    heads = v.reshape(-1, 2, HDIM // 2, v.shape[1])
    one, two = heads[:, 0], heads[:, 1]
    return jnp.stack([one * cos - two * sin, two * cos + one * sin], axis=1).reshape(v.shape)


def turn_back(v, cos, sin):
    return turn(v, cos, -sin)


def shards(sizes, tokens, lengths, block_plan, attn_gain, w_query, w_key, w_value, w_out, ffn_gain,
           w_gate, w_up, w_down, cotangent):
    n = sizes["wide"]
    at = lax.axis_index("wide")
    micro, _, slots, width = tokens.shape
    total = micro * slots
    kd = w_key.shape[1]
    ff = w_gate.shape[1]
    nq = slots // BLOCK
    nb = nq * n

    plan = block_plan[:, 0]
    sizes_of = lengths[:, 0]
    docs = sizes_of.shape[1]
    upto = jnp.arange(docs)[:, None] >= jnp.arange(docs)[None, :]
    ends = jnp.sum(jnp.where(upto[None], sizes_of[:, None, :], 0), axis=2)
    own_plan = lax.dynamic_slice_in_dim(plan, at * nq, nq, axis=1)
    position = own_plan[:, :, None] * BLOCK + jnp.arange(BLOCK, dtype=jnp.int32)
    start = jnp.sum(
        jnp.where(position[..., None] >= ends[:, None, None, :], sizes_of[:, None, None, :], 0), axis=3
    )
    info = jnp.stack([start[:, :, 0] // BLOCK, own_plan], axis=1)
    slot_block = jnp.arange(nb, dtype=jnp.int32)
    where_is = jnp.sum(
        jnp.where(plan[:, None, :] == slot_block[None, :, None], slot_block[None, None, :], 0), axis=2
    )
    start = start.reshape(1, total)
    local = position.reshape(1, total) - start
    frequency = ROPE_BASE ** (-2.0 * jnp.arange(HDIM // 2, dtype=F32) / HDIM)
    angles = frequency[:, None] * local.astype(F32)
    cos, sin = jnp.cos(angles), jnp.sin(angles)

    cube = n == CUBE and sizes["narrow"] == 4 and nq % 2 == 0

    def whole_rows(*shards_of):
        if cube:
            got = gather(shards_of, weight_chunks([a.shape for a in shards_of]), True, 1)
        else:
            got = [lax.all_gather(a, "wide", axis=0) for a in shards_of]
        return [a.reshape(-1, a.shape[2]) for a in got]

    def whole_keys(own):
        if cube:
            return gather([own], key_chunks(*own.shape[:3]), False, 2)[0]
        return lax.all_gather(own, "wide", axis=0)

    def shared(a):
        return a.reshape(n, -1, a.shape[1])

    def row_part(source, target):
        part = dot(source, target, 1, 1).astype(BF16)
        own = lax.psum_scatter(part, "wide", scatter_dimension=0, tiled=True)
        return row_sum(own, sizes["narrow"])

    x_t = tokens.reshape(total, width).T
    ct_t = cotangent.reshape(total, width).T
    x = x_t.astype(F32)

    g_query, g_key, g_value, g_out, g_gate, g_up, g_down = whole_rows(
        w_query, w_key, w_value, w_out, w_gate, w_up, w_down
    )
    rr1 = lax.rsqrt(jnp.mean(x * x, axis=0, keepdims=True) + EPS)
    xn = (x * rr1 * attn_gain[:, None]).astype(BF16)
    key_t = turn(dot(g_key, xn, 0, 0), cos, sin).astype(BF16)
    value_t = dot(g_value, xn, 0, 0).astype(BF16)
    own_kv = jnp.concatenate([key_t, value_t]).reshape(2 * kd, micro, nq, BLOCK).transpose(1, 2, 0, 3)
    q_t = (turn(dot(g_query, xn, 0, 0), cos, sin).astype(BF16) * HDIM**-0.5).astype(BF16)

    kv = whole_keys(own_kv)
    att_t, lse = attention_fwd(info, where_is, q_t, start, kv)

    res = x + dot(g_out, att_t, 0, 0)
    rr2 = lax.rsqrt(jnp.mean(res * res, axis=0, keepdims=True) + EPS)
    hn = (res * rr2 * ffn_gain[:, None]).astype(BF16)
    gate = dot(g_gate, hn, 0, 0)
    up = dot(g_up, hn, 0, 0)
    sg = 1.0 / (1.0 + jnp.exp(-gate))
    hidden = (gate * sg * up).astype(BF16)
    out = (res + dot(g_down, hidden, 0, 0)).astype(BF16).T

    d_hidden = dot(g_down, ct_t, 1, 0)
    d_gate = (d_hidden * up * sg * (1.0 + gate * (1.0 - sg))).astype(BF16)
    d_up = (d_hidden * gate * sg).astype(BF16)
    d_hn = dot(g_gate, d_gate, 1, 0) + dot(g_up, d_up, 1, 0)
    u = d_hn * ffn_gain[:, None]
    d_res = (
        ct_t.astype(F32) + rr2 * u - res * rr2**3 * jnp.mean(u * res, axis=0, keepdims=True)
    )
    gain_two = jnp.sum(d_hn * res * rr2, axis=1)
    d_attn = d_res.astype(BF16)
    do_t = dot(g_out, d_attn, 1, 0).astype(BF16)

    pairs = [(hidden, ct_t), (hn, d_gate), (hn, d_up), (att_t, d_attn)]
    if cube:
        units = weight_units(
            [(0, 0, 0, ff // n, width), (1, 1, 1, width // n, ff), (1, 2, 2, width // n, ff),
             (2, 3, 3, width // n, width)], 80 * 1024,
        )
        s_down, s_gate, s_up, s_out = sums(
            units,
            [shared(hidden), shared(hn), shared(att_t)],
            [ct_t, d_gate, d_up, d_attn],
            [(ff // n, width), (width // n, ff), (width // n, ff), (width // n, width)],
            3,
        )
    else:
        s_down, s_gate, s_up, s_out = [row_part(*p) for p in pairs]

    dq, dkv = attention_bwd(info, where_is, q_t, do_t, att_t, lse, start, cos, sin, kv)
    if cube:
        blocks = micro * nq
        keys = dkv.reshape(n, blocks * 2 * kd, BLOCK)
        units = [
            Unit(None, None, None, (2 * kd * i, 2 * kd), (0, BLOCK), (ALONG_X, ALONG_Y)[i % 2])
            for i in range(blocks)
        ] + weight_units(
            [(0, 0, 0, width // n, width), (0, None, 1, width // n, 2 * kd)], 80 * 1024
        )
        s_query, s_kv, grad_x, gains = sums(
            units,
            [shared(xn)],
            [dq],
            [(width // n, width), (width // n, 2 * kd)],
            4,
            (keys, g_query, g_key, g_value, x_t, d_res, cos, sin, rr1, attn_gain[:, None], gain_two[None]),
        )
        s_key, s_value = s_kv[:, :kd], s_kv[:, kd:]
    else:
        dkv = lax.psum_scatter(dkv, "wide", scatter_dimension=0).transpose(2, 0, 1, 3).reshape(2 * kd, total)
        dk = turn_back(dkv[:kd].astype(F32), cos, sin).astype(BF16)
        dv = dkv[kd:]
        d_xn = dot(g_query, dq, 1, 0) + dot(g_key, dk, 1, 0) + dot(g_value, dv, 1, 0)
        u = d_xn * attn_gain[:, None]
        grad_x = (d_res + rr1 * u - x * rr1**3 * jnp.mean(u * x, axis=0, keepdims=True)).T
        gain_one = jnp.sum(d_xn * x * rr1, axis=1)
        s_query, s_key, s_value = row_part(xn, dq), row_part(xn, dk), row_part(xn, dv)
        gains = lax.psum(jnp.stack([gain_one, gain_two]), ("wide", "narrow"))

    shape = (micro, 1, slots, width)
    wide_out = lambda a: a.astype(F32)
    return (
        out.reshape(shape),
        grad_x.reshape(shape),
        gains[0],
        wide_out(s_query),
        wide_out(s_key),
        wide_out(s_value),
        wide_out(s_out),
        gains[1],
        wide_out(s_gate),
        wide_out(s_up),
        wide_out(s_down),
    )


def solution(mesh):
    by_slot = P(None, "narrow", "wide", None)
    by_row = P(None, "narrow", None)
    split = P("wide", None)
    in_specs = (
        by_slot, by_row, by_row, P(), split, split, split, split, P(), split, split, split, by_slot,
    )
    out_specs = (
        by_slot, by_slot, P(), split, split, split, split, P(), split, split, split,
    )
    return jax.shard_map(
        functools.partial(shards, dict(mesh.shape)),
        mesh=mesh,
        in_specs=in_specs,
        out_specs=out_specs,
        check_vma=False,
    )
```

```python
import functools

import jax
import jax.numpy as jnp
from jax import lax
from jax.experimental import pallas as pl
from jax.experimental.pallas import tpu as pltpu
from jax.sharding import PartitionSpec as P

HDIM = 64
BLOCK = 128
EPS = 1e-05
ROPE_BASE = 100000.0
NEG_FILL = -1e30
F32 = jnp.float32
BF16 = jnp.bfloat16
VMEM_LIMIT = 56 * 1024 * 1024


def dot(a, b, ca, cb):
    return lax.dot_general(a, b, (((ca,), (cb,)), ((), ())), preferred_element_type=F32)


def live_mask(qpos, start, p):
    kpos = p * BLOCK + lax.broadcasted_iota(jnp.int32, (BLOCK, BLOCK), 0)
    return (kpos <= qpos) & (kpos >= start)


STEP = 2


def pick(kv_ref, kvat, mb, qpos, start, b, t, share):
    nq = kv_ref.shape[2]
    blocks = [b - STEP * t - i for i in range(STEP)]
    slots = [kvat[mb, jnp.maximum(p, 0)] for p in blocks]
    at = [(lax.div(s, nq), lax.rem(s, nq)) for s in slots]
    ok = jnp.concatenate([live_mask(qpos, start, p) for p in blocks], axis=0)

    def keys(g):
        rows = slice(g * HDIM, (g + 1) * HDIM)
        return jnp.concatenate([kv_ref[d, 0, s, rows, :] for d, s in at], axis=1)

    return keys, at, jnp.concatenate([ok] * share, axis=1)


def fwd_kernel(groups, share, info, kvat, q_ref, start_ref, kv_ref, o_ref, lse_ref, qs, m_s, l_s, acc, s_s, w_s):
    mb, i = pl.program_id(0), pl.program_id(1)
    lo, b = info[mb, 0, i], info[mb, 1, i]
    nq = kv_ref.shape[2]
    lanes = share * BLOCK
    for g in range(groups):
        for h in range(share):
            at = (g * share + h) * HDIM
            qs[g, :, h * BLOCK : (h + 1) * BLOCK] = q_ref[at : at + HDIM, :]
    m_s[...] = jnp.full_like(m_s, NEG_FILL)
    l_s[...] = jnp.zeros_like(l_s)
    acc[...] = jnp.zeros_like(acc)
    qpos = b * BLOCK + lax.broadcasted_iota(jnp.int32, (1, BLOCK), 1)
    start = start_ref[...]

    def step(t, carry):
        keys, at, ok = pick(kv_ref, kvat, mb, qpos, start, b, t, share)
        for g in range(groups):
            s_s[g] = jnp.where(ok, dot(keys(g), qs[g], 0, 0), NEG_FILL)
        alphas = []
        for g in range(groups):
            s = s_s[g]
            m_old = m_s[g]
            m_new = jnp.maximum(m_old, jnp.max(s, axis=0, keepdims=True))
            w = jnp.exp(s - m_new)
            alpha = jnp.exp(m_old - m_new)
            l_s[g] = l_s[g] * alpha + jnp.sum(w, axis=0, keepdims=True)
            m_s[g] = m_new
            w_s[g] = w.astype(BF16)
            alphas.append(alpha)
        for g in range(groups):
            acc[g] = acc[g] * alphas[g] + dot(keys(groups + g), w_s[g], 1, 0)
        return carry

    lax.fori_loop(0, (b - lo + STEP) // STEP, step, 0)
    for g in range(groups):
        total = l_s[g]
        out = (acc[g] / total).astype(BF16)
        for h in range(share):
            at = (g * share + h) * HDIM
            o_ref[at : at + HDIM, :] = out[:, h * BLOCK : (h + 1) * BLOCK]
        lse_ref[0, g : g + 1, :] = m_s[g] + jnp.log(total)


def attention_fwd(info, kvat, q_t, start, kv):
    width = q_t.shape[0]
    n, micro, nq, kvw, _ = kv.shape
    groups = kvw // HDIM // 2
    share = width // HDIM // groups
    lanes = share * BLOCK
    tok = lambda rows: pl.BlockSpec((rows, BLOCK), lambda m, i, *_: (0, m * nq + i))
    return pl.pallas_call(
        functools.partial(fwd_kernel, groups, share),
        grid_spec=pltpu.PrefetchScalarGridSpec(
            num_scalar_prefetch=2,
            grid=(micro, nq),
            in_specs=[
                tok(width),
                tok(1),
                pl.BlockSpec((n, 1, nq, kvw, BLOCK), lambda m, i, *_: (0, m, 0, 0, 0)),
            ],
            out_specs=[
                tok(width),
                pl.BlockSpec((1, groups, lanes), lambda m, i, *_: (m * nq + i, 0, 0)),
            ],
            scratch_shapes=[
                pltpu.VMEM((groups, HDIM, lanes), BF16),
                pltpu.VMEM((groups, 1, lanes), F32),
                pltpu.VMEM((groups, 1, lanes), F32),
                pltpu.VMEM((groups, HDIM, lanes), F32),
                pltpu.VMEM((groups, STEP * BLOCK, lanes), F32),
                pltpu.VMEM((groups, STEP * BLOCK, lanes), BF16),
            ],
        ),
        out_shape=[
            jax.ShapeDtypeStruct(q_t.shape, BF16),
            jax.ShapeDtypeStruct((micro * nq, groups, lanes), F32),
        ],
        compiler_params=pltpu.CompilerParams(vmem_limit_bytes=VMEM_LIMIT),
        cost_estimate=pl.CostEstimate(
            flops=int(1e10), bytes_accessed=int(8e6), transcendentals=int(8e6)
        ),
        name="attention_fwd",
    )(info, kvat, q_t, start, kv)


def bwd_kernel(
    groups, share, info, kvat, q_ref, do_ref, o_ref, lse_ref, start_ref, cos_ref, sin_ref, kv_ref,
    dq_ref, dkv_ref, qs, dos, delta, dq, dkv, s_s, d_s, w_s, ds_s,
):
    mb, i = pl.program_id(0), pl.program_id(1)
    lo, b = info[mb, 0, i], info[mb, 1, i]
    nq = kv_ref.shape[2]

    @pl.when(i == 0)
    def _():
        dkv[...] = jnp.zeros_like(dkv)

    for g in range(groups):
        for h in range(share):
            at = (g * share + h) * HDIM
            cols = slice(h * BLOCK, (h + 1) * BLOCK)
            d_out = do_ref[at : at + HDIM, :]
            qs[g, :, cols] = q_ref[at : at + HDIM, :]
            dos[g, :, cols] = d_out
            delta[g, :, cols] = jnp.sum(
                d_out.astype(F32) * o_ref[at : at + HDIM, :].astype(F32), axis=0, keepdims=True
            )
    dq[...] = jnp.zeros_like(dq)
    qpos = b * BLOCK + lax.broadcasted_iota(jnp.int32, (1, BLOCK), 1)
    start = start_ref[...]

    def step(t, carry):
        keys, at, ok = pick(kv_ref, kvat, mb, qpos, start, b, t, share)
        for g in range(groups):
            s_s[g] = jnp.where(ok, dot(keys(g), qs[g], 0, 0), NEG_FILL)
            d_s[g] = dot(keys(groups + g), dos[g], 0, 0)
        for g in range(groups):
            w = jnp.exp(s_s[g] - lse_ref[0, g : g + 1, :])
            w_s[g] = w.astype(BF16)
            ds_s[g] = (w * (d_s[g] - delta[g])).astype(BF16)
        for g in range(groups):
            dq[g] += dot(keys(g), ds_s[g], 1, 0)
            dk = dot(qs[g], ds_s[g], 1, 1)
            dv = dot(dos[g], w_s[g], 1, 1)
            krows = slice(g * HDIM, (g + 1) * HDIM)
            vrows = slice((groups + g) * HDIM, (groups + g + 1) * HDIM)
            for i in range(STEP):
                cols = slice(i * BLOCK, (i + 1) * BLOCK)
                dkv[at[i][0], at[i][1], krows, :] += dk[:, cols]
                dkv[at[i][0], at[i][1], vrows, :] += dv[:, cols]
        return carry

    lax.fori_loop(0, (b - lo + STEP) // STEP, step, 0)
    cos, sin = cos_ref[...], sin_ref[...]
    half = HDIM // 2
    for g in range(groups):
        for h in range(share):
            at = (g * share + h) * HDIM
            one = dq[g, :half, h * BLOCK : (h + 1) * BLOCK] * HDIM**-0.5
            two = dq[g, half:, h * BLOCK : (h + 1) * BLOCK] * HDIM**-0.5
            dq_ref[at : at + half, :] = (one * cos + two * sin).astype(BF16)
            dq_ref[at + half : at + HDIM, :] = (two * cos - one * sin).astype(BF16)

    @pl.when(i == nq - 1)
    def _():
        dkv_ref[:, 0] = dkv[...].astype(BF16)


def attention_bwd(info, kvat, q_t, do_t, o_t, lse, start, cos_t, sin_t, kv):
    width = q_t.shape[0]
    n, micro, nq, kvw, _ = kv.shape
    groups = kvw // HDIM // 2
    share = width // HDIM // groups
    lanes = share * BLOCK
    tok = lambda rows: pl.BlockSpec((rows, BLOCK), lambda m, i, *_: (0, m * nq + i))
    keys = pl.BlockSpec((n, 1, nq, kvw, BLOCK), lambda m, i, *_: (0, m, 0, 0, 0))
    return pl.pallas_call(
        functools.partial(bwd_kernel, groups, share),
        grid_spec=pltpu.PrefetchScalarGridSpec(
            num_scalar_prefetch=2,
            grid=(micro, nq),
            in_specs=[
                tok(width),
                tok(width),
                tok(width),
                pl.BlockSpec((1, groups, lanes), lambda m, i, *_: (m * nq + i, 0, 0)),
                tok(1),
                tok(HDIM // 2),
                tok(HDIM // 2),
                keys,
            ],
            out_specs=[tok(width), keys],
            scratch_shapes=[
                pltpu.VMEM((groups, HDIM, lanes), BF16),
                pltpu.VMEM((groups, HDIM, lanes), BF16),
                pltpu.VMEM((groups, 1, lanes), F32),
                pltpu.VMEM((groups, HDIM, lanes), F32),
                pltpu.VMEM((n, nq, kvw, BLOCK), F32),
                pltpu.VMEM((groups, STEP * BLOCK, lanes), F32),
                pltpu.VMEM((groups, STEP * BLOCK, lanes), F32),
                pltpu.VMEM((groups, STEP * BLOCK, lanes), BF16),
                pltpu.VMEM((groups, STEP * BLOCK, lanes), BF16),
            ],
        ),
        out_shape=[
            jax.ShapeDtypeStruct(q_t.shape, BF16),
            jax.ShapeDtypeStruct(kv.shape, BF16),
        ],
        compiler_params=pltpu.CompilerParams(vmem_limit_bytes=VMEM_LIMIT),
        cost_estimate=pl.CostEstimate(
            flops=int(2e10), bytes_accessed=int(16e6), transcendentals=int(8e6)
        ),
        name="attention_bwd",
    )(info, kvat, q_t, do_t, o_t, lse, start, cos_t, sin_t, kv)


CORE, ALONG_X, ALONG_Y = 1, 2, 4
FAR = ALONG_X + ALONG_Y
CUBE = 8
LAG = 2
LAGS = 2
SEM = pltpu.SemaphoreType.DMA


def meet(peers):
    barrier = pltpu.get_barrier_semaphore()
    for peer in peers:
        pl.semaphore_signal(barrier, inc=1, device_id=peer, device_id_type=pl.DeviceIdType.MESH)
    pl.semaphore_wait(barrier, len(peers))


def weight_chunks(shapes, most=160 * 1024):
    chunks = []
    for a, (rows, cols) in enumerate(shapes):
        n = 1
        while rows * cols // n > most and rows % (32 * n) == 0:
            n *= 2
        k = 1
        while rows // n * cols // k > most and cols % (256 * k) == 0:
            k *= 2
        for i in range(n):
            lo, hi = rows // n * i, rows // n * (i + 1)
            mid = lo + -(-(hi - lo) // 32) * 16
            for j in range(k):
                c = pl.ds(cols // k * j, cols // k)
                chunks.append((a, (pl.ds(lo, mid - lo), c), (pl.ds(mid, hi - mid), c)))
    return chunks


def pieces_of(total, size):
    return [(lo, min(size, total - lo)) for lo in range(0, total, size)]


def start_kernel(chunks, micro, *refs):
    refs = list(refs)
    take_refs = lambda n: [refs.pop(0) for _ in range(n)]
    ins = take_refs(7)
    far_x, gain_ref, cos_ref, sin_ref = take_refs(4)
    outs = take_refs(7)
    far_q, far_xn, far_kv, rr_ref = take_refs(4)
    near_w = take_refs(3)
    x, xn, q_s, own_kv, sent, came, local = take_refs(7)
    at, row = lax.axis_index("wide"), lax.axis_index("narrow")
    peer = {bit: (at ^ bit, row) for bit in (CORE, ALONG_X, ALONG_Y)}
    peer["row"] = (at, row ^ 1)
    keys = len(ins)
    source = [*ins, own_kv]
    land = [*near_w, *outs[3:], far_kv]
    n = len(chunks)
    kd = own_kv.shape[2] // 2
    nq = own_kv.shape[1]
    width, half = q_s.shape[0], HDIM // 2

    mine_in = [pltpu.make_async_copy(ins[i], near_w[i].at[at], local.at[i]) for i in range(3)]
    mine_in.append(pltpu.make_async_copy(far_x, x, local.at[3]))
    give = [pltpu.make_async_copy(near_w[i], outs[i], local.at[4 + i]) for i in range(3)]
    give_q = pltpu.make_async_copy(q_s, far_q, local.at[7])
    give_xn = pltpu.make_async_copy(xn, far_xn, local.at[8])
    give_kv = pltpu.make_async_copy(own_kv, far_kv.at[at], local.at[9])

    def norm():
        mine_in[3].wait()
        count = x.shape[0]
        square = jnp.zeros(rr_ref.shape, F32)
        for j in range(count):
            v = x[j].astype(F32)
            square += jnp.sum(v * v, axis=0, keepdims=True)
        rr = lax.rsqrt(square / width + EPS)
        rr_ref[...] = rr
        for j in range(count):
            xn[j] = (x[j].astype(F32) * rr * gain_ref[j]).astype(BF16)
        give_xn.start()

    def turned(w, lo, size):
        got = sum(dot(w[j, :, lo : lo + size], xn[j], 0, 0) for j in range(w.shape[0]))
        return got

    def heads(got):
        cos, sin = cos_ref[...], sin_ref[...]
        for h in range(0, got.shape[0], HDIM):
            one, two = got[h : h + half], got[h + half : h + HDIM]
            yield h, one * cos - two * sin
            yield h + half, two * cos + one * sin

    def to_keys(at_row, value):
        value = value.astype(BF16)
        for m in range(micro):
            for i in range(nq):
                lanes = slice((m * nq + i) * BLOCK, (m * nq + i + 1) * BLOCK)
                own_kv[m, i, at_row : at_row + value.shape[0], :] = value[:, lanes]

    def key_tile(lo, size):
        for h, v in heads(turned(near_w[1], lo, size)):
            to_keys(lo + h, v)

    def value_tile(lo, size):
        to_keys(kd + lo, turned(near_w[2], lo, size))

    def query_tile(lo, size):
        for h, v in heads(turned(near_w[0], lo, size)):
            q_s[lo + h : lo + h + half, :] = v.astype(BF16) * HDIM**-0.5

    def run(mine):
        other = 1 - mine
        used = [0] * n
        begun = []

        def part(ref, c, which):
            return ref.at[chunks[c][1 + which]]

        def copy(c, m, which, way, slot):
            a = chunks[c][0]
            there = part(land[a].at[at ^ m], c, which)
            return pltpu.make_async_remote_copy(
                src_ref=there if m else part(source[a], c, which),
                dst_ref=there,
                send_sem=sent.at[c, slot],
                recv_sem=came.at[c, m if way == "row" else m ^ way, which],
                device_id=peer[way],
                device_id_type=pl.DeviceIdType.MESH,
            )

        def push(c, m, which, way):
            r = copy(c, m, which, way, used[c])
            used[c] += 1
            r.start()
            begun.append(r)

        def take(c, m, which, *ways):
            copy(c, m ^ CORE, which, CORE, 0).wait_recv()
            for way in ways:
                push(c, m, which, way)

        planes = [c[0] != keys for c in chunks]
        bounced = [2 < c[0] < keys for c in chunks]

        def first(c):
            push(c, 0, mine, ALONG_X)
            push(c, 0, mine, ALONG_Y)
            if not planes[c]:
                push(c, 0, other, ALONG_X)
                push(c, 0, other, ALONG_Y)

        def second(c):
            if planes[c]:
                take(c, ALONG_Y, mine, ALONG_X, CORE)
                push(c, 0, other, ALONG_Y)
                take(c, ALONG_X, mine, "row", CORE)
            else:
                take(c, ALONG_X, mine, ALONG_Y, CORE)
                take(c, ALONG_Y, other, ALONG_X, CORE)
                take(c, ALONG_Y, mine, CORE)
                take(c, ALONG_X, other, CORE)
            push(c, 0, 0, CORE)
            push(c, 0, 1, CORE)

        def third(c):
            take(c, FAR, mine, *(("row", CORE) if planes[c] else (CORE,)))
            if planes[c]:
                take(c, ALONG_Y, other, CORE)
                take(c, ALONG_X, other, CORE)
            else:
                take(c, FAR, other, CORE)

        def fourth(c):
            if planes[c]:
                take(c, FAR, other, CORE)

        def fifth(c):
            for which in range(2):
                take(c, CORE, which, *((CORE,) if bounced[c] else ()))
            for m in (ALONG_X, ALONG_Y, FAR):
                for which in range(2):
                    take(c, m + CORE, which)

        def sixth(c):
            if bounced[c]:
                for which in range(2):
                    take(c, 0, which)

        steps = (first, second, third, fourth, fifth, sixth)
        begins, ready = [], 0
        for c in range(n):
            begins.append(c)
            if chunks[c][0] < 3:
                ready = c + LAG * 4
            if chunks[c][0] == keys:
                begins[c] = max(begins[c - 1] + 1, ready + 1)
        work = {1: [norm], ready: []}
        for lo, size in pieces_of(kd, 256):
            work[ready] += [functools.partial(key_tile, lo, size), functools.partial(value_tile, lo, size)]
        work[ready].append(give_kv.start)
        for i, (lo, size) in enumerate(pieces_of(width, 256)):
            work[ready + 2 + i] = [functools.partial(query_tile, lo, size)]
        for t in range(begins[-1] + LAG * (len(steps) - 1) + 1):
            for s, step in enumerate(steps):
                for c in range(n):
                    if begins[c] + LAG * s == t:
                        step(c)
            if t == ready:
                for r in mine_in[:3]:
                    r.wait()
                for r in give:
                    r.start()
            for job in work.get(t, ()):
                job()
        for r in begun:
            r.wait_send()

    for r in mine_in:
        r.start()
    meet(list(peer.values()))
    for mine in range(2):
        pl.when(row % 2 == mine)(functools.partial(run, mine))
    give_q.start()
    for r in (*give, give_q, give_xn, give_kv):
        r.wait()


def start_of(weights, x, gain, cos, sin, micro, collective_id):
    count, high, tokens = x.shape
    kd = weights[1].shape[1]
    nq = tokens // micro // BLOCK
    chunks = weight_chunks([a.shape for a in weights])
    keys = len(weights)
    for m in range(micro):
        for i in range(2):
            rows = pl.ds(kd * i, kd)
            halves = [(m, pl.ds(nq // 2 * h, nq // 2), rows) for h in range(2)]
            chunks.append((keys, *halves))
    anywhere = pl.BlockSpec(memory_space=pl.ANY)
    vmem = pl.BlockSpec(memory_space=pltpu.VMEM)
    shape = jax.ShapeDtypeStruct
    kv = (micro, nq, 2 * kd, BLOCK)
    got = pl.pallas_call(
        functools.partial(start_kernel, chunks, micro),
        in_specs=[anywhere] * (keys + 1) + [vmem] * 3,
        out_specs=[anywhere] * (keys + 3) + [vmem],
        out_shape=[shape((count,) + a.shape, BF16) for a in weights]
        + [shape((count * high, tokens), BF16), shape(x.shape, BF16), shape((count,) + kv, BF16)]
        + [shape((1, tokens), F32)],
        scratch_shapes=[pltpu.VMEM((count,) + a.shape, BF16) for a in weights[:3]]
        + [
            pltpu.VMEM(x.shape, BF16),
            pltpu.VMEM(x.shape, BF16),
            pltpu.VMEM((count * high, tokens), BF16),
            pltpu.VMEM(kv, BF16),
            SEM((len(chunks), 16)),
            SEM((len(chunks), 8, 2)),
            SEM((10,)),
        ],
        compiler_params=pltpu.CompilerParams(
            collective_id=collective_id, has_side_effects=True, vmem_limit_bytes=VMEM_LIMIT
        ),
        name="gather_and_project",
    )(*weights, x, gain, cos, sin)
    return got[:keys], got[keys], got[keys + 1], got[keys + 2], got[keys + 3]


class Unit:
    def __init__(self, source, target, out, rows, cols, first):
        self.source, self.target, self.out = source, target, out
        self.rows, self.cols, self.first = rows, cols, first

    @property
    def shape(self):
        return (self.rows[1], self.cols[1])


def weight_units(sizes, most):
    units = []
    for source, target, out, rows, cols in sizes:
        k = 1
        while cols % (256 * k) == 0 and rows * cols // k > most:
            k *= 2
        high = -(-rows // max(1, round(rows * cols / k / most)) // 16) * 16
        for rows_cut in pieces_of(rows, high):
            for cols_cut in pieces_of(cols, cols // k):
                first = (ALONG_X, ALONG_Y)[len(units) % 2]
                units.append(Unit(source, target, out, rows_cut, cols_cut, first))
    return units


RING = 3


def ring_sizes(units):
    shapes = [u.shape for u in units if u.source is not None]
    return {a: min(RING, shapes.count(a)) for a in shapes}


def sum_kernel(units, n_src, n_tgt, n_out, tail, *refs):
    refs = list(refs)
    take = lambda n: [refs.pop(0) for _ in range(n)]
    far_src, far_tgt = take(n_src), take(n_tgt)
    if tail:
        far_keys, far_w, far_x, far_res = take(1)[0], take(3), *take(2)
        cos_ref, sin_ref, rr_ref, gain_ref, gain_two = take(5)
    outs = take(n_out)
    if tail:
        far_grad, total = take(2)
    n = len(units)
    held, core_in, one_in, two_in, line_in = (take(n) for _ in range(5))
    src, tgt = take(n_src), take(n_tgt)
    lhs = take(1)[0]
    depth = ring_sizes(units)
    rings = dict(zip(depth, take(len(depth))))
    load_src, load_tgt, sent, came, stored = take(5)
    if tail:
        dkv, w, x, res, dx, grad, gain_buf, key_load, tail_load, key_sent, key_came, gain_sent, gain_came = (
            *take(1), take(3), *take(11)
        )
    at, row = lax.axis_index("wide"), lax.axis_index("narrow")
    way = {bit: (at ^ bit, row) for bit in (CORE, ALONG_X, ALONG_Y)}
    near, across = (at, row ^ 1), (at, row ^ 3)
    middle = (row == 1) | (row == 2)
    is_keys = [u.source is None for u in units]

    loads = [pltpu.make_async_copy(a, b, load_src.at[i]) for i, (a, b) in enumerate(zip(far_src, src))]
    loads_tgt = [pltpu.make_async_copy(a, b, load_tgt.at[i]) for i, (a, b) in enumerate(zip(far_tgt, tgt))]
    tail_loads = []
    if tail:
        tail_loads = [
            pltpu.make_async_copy(a, b, tail_load.at[i])
            for i, (a, b) in enumerate(zip([*far_w, far_x, far_res], [*w, x, res]))
        ]
    ready = set()

    def need(copies, i):
        if (id(copies), i) not in ready:
            ready.add((id(copies), i))
            copies[i].wait()

    def send(c, slot, a, b, to):
        return pltpu.make_async_remote_copy(
            src_ref=a, dst_ref=b, send_sem=sent.at[c, slot], recv_sem=came.at[c, slot],
            device_id=to, device_id_type=pl.DeviceIdType.MESH,
        )

    def add(dst, other):
        rows = dst.shape[-2]
        most = rows // 16
        step = 16 * max(k for k in (1, 2, 3, 4) if most % k == 0)

        def body(i, carry):
            cut = pl.ds(pl.multiple_of(i * step, 16), step)
            dst[cut, :] = dst[cut, :] + other[cut, :]
            return carry

        lax.fori_loop(0, most * 16 // step, body, 0)
        if rows % 16:
            cut = slice(most * 16, rows)
            dst[cut, :] = dst[cut, :] + other[cut, :]

    def order(c):
        first = units[c].first
        return (0, FAR - first, first, FAR)

    def slot_of(c):
        alike = [i for i in range(n) if not is_keys[i] and units[i].shape == units[c].shape]
        return alike.index(c) % depth[units[c].shape]

    def same_slot(i, c):
        alike = not is_keys[i] and not is_keys[c] and units[i].shape == units[c].shape
        return alike and slot_of(i) == slot_of(c)

    def core_copies(c):
        if is_keys[c]:
            rows = pl.ds(*units[c].rows)
            return [
                pltpu.make_async_remote_copy(
                    src_ref=far_keys.at[at ^ CORE ^ m, rows], dst_ref=core_in[c].at[i],
                    send_sem=key_sent.at[c, i], recv_sem=key_came.at[c, i],
                    device_id=way[CORE], device_id_type=pl.DeviceIdType.MESH,
                )
                for i, m in enumerate(order(c))
            ]
        return [send(c, 0, rings[units[c].shape].at[slot_of(c)], core_in[c], way[CORE])]

    def key_loads(c):
        rows = pl.ds(*units[c].rows)
        return [
            pltpu.make_async_copy(far_keys.at[at ^ m, rows], held[c].at[i], key_load.at[c, i])
            for i, m in enumerate(order(c))
        ]

    def first_copy(c):
        return send(c, 1, held[c].at[pl.ds(2, 2)], one_in[c], way[units[c].first])

    def second_copy(c):
        return send(c, 2, held[c].at[1], two_in[c], way[FAR - units[c].first])

    def inward(c):
        return send(c, 3, held[c].at[0], line_in[c].at[0], near)

    def over(c):
        return send(c, 4, held[c].at[0], line_in[c].at[1], across)

    def outward(c):
        return send(c, 3, line_in[c].at[1], line_in[c].at[0], near)

    def store(c, slot):
        cut = (pl.ds(*units[c].rows), pl.ds(*units[c].cols))
        return pltpu.make_async_copy(line_in[c].at[slot], outs[units[c].out].at[cut], stored.at[c])

    def products(c, mine):
        u = units[c]
        rows, cols = u.shape
        whole = pl.ds(*u.rows)
        if u.source is not None:
            need(loads, u.source)
        b = dkv if u.target is None else tgt[u.target]
        if u.target is not None:
            need(loads_tgt, u.target)
        for i, m in enumerate(order(c)):
            lhs[pl.ds(i * rows, rows), :] = src[u.source][at ^ m ^ mine, whole, :]
        a = lhs[pl.ds(0, 4 * rows), :]
        into = (lambda cut: held[c].at[:, :, cut]) if mine == 0 else (
            lambda cut: rings[u.shape].at[slot_of(c), :, :, cut]
        )

        def one(lo, size, start):
            got = dot(a, b[pl.ds(start, size), :], 1, 1).astype(BF16)
            into(lo)[...] = got.reshape(4, rows, size)

        for lo, size in pieces_of(cols, 256):
            one(pl.ds(lo, size), size, u.cols[0] + lo)

    def s0(c):
        if is_keys[c]:
            for r in core_copies(c) + key_loads(c):
                r.start()
            return
        before = [i for i in range(c) if same_slot(i, c)]
        if before:
            core_copies(before[-1])[0].wait_send()
        products(c, CORE)
        core_copies(c)[0].start()
        products(c, 0)

    def s1(c):
        if is_keys[c]:
            for r in key_loads(c):
                r.wait()
        for r in core_copies(c):
            r.wait_recv()
        for i in (2, 3, 0, 1):
            add(held[c].at[i], core_in[c].at[i])
            if i == 3:
                first_copy(c).start()

    def s2(c):
        first_copy(c).wait_recv()
        add(held[c].at[1], one_in[c].at[1])
        second_copy(c).start()
        add(held[c].at[0], one_in[c].at[0])

    def s3(c):
        second_copy(c).wait_recv()
        add(held[c].at[0], two_in[c])
        if is_keys[c]:
            keys_done(c)
        else:
            pl.when(~middle)(lambda: inward(c).start())

    def s4(c):
        @pl.when(middle)
        def _():
            inward(c).wait_recv()
            add(held[c].at[0], line_in[c].at[0])
            over(c).start()

    def s5(c):
        @pl.when(middle)
        def _():
            over(c).wait_recv()
            add(line_in[c].at[1], held[c].at[0])
            outward(c).start()
            store(c, 1).start()

    def s6(c):
        @pl.when(~middle)
        def _():
            outward(c).wait_recv()
            store(c, 0).start()

    def keys_done(c):
        lanes = slice(c * BLOCK, (c + 1) * BLOCK)
        cs, sn = cos_ref[:, lanes], sin_ref[:, lanes]
        half, kd = HDIM // 2, dkv.shape[0] // 2
        for h in range(0, kd, HDIM):
            one = held[c][0, h : h + half, :].astype(F32)
            two = held[c][0, h + half : h + HDIM, :].astype(F32)
            dkv[h : h + half, lanes] = (one * cs + two * sn).astype(BF16)
            dkv[h + half : h + HDIM, lanes] = (two * cs - one * sn).astype(BF16)
        dkv[kd:, lanes] = held[c][0, kd:, :]

    def input_grad():
        for i in range(len(tail_loads)):
            need(tail_loads, i)
        kd = dkv.shape[0] // 2
        width = x.shape[0]
        rr = rr_ref[...]
        mean = jnp.zeros_like(rr)
        for lo, size in pieces_of(width, 128):
            cut = slice(lo, lo + size)
            d = dot(w[0][cut, :], tgt[0][...], 1, 0)
            d += dot(w[1][cut, :], dkv[:kd, :], 1, 0)
            d += dot(w[2][cut, :], dkv[kd:, :], 1, 0)
            dx[cut, :] = d
            xf = x[cut, :].astype(F32)
            p = d * xf
            mean += jnp.sum(p * gain_ref[cut, :], axis=0, keepdims=True)
            g = jnp.sum(p * rr, axis=1, keepdims=True)
            gain_buf[0, 0:1, cut] = jnp.broadcast_to(g, (size, BLOCK)).T[0:1]
        gain_buf[0, 1:2, :] = gain_two[...]
        mean = mean * (rr * rr * rr / width)
        for lo, size in pieces_of(width, 128):
            cut = slice(lo, lo + size)
            g = res[cut, :] + rr * (dx[cut, :] * gain_ref[cut, :]) - x[cut, :].astype(F32) * mean
            grad[:, cut] = g.T
        pltpu.make_async_copy(grad, far_grad, tail_load.at[len(tail_loads)]).start()

    gain_ways = [way[CORE], way[ALONG_X], way[ALONG_Y], near, across]

    def gain_copy(i):
        return pltpu.make_async_remote_copy(
            src_ref=gain_buf.at[2 * i], dst_ref=gain_buf.at[2 * i + 1], send_sem=gain_sent.at[i],
            recv_sem=gain_came.at[i], device_id=gain_ways[i], device_id_type=pl.DeviceIdType.MESH,
        )

    def gain_step(i):
        if i:
            gain_copy(i - 1).wait_recv()
            gain_buf[2 * i] = gain_buf[2 * i - 2] + gain_buf[2 * i - 1]
        if i < len(gain_ways):
            gain_copy(i).start()

    for r in loads + loads_tgt + tail_loads:
        r.start()
    meet([*way.values(), near, across])
    steps = (s0, s1, s2, s3, s4, s5, s6)
    begins, after = [], 0
    for c in range(n):
        begins.append(c if not begins else begins[-1] + 1)
        if is_keys[c]:
            after = begins[-1] + 3 * LAGS + 1
        elif units[c].target is None:
            begins[-1] = max(begins[-1], after)
    gains_at = 0
    for t in range(begins[-1] + LAGS * (len(steps) - 1) + 1):
        for s, step in enumerate(steps):
            for c in range(n):
                if begins[c] + LAGS * s == t and not (is_keys[c] and s > 3):
                    step(c)
        if tail and t == after:
            input_grad()
        if tail and t >= after and gains_at <= len(gain_ways):
            gain_step(gains_at)
            gains_at += 1
    if tail:
        for i in range(gains_at, len(gain_ways) + 1):
            gain_step(i)
        total[...] = gain_buf[2 * len(gain_ways)]
    for c in range(n):
        if not any(same_slot(c, i) for i in range(c + 1, n)):
            for r in core_copies(c):
                r.wait_send()
        first_copy(c).wait_send()
        second_copy(c).wait_send()
        if not is_keys[c]:
            inward(c).wait_send()
            pl.when(middle)(lambda: over(c).wait_send())
            store(c, 0).wait()
    if tail:
        for i in range(len(gain_ways)):
            gain_copy(i).wait_send()
        pltpu.make_async_copy(grad, far_grad, tail_load.at[len(tail_loads)]).wait()


def sums(units, sources, targets, out_shapes, collective_id, tail=None):
    n = len(units)
    anywhere = pl.BlockSpec(memory_space=pl.ANY)
    vmem = pl.BlockSpec(memory_space=pltpu.VMEM)
    room = lambda *lead: [pltpu.VMEM(lead + u.shape, BF16) for u in units]
    line = [pltpu.VMEM((2,) + u.shape if u.source is not None else (8, BLOCK), BF16) for u in units]
    tokens = sources[0].shape[2]
    rows = max(u.shape[0] for u in units if u.source is not None)
    scratch = room(4) + room(4) + room(2) + room() + line
    scratch += [pltpu.VMEM(a.shape, BF16) for a in (*sources, *targets)]
    scratch += [pltpu.VMEM((4 * rows, tokens), BF16)]
    scratch += [pltpu.VMEM((d, 4) + a, BF16) for a, d in ring_sizes(units).items()]
    scratch += [SEM((len(sources),)), SEM((len(targets),)), SEM((n, 5)), SEM((n, 5)), SEM((n,))]
    args = [*sources, *targets]
    specs = [anywhere] * len(args)
    out_shape = [jax.ShapeDtypeStruct(s, BF16) for s in out_shapes]
    out_specs = [anywhere] * len(out_shapes)
    if tail:
        big, small = tail[:6], tail[6:]
        args += [*big, *small]
        specs += [anywhere] * len(big) + [vmem] * len(small)
        width = big[4].shape[0]
        out_shape += [jax.ShapeDtypeStruct((tokens, width), F32), jax.ShapeDtypeStruct((2, width), F32)]
        out_specs += [anywhere, vmem]
        scratch += [pltpu.VMEM((big[0].shape[1] * BLOCK // tokens, tokens), BF16)]
        scratch += [pltpu.VMEM(a.shape, a.dtype) for a in big[1:]]
        scratch += [pltpu.VMEM((width, tokens), F32), pltpu.VMEM((tokens, width), F32)]
        scratch += [pltpu.VMEM((11, 2, width), F32), SEM((n, 4)), SEM((6,)), SEM((n, 4)), SEM((n, 4))]
        scratch += [SEM((5,)), SEM((5,))]
    return pl.pallas_call(
        functools.partial(sum_kernel, units, len(sources), len(targets), len(out_shapes), bool(tail)),
        in_specs=specs,
        out_specs=out_specs,
        out_shape=out_shape,
        scratch_shapes=scratch,
        compiler_params=pltpu.CompilerParams(
            collective_id=collective_id, has_side_effects=True, vmem_limit_bytes=60 * 1024 * 1024
        ),
        name="sum_with_keys" if tail else "sum_weights",
    )(*args)


def row_sum(part, size):
    if size != 4:
        return lax.psum(part, "narrow")
    add = lambda a, b: (a.astype(F32) + b.astype(F32)).astype(BF16)
    part = add(part, lax.ppermute(part, "narrow", [(0, 1), (3, 2)]))
    part = add(part, lax.ppermute(part, "narrow", [(1, 2), (2, 1)]))
    back = lax.ppermute(part, "narrow", [(1, 0), (2, 3)])
    at = lax.axis_index("narrow")
    return jnp.where((at == 1) | (at == 2), part, back)


def turn(v, cos, sin):
    heads = v.reshape(-1, 2, HDIM // 2, v.shape[1])
    one, two = heads[:, 0], heads[:, 1]
    return jnp.stack([one * cos - two * sin, two * cos + one * sin], axis=1).reshape(v.shape)


def turn_back(v, cos, sin):
    return turn(v, cos, -sin)


def shards(sizes, tokens, lengths, block_plan, attn_gain, w_query, w_key, w_value, w_out, ffn_gain,
           w_gate, w_up, w_down, cotangent):
    n = sizes["wide"]
    at = lax.axis_index("wide")
    micro, _, slots, width = tokens.shape
    total = micro * slots
    kd = w_key.shape[1]
    ff = w_gate.shape[1]
    nq = slots // BLOCK
    nb = nq * n

    plan = block_plan[:, 0]
    sizes_of = lengths[:, 0]
    docs = sizes_of.shape[1]
    upto = jnp.arange(docs)[:, None] >= jnp.arange(docs)[None, :]
    ends = jnp.sum(jnp.where(upto[None], sizes_of[:, None, :], 0), axis=2)
    own_plan = lax.dynamic_slice_in_dim(plan, at * nq, nq, axis=1)
    position = own_plan[:, :, None] * BLOCK + jnp.arange(BLOCK, dtype=jnp.int32)
    start = jnp.sum(
        jnp.where(position[..., None] >= ends[:, None, None, :], sizes_of[:, None, None, :], 0), axis=3
    )
    info = jnp.stack([start[:, :, 0] // BLOCK, own_plan], axis=1)
    slot_block = jnp.arange(nb, dtype=jnp.int32)
    where_is = jnp.sum(
        jnp.where(plan[:, None, :] == slot_block[None, :, None], slot_block[None, None, :], 0), axis=2
    )
    start = start.reshape(1, total)
    local = position.reshape(1, total) - start
    frequency = ROPE_BASE ** (-2.0 * jnp.arange(HDIM // 2, dtype=F32) / HDIM)
    angles = frequency[:, None] * local.astype(F32)
    cos, sin = jnp.cos(angles), jnp.sin(angles)

    cube = n == CUBE and sizes["narrow"] == 4 and nq % 2 == 0

    def shared(a):
        return a.reshape(n, -1, a.shape[1])

    def row_part(source, target):
        part = dot(source, target, 1, 1).astype(BF16)
        own = lax.psum_scatter(part, "wide", scatter_dimension=0, tiled=True)
        return row_sum(own, sizes["narrow"])

    x_t = tokens.reshape(total, width).T
    ct_t = cotangent.reshape(total, width).T
    x = x_t.astype(F32)

    weights = (w_query, w_key, w_value, w_out, w_gate, w_up, w_down)
    if cube:
        by_device = lambda a: a.reshape(n, width // n, a.shape[1])
        got, q_t, xn, kv, rr1 = start_of(
            weights, by_device(x_t), by_device(attn_gain[:, None]), cos, sin, micro, 2
        )
        xn = xn.reshape(width, total)
    else:
        got = [lax.all_gather(a, "wide", axis=0) for a in weights]
    g_query, g_key, g_value, g_out, g_gate, g_up, g_down = [a.reshape(-1, a.shape[2]) for a in got]
    if not cube:
        rr1 = lax.rsqrt(jnp.mean(x * x, axis=0, keepdims=True) + EPS)
        xn = (x * rr1 * attn_gain[:, None]).astype(BF16)
        key_t = turn(dot(g_key, xn, 0, 0), cos, sin).astype(BF16)
        value_t = dot(g_value, xn, 0, 0).astype(BF16)
        own_kv = jnp.concatenate([key_t, value_t]).reshape(2 * kd, micro, nq, BLOCK).transpose(1, 2, 0, 3)
        q_t = (turn(dot(g_query, xn, 0, 0), cos, sin).astype(BF16) * HDIM**-0.5).astype(BF16)
        kv = lax.all_gather(own_kv, "wide", axis=0)
    att_t, lse = attention_fwd(info, where_is, q_t, start, kv)

    res = x + dot(g_out, att_t, 0, 0)
    rr2 = lax.rsqrt(jnp.mean(res * res, axis=0, keepdims=True) + EPS)
    hn = (res * rr2 * ffn_gain[:, None]).astype(BF16)
    gate = dot(g_gate, hn, 0, 0)
    up = dot(g_up, hn, 0, 0)
    sg = 1.0 / (1.0 + jnp.exp(-gate))
    hidden = (gate * sg * up).astype(BF16)
    out = (res + dot(g_down, hidden, 0, 0)).astype(BF16).T

    d_hidden = dot(g_down, ct_t, 1, 0)
    d_gate = (d_hidden * up * sg * (1.0 + gate * (1.0 - sg))).astype(BF16)
    d_up = (d_hidden * gate * sg).astype(BF16)
    d_hn = dot(g_gate, d_gate, 1, 0) + dot(g_up, d_up, 1, 0)
    u = d_hn * ffn_gain[:, None]
    d_res = (
        ct_t.astype(F32) + rr2 * u - res * rr2**3 * jnp.mean(u * res, axis=0, keepdims=True)
    )
    gain_two = jnp.sum(d_hn * res * rr2, axis=1)
    d_attn = d_res.astype(BF16)
    do_t = dot(g_out, d_attn, 1, 0).astype(BF16)

    pairs = [(hidden, ct_t), (hn, d_gate), (hn, d_up), (att_t, d_attn)]
    most = 80 * 1024
    high = width // n
    if cube:
        s_down, s_gate = sums(
            weight_units([(0, 0, 0, ff // n, width), (1, 1, 1, high, ff)], most),
            [shared(hidden), shared(hn)],
            [ct_t, d_gate],
            [(ff // n, width), (high, ff)],
            3,
        )
    else:
        s_down, s_gate, s_up, s_out = [row_part(*p) for p in pairs]

    dq, dkv = attention_bwd(info, where_is, q_t, do_t, att_t, lse, start, cos, sin, kv)
    if cube:
        blocks = micro * nq
        keys = dkv.reshape(n, blocks * 2 * kd, BLOCK)
        units = [
            Unit(None, None, None, (2 * kd * i, 2 * kd), (0, BLOCK), (ALONG_X, ALONG_Y)[i % 2])
            for i in range(blocks)
        ] + weight_units(
            [(1, 1, 2, high, ff), (2, 2, 3, high, width), (0, 0, 0, high, width), (0, None, 1, high, 2 * kd)],
            most,
        )
        s_query, s_kv, s_up, s_out, grad_x, gains = sums(
            units,
            [shared(xn), shared(hn), shared(att_t)],
            [dq, d_up, d_attn],
            [(high, width), (high, 2 * kd), (high, ff), (high, width)],
            4,
            (keys, g_query, g_key, g_value, x_t, d_res, cos, sin, rr1, attn_gain[:, None], gain_two[None]),
        )
        s_key, s_value = s_kv[:, :kd], s_kv[:, kd:]
    else:
        dkv = lax.psum_scatter(dkv, "wide", scatter_dimension=0).transpose(2, 0, 1, 3).reshape(2 * kd, total)
        dk = turn_back(dkv[:kd].astype(F32), cos, sin).astype(BF16)
        dv = dkv[kd:]
        d_xn = dot(g_query, dq, 1, 0) + dot(g_key, dk, 1, 0) + dot(g_value, dv, 1, 0)
        u = d_xn * attn_gain[:, None]
        grad_x = (d_res + rr1 * u - x * rr1**3 * jnp.mean(u * x, axis=0, keepdims=True)).T
        gain_one = jnp.sum(d_xn * x * rr1, axis=1)
        s_query, s_key, s_value = row_part(xn, dq), row_part(xn, dk), row_part(xn, dv)
        gains = lax.psum(jnp.stack([gain_one, gain_two]), ("wide", "narrow"))

    shape = (micro, 1, slots, width)
    wide_out = lambda a: a.astype(F32)
    return (
        out.reshape(shape),
        grad_x.reshape(shape),
        gains[0],
        wide_out(s_query),
        wide_out(s_key),
        wide_out(s_value),
        wide_out(s_out),
        gains[1],
        wide_out(s_gate),
        wide_out(s_up),
        wide_out(s_down),
    )


def solution(mesh):
    by_slot = P(None, "narrow", "wide", None)
    by_row = P(None, "narrow", None)
    split = P("wide", None)
    in_specs = (
        by_slot, by_row, by_row, P(), split, split, split, split, P(), split, split, split, by_slot,
    )
    out_specs = (
        by_slot, by_slot, P(), split, split, split, split, P(), split, split, split,
    )
    return jax.shard_map(
        functools.partial(shards, dict(mesh.shape)),
        mesh=mesh,
        in_specs=in_specs,
        out_specs=out_specs,
        check_vma=False,
    )
```

```python
import functools

import jax
import jax.numpy as jnp
from jax import lax
from jax.experimental import pallas as pl
from jax.experimental.pallas import tpu as pltpu
from jax.sharding import PartitionSpec as P

HDIM = 64
BLOCK = 128
EPS = 1e-05
ROPE_BASE = 100000.0
NEG_FILL = -1e30
F32 = jnp.float32
BF16 = jnp.bfloat16
VMEM_LIMIT = 56 * 1024 * 1024


def dot(a, b, ca, cb):
    return lax.dot_general(a, b, (((ca,), (cb,)), ((), ())), preferred_element_type=F32)


def live_mask(qpos, start, p):
    kpos = p * BLOCK + lax.broadcasted_iota(jnp.int32, (BLOCK, BLOCK), 0)
    return (kpos <= qpos) & (kpos >= start)


STEP = 2


def pick(kv_ref, kvat, mb, qpos, start, b, t, share):
    nq = kv_ref.shape[2]
    blocks = [b - STEP * t - i for i in range(STEP)]
    slots = [kvat[mb, jnp.maximum(p, 0)] for p in blocks]
    at = [(lax.div(s, nq), lax.rem(s, nq)) for s in slots]
    ok = jnp.concatenate([live_mask(qpos, start, p) for p in blocks], axis=0)

    def keys(g):
        rows = slice(g * HDIM, (g + 1) * HDIM)
        return jnp.concatenate([kv_ref[d, 0, s, rows, :] for d, s in at], axis=1)

    return keys, at, jnp.concatenate([ok] * share, axis=1)


def fwd_kernel(groups, share, info, kvat, q_ref, start_ref, kv_ref, o_ref, lse_ref, qs, m_s, l_s, acc, s_s, w_s):
    mb, i = pl.program_id(0), pl.program_id(1)
    lo, b = info[mb, 0, i], info[mb, 1, i]
    nq = kv_ref.shape[2]
    lanes = share * BLOCK
    for g in range(groups):
        for h in range(share):
            at = (g * share + h) * HDIM
            qs[g, :, h * BLOCK : (h + 1) * BLOCK] = q_ref[at : at + HDIM, :]
    m_s[...] = jnp.full_like(m_s, NEG_FILL)
    l_s[...] = jnp.zeros_like(l_s)
    acc[...] = jnp.zeros_like(acc)
    qpos = b * BLOCK + lax.broadcasted_iota(jnp.int32, (1, BLOCK), 1)
    start = start_ref[...]

    def step(t, carry):
        keys, at, ok = pick(kv_ref, kvat, mb, qpos, start, b, t, share)
        for g in range(groups):
            s_s[g] = jnp.where(ok, dot(keys(g), qs[g], 0, 0), NEG_FILL)
        alphas = []
        for g in range(groups):
            s = s_s[g]
            m_old = m_s[g]
            m_new = jnp.maximum(m_old, jnp.max(s, axis=0, keepdims=True))
            w = jnp.exp(s - m_new)
            alpha = jnp.exp(m_old - m_new)
            l_s[g] = l_s[g] * alpha + jnp.sum(w, axis=0, keepdims=True)
            m_s[g] = m_new
            w_s[g] = w.astype(BF16)
            alphas.append(alpha)
        for g in range(groups):
            acc[g] = acc[g] * alphas[g] + dot(keys(groups + g), w_s[g], 1, 0)
        return carry

    lax.fori_loop(0, (b - lo + STEP) // STEP, step, 0)
    for g in range(groups):
        total = l_s[g]
        out = (acc[g] / total).astype(BF16)
        for h in range(share):
            at = (g * share + h) * HDIM
            o_ref[at : at + HDIM, :] = out[:, h * BLOCK : (h + 1) * BLOCK]
        lse_ref[0, g : g + 1, :] = m_s[g] + jnp.log(total)


def attention_fwd(info, kvat, q_t, start, kv):
    width = q_t.shape[0]
    n, micro, nq, kvw, _ = kv.shape
    groups = kvw // HDIM // 2
    share = width // HDIM // groups
    lanes = share * BLOCK
    tok = lambda rows: pl.BlockSpec((rows, BLOCK), lambda m, i, *_: (0, m * nq + i))
    return pl.pallas_call(
        functools.partial(fwd_kernel, groups, share),
        grid_spec=pltpu.PrefetchScalarGridSpec(
            num_scalar_prefetch=2,
            grid=(micro, nq),
            in_specs=[
                tok(width),
                tok(1),
                pl.BlockSpec((n, 1, nq, kvw, BLOCK), lambda m, i, *_: (0, m, 0, 0, 0)),
            ],
            out_specs=[
                tok(width),
                pl.BlockSpec((1, groups, lanes), lambda m, i, *_: (m * nq + i, 0, 0)),
            ],
            scratch_shapes=[
                pltpu.VMEM((groups, HDIM, lanes), BF16),
                pltpu.VMEM((groups, 1, lanes), F32),
                pltpu.VMEM((groups, 1, lanes), F32),
                pltpu.VMEM((groups, HDIM, lanes), F32),
                pltpu.VMEM((groups, STEP * BLOCK, lanes), F32),
                pltpu.VMEM((groups, STEP * BLOCK, lanes), BF16),
            ],
        ),
        out_shape=[
            jax.ShapeDtypeStruct(q_t.shape, BF16),
            jax.ShapeDtypeStruct((micro * nq, groups, lanes), F32),
        ],
        compiler_params=pltpu.CompilerParams(vmem_limit_bytes=VMEM_LIMIT),
        cost_estimate=pl.CostEstimate(
            flops=int(1e10), bytes_accessed=int(8e6), transcendentals=int(8e6)
        ),
        name="attention_fwd",
    )(info, kvat, q_t, start, kv)


def bwd_kernel(
    groups, share, info, kvat, q_ref, do_ref, o_ref, lse_ref, start_ref, cos_ref, sin_ref, kv_ref,
    dq_ref, dkv_ref, qs, dos, delta, dq, dkv, s_s, d_s, w_s, ds_s,
):
    mb, i = pl.program_id(0), pl.program_id(1)
    lo, b = info[mb, 0, i], info[mb, 1, i]
    nq = kv_ref.shape[2]

    @pl.when(i == 0)
    def _():
        dkv[...] = jnp.zeros_like(dkv)

    for g in range(groups):
        for h in range(share):
            at = (g * share + h) * HDIM
            cols = slice(h * BLOCK, (h + 1) * BLOCK)
            d_out = do_ref[at : at + HDIM, :]
            qs[g, :, cols] = q_ref[at : at + HDIM, :]
            dos[g, :, cols] = d_out
            delta[g, :, cols] = jnp.sum(
                d_out.astype(F32) * o_ref[at : at + HDIM, :].astype(F32), axis=0, keepdims=True
            )
    dq[...] = jnp.zeros_like(dq)
    qpos = b * BLOCK + lax.broadcasted_iota(jnp.int32, (1, BLOCK), 1)
    start = start_ref[...]

    def step(t, carry):
        keys, at, ok = pick(kv_ref, kvat, mb, qpos, start, b, t, share)
        for g in range(groups):
            s_s[g] = jnp.where(ok, dot(keys(g), qs[g], 0, 0), NEG_FILL)
            d_s[g] = dot(keys(groups + g), dos[g], 0, 0)
        for g in range(groups):
            w = jnp.exp(s_s[g] - lse_ref[0, g : g + 1, :])
            w_s[g] = w.astype(BF16)
            ds_s[g] = (w * (d_s[g] - delta[g])).astype(BF16)
        for g in range(groups):
            dq[g] += dot(keys(g), ds_s[g], 1, 0)
            dk = dot(qs[g], ds_s[g], 1, 1)
            dv = dot(dos[g], w_s[g], 1, 1)
            krows = slice(g * HDIM, (g + 1) * HDIM)
            vrows = slice((groups + g) * HDIM, (groups + g + 1) * HDIM)
            for i in range(STEP):
                cols = slice(i * BLOCK, (i + 1) * BLOCK)
                dkv[at[i][0], at[i][1], krows, :] += dk[:, cols]
                dkv[at[i][0], at[i][1], vrows, :] += dv[:, cols]
        return carry

    lax.fori_loop(0, (b - lo + STEP) // STEP, step, 0)
    cos, sin = cos_ref[...], sin_ref[...]
    half = HDIM // 2
    for g in range(groups):
        for h in range(share):
            at = (g * share + h) * HDIM
            one = dq[g, :half, h * BLOCK : (h + 1) * BLOCK] * HDIM**-0.5
            two = dq[g, half:, h * BLOCK : (h + 1) * BLOCK] * HDIM**-0.5
            dq_ref[at : at + half, :] = (one * cos + two * sin).astype(BF16)
            dq_ref[at + half : at + HDIM, :] = (two * cos - one * sin).astype(BF16)

    @pl.when(i == nq - 1)
    def _():
        dkv_ref[:, 0] = dkv[...].astype(BF16)


def attention_bwd(info, kvat, q_t, do_t, o_t, lse, start, cos_t, sin_t, kv):
    width = q_t.shape[0]
    n, micro, nq, kvw, _ = kv.shape
    groups = kvw // HDIM // 2
    share = width // HDIM // groups
    lanes = share * BLOCK
    tok = lambda rows: pl.BlockSpec((rows, BLOCK), lambda m, i, *_: (0, m * nq + i))
    keys = pl.BlockSpec((n, 1, nq, kvw, BLOCK), lambda m, i, *_: (0, m, 0, 0, 0))
    return pl.pallas_call(
        functools.partial(bwd_kernel, groups, share),
        grid_spec=pltpu.PrefetchScalarGridSpec(
            num_scalar_prefetch=2,
            grid=(micro, nq),
            in_specs=[
                tok(width),
                tok(width),
                tok(width),
                pl.BlockSpec((1, groups, lanes), lambda m, i, *_: (m * nq + i, 0, 0)),
                tok(1),
                tok(HDIM // 2),
                tok(HDIM // 2),
                keys,
            ],
            out_specs=[tok(width), keys],
            scratch_shapes=[
                pltpu.VMEM((groups, HDIM, lanes), BF16),
                pltpu.VMEM((groups, HDIM, lanes), BF16),
                pltpu.VMEM((groups, 1, lanes), F32),
                pltpu.VMEM((groups, HDIM, lanes), F32),
                pltpu.VMEM((n, nq, kvw, BLOCK), F32),
                pltpu.VMEM((groups, STEP * BLOCK, lanes), F32),
                pltpu.VMEM((groups, STEP * BLOCK, lanes), F32),
                pltpu.VMEM((groups, STEP * BLOCK, lanes), BF16),
                pltpu.VMEM((groups, STEP * BLOCK, lanes), BF16),
            ],
        ),
        out_shape=[
            jax.ShapeDtypeStruct(q_t.shape, BF16),
            jax.ShapeDtypeStruct(kv.shape, BF16),
        ],
        compiler_params=pltpu.CompilerParams(vmem_limit_bytes=VMEM_LIMIT),
        cost_estimate=pl.CostEstimate(
            flops=int(2e10), bytes_accessed=int(16e6), transcendentals=int(8e6)
        ),
        name="attention_bwd",
    )(info, kvat, q_t, do_t, o_t, lse, start, cos_t, sin_t, kv)


CORE, ALONG_X, ALONG_Y = 1, 2, 4
FAR = ALONG_X + ALONG_Y
CUBE = 8
LAG = 2
LAGS = 2
SEM = pltpu.SemaphoreType.DMA


def meet(peers):
    barrier = pltpu.get_barrier_semaphore()
    for peer in peers:
        pl.semaphore_signal(barrier, inc=1, device_id=peer, device_id_type=pl.DeviceIdType.MESH)
    pl.semaphore_wait(barrier, len(peers))


def weight_chunks(shapes, most=160 * 1024):
    chunks = []
    for a, (rows, cols) in enumerate(shapes):
        n = 1
        while rows * cols // n > most and rows % (32 * n) == 0:
            n *= 2
        k = 1
        while rows // n * cols // k > most and cols % (256 * k) == 0:
            k *= 2
        for i in range(n):
            lo, hi = rows // n * i, rows // n * (i + 1)
            mid = lo + -(-(hi - lo) // 32) * 16
            for j in range(k):
                c = pl.ds(cols // k * j, cols // k)
                chunks.append((a, (pl.ds(lo, mid - lo), c), (pl.ds(mid, hi - mid), c)))
    return chunks


def pieces_of(total, size):
    return [(lo, min(size, total - lo)) for lo in range(0, total, size)]


def start_kernel(chunks, micro, *refs):
    refs = list(refs)
    take_refs = lambda n: [refs.pop(0) for _ in range(n)]
    ins = take_refs(7)
    far_x, gain_ref, cos_ref, sin_ref = take_refs(4)
    outs = take_refs(7)
    far_q, far_xn, far_kv, rr_ref = take_refs(4)
    near_w = take_refs(3)
    x, xn, q_s, own_kv, sent, came, local = take_refs(7)
    at, row = lax.axis_index("wide"), lax.axis_index("narrow")
    peer = {bit: (at ^ bit, row) for bit in (CORE, ALONG_X, ALONG_Y)}
    peer["row"] = (at, row ^ 1)
    keys = len(ins)
    source = [*ins, own_kv]
    land = [*near_w, *outs[3:], far_kv]
    n = len(chunks)
    kd = own_kv.shape[2] // 2
    nq = own_kv.shape[1]
    width, half = q_s.shape[0], HDIM // 2

    mine_in = [pltpu.make_async_copy(ins[i], near_w[i].at[at], local.at[i]) for i in range(3)]
    mine_in.append(pltpu.make_async_copy(far_x, x, local.at[3]))
    give = [pltpu.make_async_copy(near_w[i], outs[i], local.at[4 + i]) for i in range(3)]
    give_q = pltpu.make_async_copy(q_s, far_q, local.at[7])
    give_xn = pltpu.make_async_copy(xn, far_xn, local.at[8])
    give_kv = pltpu.make_async_copy(own_kv, far_kv.at[at], local.at[9])

    def norm():
        mine_in[3].wait()
        count = x.shape[0]
        square = jnp.zeros(rr_ref.shape, F32)
        for j in range(count):
            v = x[j].astype(F32)
            square += jnp.sum(v * v, axis=0, keepdims=True)
        rr = lax.rsqrt(square / width + EPS)
        rr_ref[...] = rr
        for j in range(count):
            xn[j] = (x[j].astype(F32) * rr * gain_ref[j]).astype(BF16)
        give_xn.start()

    def turned(w, lo, size):
        got = sum(dot(w[j, :, lo : lo + size], xn[j], 0, 0) for j in range(w.shape[0]))
        return got

    def heads(got):
        cos, sin = cos_ref[...], sin_ref[...]
        for h in range(0, got.shape[0], HDIM):
            one, two = got[h : h + half], got[h + half : h + HDIM]
            yield h, one * cos - two * sin
            yield h + half, two * cos + one * sin

    def to_keys(at_row, value):
        value = value.astype(BF16)
        for m in range(micro):
            for i in range(nq):
                lanes = slice((m * nq + i) * BLOCK, (m * nq + i + 1) * BLOCK)
                own_kv[m, i, at_row : at_row + value.shape[0], :] = value[:, lanes]

    def key_tile(lo, size):
        for h, v in heads(turned(near_w[1], lo, size)):
            to_keys(lo + h, v)

    def value_tile(lo, size):
        to_keys(kd + lo, turned(near_w[2], lo, size))

    def query_tile(lo, size):
        for h, v in heads(turned(near_w[0], lo, size)):
            q_s[lo + h : lo + h + half, :] = v.astype(BF16) * HDIM**-0.5

    def run(mine):
        other = 1 - mine
        used = [0] * n
        begun = []

        def part(ref, c, which):
            return ref.at[chunks[c][1 + which]]

        def copy(c, m, which, way, slot):
            a = chunks[c][0]
            there = part(land[a].at[at ^ m], c, which)
            return pltpu.make_async_remote_copy(
                src_ref=there if m else part(source[a], c, which),
                dst_ref=there,
                send_sem=sent.at[c, slot],
                recv_sem=came.at[c, m if way == "row" else m ^ way, which],
                device_id=peer[way],
                device_id_type=pl.DeviceIdType.MESH,
            )

        def push(c, m, which, way):
            r = copy(c, m, which, way, used[c])
            used[c] += 1
            r.start()
            begun.append(r)

        def take(c, m, which, *ways):
            copy(c, m ^ CORE, which, CORE, 0).wait_recv()
            for way in ways:
                push(c, m, which, way)

        planes = [c[0] != keys for c in chunks]
        bounced = [2 < c[0] < keys for c in chunks]

        def first(c):
            push(c, 0, mine, ALONG_X)
            push(c, 0, mine, ALONG_Y)
            if not planes[c]:
                push(c, 0, other, ALONG_X)
                push(c, 0, other, ALONG_Y)

        def second(c):
            if planes[c]:
                take(c, ALONG_Y, mine, ALONG_X, CORE)
                push(c, 0, other, ALONG_Y)
                take(c, ALONG_X, mine, "row", CORE)
            else:
                take(c, ALONG_X, mine, ALONG_Y, CORE)
                take(c, ALONG_Y, other, ALONG_X, CORE)
                take(c, ALONG_Y, mine, CORE)
                take(c, ALONG_X, other, CORE)
            push(c, 0, 0, CORE)
            push(c, 0, 1, CORE)

        def third(c):
            take(c, FAR, mine, *(("row", CORE) if planes[c] else (CORE,)))
            if planes[c]:
                take(c, ALONG_Y, other, CORE)
                take(c, ALONG_X, other, CORE)
            else:
                take(c, FAR, other, CORE)

        def fourth(c):
            if planes[c]:
                take(c, FAR, other, CORE)

        def fifth(c):
            for which in range(2):
                take(c, CORE, which, *((CORE,) if bounced[c] else ()))
            for m in (ALONG_X, ALONG_Y, FAR):
                for which in range(2):
                    take(c, m + CORE, which)

        def sixth(c):
            if bounced[c]:
                for which in range(2):
                    take(c, 0, which)

        steps = (first, second, third, fourth, fifth, sixth)
        begins, ready = [], 0
        for c in range(n):
            begins.append(c)
            if chunks[c][0] < 3:
                ready = c + LAG * 4
            if chunks[c][0] == keys:
                begins[c] = max(begins[c - 1] + 1, ready + 1)
        work = {1: [norm], ready: []}
        for lo, size in pieces_of(kd, 256):
            work[ready] += [functools.partial(key_tile, lo, size), functools.partial(value_tile, lo, size)]
        work[ready].append(give_kv.start)
        for i, (lo, size) in enumerate(pieces_of(width, 256)):
            work[ready + 2 + i] = [functools.partial(query_tile, lo, size)]
        for t in range(begins[-1] + LAG * (len(steps) - 1) + 1):
            for s, step in enumerate(steps):
                for c in range(n):
                    if begins[c] + LAG * s == t:
                        step(c)
            if t == ready:
                for r in mine_in[:3]:
                    r.wait()
                for r in give:
                    r.start()
            for job in work.get(t, ()):
                job()
        for r in begun:
            r.wait_send()

    for r in mine_in:
        r.start()
    meet(list(peer.values()))
    for mine in range(2):
        pl.when(row % 2 == mine)(functools.partial(run, mine))
    give_q.start()
    for r in (*give, give_q, give_xn, give_kv):
        r.wait()


def start_of(weights, x, gain, cos, sin, micro, collective_id):
    count, high, tokens = x.shape
    kd = weights[1].shape[1]
    nq = tokens // micro // BLOCK
    chunks = weight_chunks([a.shape for a in weights])
    keys = len(weights)
    for m in range(micro):
        for i in range(2):
            rows = pl.ds(kd * i, kd)
            halves = [(m, pl.ds(nq // 2 * h, nq // 2), rows) for h in range(2)]
            chunks.append((keys, *halves))
    anywhere = pl.BlockSpec(memory_space=pl.ANY)
    vmem = pl.BlockSpec(memory_space=pltpu.VMEM)
    shape = jax.ShapeDtypeStruct
    kv = (micro, nq, 2 * kd, BLOCK)
    got = pl.pallas_call(
        functools.partial(start_kernel, chunks, micro),
        in_specs=[anywhere] * (keys + 1) + [vmem] * 3,
        out_specs=[anywhere] * (keys + 3) + [vmem],
        out_shape=[shape((count,) + a.shape, BF16) for a in weights]
        + [shape((count * high, tokens), BF16), shape(x.shape, BF16), shape((count,) + kv, BF16)]
        + [shape((1, tokens), F32)],
        scratch_shapes=[pltpu.VMEM((count,) + a.shape, BF16) for a in weights[:3]]
        + [
            pltpu.VMEM(x.shape, BF16),
            pltpu.VMEM(x.shape, BF16),
            pltpu.VMEM((count * high, tokens), BF16),
            pltpu.VMEM(kv, BF16),
            SEM((len(chunks), 16)),
            SEM((len(chunks), 8, 2)),
            SEM((10,)),
        ],
        compiler_params=pltpu.CompilerParams(
            collective_id=collective_id, has_side_effects=True, vmem_limit_bytes=VMEM_LIMIT
        ),
        name="gather_and_project",
    )(*weights, x, gain, cos, sin)
    return got[:keys], got[keys], got[keys + 1], got[keys + 2], got[keys + 3]


class Unit:
    def __init__(self, source, target, out, rows, cols, first):
        self.source, self.target, self.out = source, target, out
        self.rows, self.cols, self.first = rows, cols, first

    @property
    def shape(self):
        return (self.rows[1], self.cols[1])


def weight_units(sizes, most, units=()):
    units = list(units)
    for source, target, out, rows, cols in sizes:
        k = 1
        while cols % (256 * k) == 0 and rows * cols // k > most:
            k *= 2
        high = -(-rows // max(1, round(rows * cols / k / most)) // 16) * 16
        cols_cuts = pieces_of(cols, cols // k)
        if out == sizes[-1][2] and cols % BLOCK == 0:
            lo, size = cols_cuts.pop()
            while size > BLOCK:
                part = -(-size // (2 * BLOCK)) * BLOCK
                cols_cuts.append((lo, part))
                lo, size = lo + part, size - part
            cols_cuts.append((lo, size))
        for rows_cut in pieces_of(rows, high):
            for cols_cut in cols_cuts:
                first = (ALONG_X, ALONG_Y)[len(units) % 2]
                units.append(Unit(source, target, out, rows_cut, cols_cut, first))
    return units


RING = 3


def ring_sizes(units):
    shapes = [u.shape for u in units if u.source is not None]
    return {a: min(RING, shapes.count(a)) for a in shapes}


def sum_scratch(units, tokens):
    n = len(units)
    room = lambda *lead: [pltpu.VMEM(lead + u.shape, BF16) for u in units]
    line = [pltpu.VMEM((2,) + u.shape if u.source is not None else (8, BLOCK), BF16) for u in units]
    rows = max(u.shape[0] for u in units if u.source is not None)
    scratch = room(4) + room(4) + room(2) + room() + line
    scratch += [pltpu.VMEM((4 * rows, tokens), BF16)]
    scratch += [pltpu.VMEM((d, 4) + a, BF16) for a, d in ring_sizes(units).items()]
    return scratch + [SEM((n, 5)), SEM((n, 5)), SEM((n,)), SEM((n, 4)), SEM((n, 4)), SEM((n, 4))]


class Sums:
    def __init__(self, units, take, outs, source, product, far_keys=None, keys_done=None):
        n = len(units)
        self.units, self.outs, self.source, self.product = units, outs, source, product
        self.far_keys, self.keys_done = far_keys, keys_done
        self.held, self.core_in, self.one_in, self.two_in, self.line_in = (take(n) for _ in range(5))
        self.lhs = take(1)[0]
        self.depth = ring_sizes(units)
        self.rings = dict(zip(self.depth, take(len(self.depth))))
        self.sent, self.came, self.stored, self.key_load, self.key_sent, self.key_came = take(6)
        self.at, self.row = lax.axis_index("wide"), lax.axis_index("narrow")
        self.way = {bit: (self.at ^ bit, self.row) for bit in (CORE, ALONG_X, ALONG_Y)}
        self.near, self.across = (self.at, self.row ^ 1), (self.at, self.row ^ 3)
        self.middle = (self.row == 1) | (self.row == 2)
        self.is_keys = [u.source is None for u in units]
        self.steps = (self.s0, self.s1, self.s2, self.s3, self.s4, self.s5, self.s6)

    def meet(self):
        meet([*self.way.values(), self.near, self.across])

    def send(self, c, slot, a, b, to):
        return pltpu.make_async_remote_copy(
            src_ref=a, dst_ref=b, send_sem=self.sent.at[c, slot], recv_sem=self.came.at[c, slot],
            device_id=to, device_id_type=pl.DeviceIdType.MESH,
        )

    @staticmethod
    def add(dst, other):
        rows = dst.shape[-2]
        most = rows // 16
        step = 16 * max(k for k in (1, 2, 3, 4) if most % k == 0)

        def body(i, carry):
            cut = pl.ds(pl.multiple_of(i * step, 16), step)
            dst[cut, :] = dst[cut, :] + other[cut, :]
            return carry

        lax.fori_loop(0, most * 16 // step, body, 0)
        if rows % 16:
            cut = slice(most * 16, rows)
            dst[cut, :] = dst[cut, :] + other[cut, :]

    def order(self, c):
        first = self.units[c].first
        return (0, FAR - first, first, FAR)

    def slot_of(self, c):
        shape = self.units[c].shape
        alike = [i for i, u in enumerate(self.units) if u.source is not None and u.shape == shape]
        return alike.index(c) % self.depth[shape]

    def same_slot(self, i, c):
        if self.is_keys[i] or self.is_keys[c] or self.units[i].shape != self.units[c].shape:
            return False
        return self.slot_of(i) == self.slot_of(c)

    def core_copies(self, c):
        u = self.units[c]
        if not self.is_keys[c]:
            return [self.send(c, 0, self.rings[u.shape].at[self.slot_of(c)], self.core_in[c], self.way[CORE])]
        return [
            pltpu.make_async_remote_copy(
                src_ref=self.far_keys.at[self.at ^ CORE ^ m, pl.ds(*u.rows)], dst_ref=self.core_in[c].at[i],
                send_sem=self.key_sent.at[c, i], recv_sem=self.key_came.at[c, i],
                device_id=self.way[CORE], device_id_type=pl.DeviceIdType.MESH,
            )
            for i, m in enumerate(self.order(c))
        ]

    def key_loads(self, c):
        rows = pl.ds(*self.units[c].rows)
        return [
            pltpu.make_async_copy(self.far_keys.at[self.at ^ m, rows], self.held[c].at[i], self.key_load.at[c, i])
            for i, m in enumerate(self.order(c))
        ]

    def first_copy(self, c):
        return self.send(c, 1, self.held[c].at[pl.ds(2, 2)], self.one_in[c], self.way[self.units[c].first])

    def second_copy(self, c):
        return self.send(c, 2, self.held[c].at[1], self.two_in[c], self.way[FAR - self.units[c].first])

    def inward(self, c):
        return self.send(c, 3, self.held[c].at[0], self.line_in[c].at[0], self.near)

    def over(self, c):
        return self.send(c, 4, self.held[c].at[0], self.line_in[c].at[1], self.across)

    def outward(self, c):
        return self.send(c, 3, self.line_in[c].at[1], self.line_in[c].at[0], self.near)

    def store(self, c, slot):
        u = self.units[c]
        cut = (pl.ds(*u.rows), pl.ds(*u.cols))
        return pltpu.make_async_copy(self.line_in[c].at[slot], self.outs[u.out].at[cut], self.stored.at[c])

    def products(self, c, mine):
        u = self.units[c]
        rows, cols = u.shape
        for i, m in enumerate(self.order(c)):
            self.lhs[pl.ds(i * rows, rows), :] = self.source(u, self.at ^ m ^ mine)
        a = self.lhs[pl.ds(0, 4 * rows), :]
        for lo, size in pieces_of(cols, 256):
            got = self.product(u, a, u.cols[0] + lo, size).astype(BF16).reshape(4, rows, size)
            if mine:
                self.rings[u.shape][self.slot_of(c), :, :, lo : lo + size] = got
            else:
                self.held[c][:, :, lo : lo + size] = got

    def s0(self, c):
        if self.is_keys[c]:
            for r in self.core_copies(c) + self.key_loads(c):
                r.start()
            return
        before = [i for i in range(c) if self.same_slot(i, c)]
        if before:
            self.core_copies(before[-1])[0].wait_send()
        self.products(c, CORE)
        self.core_copies(c)[0].start()
        self.products(c, 0)

    def s1(self, c):
        if self.is_keys[c]:
            for r in self.key_loads(c):
                r.wait()
        for r in self.core_copies(c):
            r.wait_recv()
        for i in (2, 3, 0, 1):
            self.add(self.held[c].at[i], self.core_in[c].at[i])
            if i == 3:
                self.first_copy(c).start()

    def s2(self, c):
        self.first_copy(c).wait_recv()
        self.add(self.held[c].at[1], self.one_in[c].at[1])
        self.second_copy(c).start()
        self.add(self.held[c].at[0], self.one_in[c].at[0])

    def s3(self, c):
        self.second_copy(c).wait_recv()
        self.add(self.held[c].at[0], self.two_in[c])
        if self.is_keys[c]:
            self.keys_done(c, self.held[c].at[0])
        else:
            pl.when(~self.middle)(lambda: self.inward(c).start())

    def s4(self, c):
        @pl.when(self.middle)
        def _():
            self.inward(c).wait_recv()
            self.add(self.held[c].at[0], self.line_in[c].at[0])
            self.over(c).start()

    def s5(self, c):
        @pl.when(self.middle)
        def _():
            self.over(c).wait_recv()
            self.add(self.line_in[c].at[1], self.held[c].at[0])
            self.outward(c).start()
            self.store(c, 1).start()

    def s6(self, c):
        @pl.when(~self.middle)
        def _():
            self.outward(c).wait_recv()
            self.store(c, 0).start()

    def finish(self):
        n = len(self.units)
        for c in range(n):
            if not any(self.same_slot(c, i) for i in range(c + 1, n)):
                for r in self.core_copies(c):
                    r.wait_send()
            self.first_copy(c).wait_send()
            self.second_copy(c).wait_send()
            if not self.is_keys[c]:
                self.inward(c).wait_send()
                pl.when(self.middle)(lambda: self.over(c).wait_send())
                self.store(c, 0).wait()

    def run(self, begins, work):
        last = max(b + LAGS * (len(self.steps) - 1) for b in begins)
        for t in range(max([last, *work]) + 1):
            for s, step in enumerate(self.steps):
                for c, b in enumerate(begins):
                    if b + LAGS * s == t and not (self.is_keys[c] and s > 3):
                        step(c)
            for job in work.get(t, ()):
                job()


TILE = 256


def ffn_kernel(units, *refs):
    refs = list(refs)
    take = lambda n: [refs.pop(0) for _ in range(n)]
    far_att, far_x, far_ct, far_out_w, far_gate_w, far_up_w, far_down_w, gain_ref = take(8)
    far_out, far_res, far_do, far_hn, far_d_up, far_d_attn, gain_sum = take(7)
    outs = take(2)
    att, x, ct, out_w, wg, wu, wd, res, hn, hn_t, hid_t, d_gate, d_up, out_acc, hn_acc = take(15)
    load, give = take(2)
    do, d_attn = att, hn
    width, tokens = att.shape
    ff = hid_t.shape[0]
    tiles = ff // TILE
    slots = range(0, tokens, BLOCK)
    loads = [
        pltpu.make_async_copy(a, b, load.at[i])
        for i, (a, b) in enumerate(
            zip(
                (far_att, far_out_w, far_x, far_gate_w, far_up_w, far_down_w, far_ct),
                (att, out_w, x, wg, wu, wd, ct),
            )
        )
    ]
    gives = [
        pltpu.make_async_copy(a, b, give.at[i])
        for i, (a, b) in enumerate(
            ((x, far_out), (res, far_res), (do, far_do), (hn_t, far_hn), (d_up, far_d_up), (d_attn, far_d_attn))
        )
    ]

    def attend():
        for r in loads[:3]:
            r.wait()
        for lo in slots:
            cut = slice(lo, lo + BLOCK)
            r = x[cut, :].astype(F32) + dot(att[:, cut], out_w[...], 0, 0)
            res[cut, :] = r
            rr = lax.rsqrt(jnp.mean(r * r, axis=1, keepdims=True) + EPS)
            h = r * rr * gain_ref[...]
            hn[cut, :] = h.astype(BF16)
            h = h.T
            high = hn_t.shape[1]
            for j in range(hn_t.shape[0]):
                hn_t[j, :, cut] = h[j * high : (j + 1) * high].astype(BF16)
        gives[3].start()

    def hidden_tile(i):
        cut = slice(i * TILE, (i + 1) * TILE)
        gate, up = dot(hn[...], wg[:, cut], 1, 0), dot(hn[...], wu[:, cut], 1, 0)
        hidden = (gate / (1.0 + jnp.exp(-gate)) * up).astype(BF16)
        hid_t[cut, :] = hidden.T

    def back_tile(i):
        cut = slice(i * TILE, (i + 1) * TILE)
        gate, up = dot(hn[...], wg[:, cut], 1, 0), dot(hn[...], wu[:, cut], 1, 0)
        sg = 1.0 / (1.0 + jnp.exp(-gate))
        act = gate * sg
        hidden = (act * up).astype(BF16)
        d_hidden = dot(ct[...], wd[cut, :], 1, 1)
        d_gate[:, cut] = (d_hidden * up * sg * (1.0 + gate * (1.0 - sg))).astype(BF16)
        d_up[:, cut] = (d_hidden * act).astype(BF16)
        forward = dot(hidden, wd[cut, :], 1, 0)
        back = dot(d_gate[:, cut], wg[:, cut], 1, 1) + dot(d_up[:, cut], wu[:, cut], 1, 1)
        if i == 0:
            out_acc[...] = forward
            hn_acc[...] = back
        else:
            out_acc[...] += forward
            hn_acc[...] += back

    def residual():
        gives[4].start()
        total = jnp.zeros(gain_sum.shape, F32)
        for lo in slots:
            cut = slice(lo, lo + BLOCK)
            r, d = res[cut, :], hn_acc[cut, :]
            rr = lax.rsqrt(jnp.mean(r * r, axis=1, keepdims=True) + EPS)
            total += jnp.sum(d * r * rr, axis=0, keepdims=True)
            u = d * gain_ref[...]
            x[cut, :] = (r + out_acc[cut, :]).astype(BF16)
            mean = jnp.mean(u * r, axis=1, keepdims=True)
            d = ct[cut, :].astype(F32) + rr * u - r * (rr * rr * rr * mean)
            res[cut, :] = d
            d_attn[cut, :] = d.astype(BF16)
            do[:, cut] = dot(out_w[...], d_attn[cut, :], 1, 1).astype(BF16)
        gain_sum[...] = total
        for i in (0, 1, 2, 5):
            gives[i].start()

    def source(u, device):
        lo, size = u.rows
        if u.source == 0:
            per = ff // CUBE
            return hid_t[pl.ds(pl.multiple_of(device * per + lo, 16), size), :]
        return hn_t[device, pl.ds(lo, size), :]

    def product(u, a, lo, size):
        b = ct if u.target == 0 else d_gate
        return dot(a, b[:, pl.ds(lo, size)], 1, 0)

    sums = Sums(units, take, outs, source, product)
    for r in loads:
        r.start()
    sums.meet()
    attend()
    for r in loads[3:5]:
        r.wait()
    for i in range(tiles):
        hidden_tile(i)
    for r in loads[5:]:
        r.wait()
    downs = sum(u.source == 0 for u in units)
    spread = max(1, downs)
    work = {}
    for i in range(tiles):
        work.setdefault(i * spread // tiles, []).append(functools.partial(back_tile, i))
    work.setdefault(spread + 1, []).append(residual)
    begins = [c if c < downs else c for c in range(len(units))]
    sums.run(begins, work)
    sums.finish()
    for r in gives:
        r.wait()


def ffn(att_t, x, ct, g_out, g_gate, g_up, g_down, gain, collective_id, most):
    width, tokens = att_t.shape
    ff = g_gate.shape[1]
    high = width // CUBE
    units = weight_units([(0, 0, 0, ff // CUBE, width), (1, 1, 1, high, ff)], most)
    anywhere = pl.BlockSpec(memory_space=pl.ANY)
    vmem = pl.BlockSpec(memory_space=pltpu.VMEM)
    shape = jax.ShapeDtypeStruct
    by_token, by_width = (tokens, width), (width, tokens)
    return pl.pallas_call(
        functools.partial(ffn_kernel, units),
        in_specs=[anywhere] * 7 + [vmem],
        out_specs=[anywhere] * 6 + [vmem] + [anywhere] * 2,
        out_shape=[
            shape(by_token, BF16), shape(by_token, F32), shape(by_width, BF16),
            shape((CUBE, high, tokens), BF16), shape((tokens, ff), BF16), shape(by_token, BF16),
            shape((1, width), F32), shape((ff // CUBE, width), BF16), shape((high, ff), BF16),
        ],
        scratch_shapes=[
            pltpu.VMEM(by_width, BF16), pltpu.VMEM(by_token, BF16), pltpu.VMEM(by_token, BF16),
            pltpu.VMEM((width, width), BF16), pltpu.VMEM((width, ff), BF16),
            pltpu.VMEM((width, ff), BF16), pltpu.VMEM((ff, width), BF16),
            pltpu.VMEM(by_token, F32), pltpu.VMEM(by_token, BF16),
            pltpu.VMEM((CUBE, high, tokens), BF16), pltpu.VMEM((ff, tokens), BF16),
            pltpu.VMEM((tokens, ff), BF16), pltpu.VMEM((tokens, ff), BF16),
            pltpu.VMEM(by_token, F32), pltpu.VMEM(by_token, F32), SEM((7,)), SEM((6,)),
        ] + sum_scratch(units, tokens),
        compiler_params=pltpu.CompilerParams(
            collective_id=collective_id, has_side_effects=True, vmem_limit_bytes=62 * 1024 * 1024
        ),
        name="feed_forward",
    )(att_t, x, ct, g_out, g_gate, g_up, g_down, gain)


def last_kernel(units, *refs):
    refs = list(refs)
    take = lambda n: [refs.pop(0) for _ in range(n)]
    far = take(6)
    far_keys, far_w, far_x, far_res = *take(1), take(3), *take(2)
    cos_ref, sin_ref, gain_ref, gain_two = take(4)
    outs = take(4)
    far_grad, total = take(2)
    near = take(6)
    xn_t, hn_t, att, dq, d_up, d_attn = near
    dkv, w, x, res, gain_buf = *take(1), take(3), *take(3)
    load, tail_load, gain_sent, gain_came = take(4)
    kd, tokens = dkv.shape[0] // 2, dkv.shape[1]
    loads = [pltpu.make_async_copy(a, b, load.at[i]) for i, (a, b) in enumerate(zip(far, near))]
    tail_loads = [
        pltpu.make_async_copy(a, b, tail_load.at[i])
        for i, (a, b) in enumerate(zip([*far_w, far_x, far_res], [*w, x, res]))
    ]
    give = pltpu.make_async_copy(res, far_grad, tail_load.at[len(tail_loads)])
    ready = set()

    def need(copies, i):
        if (copies is loads, i) not in ready:
            ready.add((copies is loads, i))
            copies[i].wait()

    def source(u, device):
        need(loads, u.source)
        return near[u.source][device, pl.ds(*u.rows), :]

    def product(u, a, lo, size):
        if u.target is None:
            return dot(a, dkv[pl.ds(lo, size), :], 1, 1)
        need(loads, u.target)
        if u.target == 3:
            return dot(a, dq[pl.ds(lo, size), :], 1, 1)
        return dot(a, near[u.target][:, pl.ds(lo, size)], 1, 0)

    def keys_done(c, got):
        lanes = slice(c * BLOCK, (c + 1) * BLOCK)
        cs, sn = cos_ref[:, lanes], sin_ref[:, lanes]
        half = HDIM // 2
        for h in range(0, kd, HDIM):
            one = got[h : h + half, :].astype(F32)
            two = got[h + half : h + HDIM, :].astype(F32)
            dkv[h : h + half, lanes] = (one * cs + two * sn).astype(BF16)
            dkv[h + half : h + HDIM, lanes] = (two * cs - one * sn).astype(BF16)
        dkv[kd:, lanes] = got[kd:, :]

    def input_grad():
        need(loads, 3)
        for i in range(len(tail_loads)):
            need(tail_loads, i)
        sum_one = jnp.zeros(gain_two.shape, F32)
        for lo in range(0, tokens, BLOCK):
            cut = slice(lo, lo + BLOCK)
            d = dot(dq[:, cut], w[0][...], 0, 1)
            d += dot(dkv[:kd, cut], w[1][...], 0, 1)
            d += dot(dkv[kd:, cut], w[2][...], 0, 1)
            v = x[cut, :].astype(F32)
            rr = lax.rsqrt(jnp.mean(v * v, axis=1, keepdims=True) + EPS)
            sum_one += jnp.sum(d * v * rr, axis=0, keepdims=True)
            u = d * gain_ref[...]
            mean = jnp.mean(u * v, axis=1, keepdims=True)
            res[cut, :] = res[cut, :] + rr * u - v * (rr * rr * rr * mean)
        gain_buf[0, 0:1, :] = sum_one
        gain_buf[0, 1:2, :] = gain_two[...]
        give.start()

    sums = Sums(units, take, outs, source, product, far_keys, keys_done)
    gain_ways = [*sums.way.values(), sums.near, sums.across]

    def gain_copy(i):
        return pltpu.make_async_remote_copy(
            src_ref=gain_buf.at[2 * i], dst_ref=gain_buf.at[2 * i + 1], send_sem=gain_sent.at[i],
            recv_sem=gain_came.at[i], device_id=gain_ways[i], device_id_type=pl.DeviceIdType.MESH,
        )

    def gain_step(i):
        if i:
            gain_copy(i - 1).wait_recv()
            gain_buf[2 * i] = gain_buf[2 * i - 2] + gain_buf[2 * i - 1]
        if i < len(gain_ways):
            gain_copy(i).start()

    for r in loads + tail_loads:
        r.start()
    sums.meet()
    begins, after = [], 0
    for c, u in enumerate(units):
        begins.append(c if not begins else begins[-1] + 1)
        if u.source is None:
            after = begins[-1] + 3 * LAGS + 1
        elif u.target is None:
            begins[-1] = max(begins[-1], after)
    work = {after: [input_grad]}
    for i in range(len(gain_ways) + 1):
        work.setdefault(after + i, []).append(functools.partial(gain_step, i))
    sums.run(begins, work)
    total[...] = gain_buf[2 * len(gain_ways)]
    sums.finish()
    for i in range(len(gain_ways)):
        gain_copy(i).wait_send()
    give.wait()


def last_sums(xn_t, hn_t, att_t, dq, d_up, d_attn, keys, weights, x, d_res, cos, sin, gain, gain_two, collective_id, most):
    count, high, tokens = xn_t.shape
    width, ff = count * high, d_up.shape[1]
    rows = keys.shape[1] * BLOCK // tokens
    units = [
        Unit(None, None, None, (rows * i, rows), (0, BLOCK), (ALONG_X, ALONG_Y)[i % 2])
        for i in range(tokens // BLOCK)
    ]
    units = weight_units(
        [(1, 4, 2, high, ff), (2, 5, 3, high, width), (0, 3, 0, high, width), (0, None, 1, high, rows)], most, units
    )
    anywhere = pl.BlockSpec(memory_space=pl.ANY)
    vmem = pl.BlockSpec(memory_space=pltpu.VMEM)
    shape = jax.ShapeDtypeStruct
    near = (xn_t, hn_t, att_t, dq, d_up, d_attn)
    return pl.pallas_call(
        functools.partial(last_kernel, units),
        in_specs=[anywhere] * 12 + [vmem] * 4,
        out_specs=[anywhere] * 5 + [vmem],
        out_shape=[
            shape((high, width), BF16), shape((high, rows), BF16), shape((high, ff), BF16),
            shape((high, width), BF16), shape((tokens, width), F32), shape((2, width), F32),
        ],
        scratch_shapes=[pltpu.VMEM(a.shape, a.dtype) for a in near]
        + [pltpu.VMEM((rows, tokens), BF16)]
        + [pltpu.VMEM(a.shape, a.dtype) for a in (*weights, x, d_res)]
        + [pltpu.VMEM((11, 2, width), F32), SEM((6,)), SEM((6,)), SEM((5,)), SEM((5,))]
        + sum_scratch(units, tokens),
        compiler_params=pltpu.CompilerParams(
            collective_id=collective_id, has_side_effects=True, vmem_limit_bytes=62 * 1024 * 1024
        ),
        name="last_sums",
    )(*near, keys, *weights, x, d_res, cos, sin, gain, gain_two)


def row_sum(part, size):
    if size != 4:
        return lax.psum(part, "narrow")
    add = lambda a, b: (a.astype(F32) + b.astype(F32)).astype(BF16)
    part = add(part, lax.ppermute(part, "narrow", [(0, 1), (3, 2)]))
    part = add(part, lax.ppermute(part, "narrow", [(1, 2), (2, 1)]))
    back = lax.ppermute(part, "narrow", [(1, 0), (2, 3)])
    at = lax.axis_index("narrow")
    return jnp.where((at == 1) | (at == 2), part, back)


def turn(v, cos, sin):
    heads = v.reshape(-1, 2, HDIM // 2, v.shape[1])
    one, two = heads[:, 0], heads[:, 1]
    return jnp.stack([one * cos - two * sin, two * cos + one * sin], axis=1).reshape(v.shape)


def turn_back(v, cos, sin):
    return turn(v, cos, -sin)


def shards(sizes, tokens, lengths, block_plan, attn_gain, w_query, w_key, w_value, w_out, ffn_gain,
           w_gate, w_up, w_down, cotangent):
    n = sizes["wide"]
    at = lax.axis_index("wide")
    micro, _, slots, width = tokens.shape
    total = micro * slots
    kd = w_key.shape[1]
    ff = w_gate.shape[1]
    nq = slots // BLOCK
    nb = nq * n

    plan = block_plan[:, 0]
    sizes_of = lengths[:, 0]
    docs = sizes_of.shape[1]
    upto = jnp.arange(docs)[:, None] >= jnp.arange(docs)[None, :]
    ends = jnp.sum(jnp.where(upto[None], sizes_of[:, None, :], 0), axis=2)
    own_plan = lax.dynamic_slice_in_dim(plan, at * nq, nq, axis=1)
    position = own_plan[:, :, None] * BLOCK + jnp.arange(BLOCK, dtype=jnp.int32)
    start = jnp.sum(
        jnp.where(position[..., None] >= ends[:, None, None, :], sizes_of[:, None, None, :], 0), axis=3
    )
    info = jnp.stack([start[:, :, 0] // BLOCK, own_plan], axis=1)
    slot_block = jnp.arange(nb, dtype=jnp.int32)
    where_is = jnp.sum(
        jnp.where(plan[:, None, :] == slot_block[None, :, None], slot_block[None, None, :], 0), axis=2
    )
    start = start.reshape(1, total)
    local = position.reshape(1, total) - start
    frequency = ROPE_BASE ** (-2.0 * jnp.arange(HDIM // 2, dtype=F32) / HDIM)
    angles = frequency[:, None] * local.astype(F32)
    cos, sin = jnp.cos(angles), jnp.sin(angles)

    cube = n == CUBE and sizes["narrow"] == 4 and nq % 2 == 0

    x = tokens.reshape(total, width)
    ct = cotangent.reshape(total, width)
    x_t = x.T
    most = 64 * 1024
    high = width // n
    weights = (w_query, w_key, w_value, w_out, w_gate, w_up, w_down)
    by_device = lambda a: a.reshape(n, -1, a.shape[1])
    gain_one_row, gain_two_row = attn_gain[None], ffn_gain[None]
    if cube:
        got, q_t, xn, kv, _ = start_of(
            weights, by_device(x_t), by_device(attn_gain[:, None]), cos, sin, micro, 2
        )
        g_query, g_key, g_value, g_out, g_gate, g_up, g_down = [a.reshape(-1, a.shape[2]) for a in got]
        att_t, lse = attention_fwd(info, where_is, q_t, start, kv)
        out, d_res, do_t, hn_t, d_up, d_attn, gain_two, s_down, s_gate = ffn(
            att_t, x, ct, g_out, g_gate, g_up, g_down, gain_two_row, 3, most
        )
        dq, dkv = attention_bwd(info, where_is, q_t, do_t, att_t, lse, start, cos, sin, kv)
        s_query, s_kv, s_up, s_out, grad_x, gains = last_sums(
            xn, hn_t, by_device(att_t), dq, d_up, d_attn, dkv.reshape(n, -1, BLOCK),
            (g_query, g_key, g_value), x, d_res, cos, sin, gain_one_row, gain_two, 4, most,
        )
        s_key, s_value = s_kv[:, :kd], s_kv[:, kd:]
    else:
        got = [lax.all_gather(a, "wide", axis=0, tiled=True) for a in weights]
        g_query, g_key, g_value, g_out, g_gate, g_up, g_down = got
        x = x.astype(F32)
        rr1 = lax.rsqrt(jnp.mean(x * x, axis=1, keepdims=True) + EPS)
        xn = (x * rr1 * attn_gain).astype(BF16)
        key_t = turn(dot(g_key, xn, 0, 1), cos, sin).astype(BF16)
        value_t = dot(g_value, xn, 0, 1).astype(BF16)
        own_kv = jnp.concatenate([key_t, value_t]).reshape(2 * kd, micro, nq, BLOCK).transpose(1, 2, 0, 3)
        q_t = (turn(dot(g_query, xn, 0, 1), cos, sin).astype(BF16) * HDIM**-0.5).astype(BF16)
        kv = lax.all_gather(own_kv, "wide", axis=0)
        att_t, lse = attention_fwd(info, where_is, q_t, start, kv)

        res = x + dot(att_t, g_out, 0, 0)
        rr2 = lax.rsqrt(jnp.mean(res * res, axis=1, keepdims=True) + EPS)
        hn = (res * rr2 * ffn_gain).astype(BF16)
        gate, up = dot(hn, g_gate, 1, 0), dot(hn, g_up, 1, 0)
        sg = 1.0 / (1.0 + jnp.exp(-gate))
        hidden = (gate * sg * up).astype(BF16)
        out = (res + dot(hidden, g_down, 1, 0)).astype(BF16)
        d_hidden = dot(ct, g_down, 1, 1)
        d_gate = (d_hidden * up * sg * (1.0 + gate * (1.0 - sg))).astype(BF16)
        d_up = (d_hidden * gate * sg).astype(BF16)
        d_hn = dot(d_gate, g_gate, 1, 1) + dot(d_up, g_up, 1, 1)
        u = d_hn * ffn_gain
        mean = jnp.mean(u * res, axis=1, keepdims=True)
        d_res = ct.astype(F32) + rr2 * u - res * rr2**3 * mean
        gain_two = jnp.sum(d_hn * res * rr2, axis=0)
        d_attn = d_res.astype(BF16)
        do_t = dot(g_out, d_attn, 1, 1).astype(BF16)

        dq, dkv = attention_bwd(info, where_is, q_t, do_t, att_t, lse, start, cos, sin, kv)
        dkv = lax.psum_scatter(dkv, "wide", scatter_dimension=0).transpose(2, 0, 1, 3).reshape(2 * kd, total)
        dk = turn_back(dkv[:kd].astype(F32), cos, sin).astype(BF16)
        dv = dkv[kd:]
        d_xn = dot(dq, g_query, 0, 1) + dot(dk, g_key, 0, 1) + dot(dv, g_value, 0, 1)
        u = d_xn * attn_gain
        grad_x = d_res + rr1 * u - x * rr1**3 * jnp.mean(u * x, axis=1, keepdims=True)
        gain_one = jnp.sum(d_xn * x * rr1, axis=0)
        gains = lax.psum(jnp.stack([gain_one, gain_two]), ("wide", "narrow"))

        def row_part(source, target, ca, cb):
            part = dot(source, target, ca, cb).astype(BF16)
            own = lax.psum_scatter(part, "wide", scatter_dimension=0, tiled=True)
            return row_sum(own, sizes["narrow"])

        s_query, s_key, s_value = row_part(xn, dq, 0, 1), row_part(xn, dk, 0, 1), row_part(xn, dv, 0, 1)
        s_out, s_down = row_part(att_t, d_attn, 1, 0), row_part(hidden, ct, 0, 0)
        s_gate, s_up = row_part(hn, d_gate, 0, 0), row_part(hn, d_up, 0, 0)

    shape = (micro, 1, slots, width)
    wide_out = lambda a: a.astype(F32)
    return (
        out.reshape(shape),
        grad_x.reshape(shape),
        gains[0],
        wide_out(s_query),
        wide_out(s_key),
        wide_out(s_value),
        wide_out(s_out),
        gains[1],
        wide_out(s_gate),
        wide_out(s_up),
        wide_out(s_down),
    )


def solution(mesh):
    by_slot = P(None, "narrow", "wide", None)
    by_row = P(None, "narrow", None)
    split = P("wide", None)
    in_specs = (
        by_slot, by_row, by_row, P(), split, split, split, split, P(), split, split, split, by_slot,
    )
    out_specs = (
        by_slot, by_slot, P(), split, split, split, split, P(), split, split, split,
    )
    return jax.shard_map(
        functools.partial(shards, dict(mesh.shape)),
        mesh=mesh,
        in_specs=in_specs,
        out_specs=out_specs,
        check_vma=False,
    )
```

```python
import functools

import jax
import jax.numpy as jnp
from jax import lax
from jax.experimental import pallas as pl
from jax.experimental.pallas import tpu as pltpu
from jax.sharding import PartitionSpec as P

HDIM = 64
BLOCK = 128
EPS = 1e-05
ROPE_BASE = 100000.0
NEG_FILL = -1e30
F32 = jnp.float32
BF16 = jnp.bfloat16
VMEM_LIMIT = 56 * 1024 * 1024


def dot(a, b, ca, cb):
    return lax.dot_general(a, b, (((ca,), (cb,)), ((), ())), preferred_element_type=F32)


def live_mask(qpos, start, p):
    kpos = p * BLOCK + lax.broadcasted_iota(jnp.int32, (BLOCK, BLOCK), 0)
    return (kpos <= qpos) & (kpos >= start)


STEP = 2


def pick(kv_ref, kvat, mb, qpos, start, b, t, share):
    nq = kv_ref.shape[2]
    blocks = [b - STEP * t - i for i in range(STEP)]
    slots = [kvat[mb, jnp.maximum(p, 0)] for p in blocks]
    at = [(lax.div(s, nq), lax.rem(s, nq)) for s in slots]
    ok = jnp.concatenate([live_mask(qpos, start, p) for p in blocks], axis=0)

    def keys(g):
        rows = slice(g * HDIM, (g + 1) * HDIM)
        return jnp.concatenate([kv_ref[d, 0, s, rows, :] for d, s in at], axis=1)

    return keys, at, jnp.concatenate([ok] * share, axis=1)


def fwd_kernel(groups, share, info, kvat, q_ref, start_ref, kv_ref, o_ref, lse_ref, qs, m_s, l_s, acc, s_s, w_s):
    mb, i = pl.program_id(0), pl.program_id(1)
    lo, b = info[mb, 0, i], info[mb, 1, i]
    nq = kv_ref.shape[2]
    lanes = share * BLOCK
    for g in range(groups):
        for h in range(share):
            at = (g * share + h) * HDIM
            qs[g, :, h * BLOCK : (h + 1) * BLOCK] = q_ref[at : at + HDIM, :]
    m_s[...] = jnp.full_like(m_s, NEG_FILL)
    l_s[...] = jnp.zeros_like(l_s)
    acc[...] = jnp.zeros_like(acc)
    qpos = b * BLOCK + lax.broadcasted_iota(jnp.int32, (1, BLOCK), 1)
    start = start_ref[...]

    def step(t, carry):
        keys, at, ok = pick(kv_ref, kvat, mb, qpos, start, b, t, share)
        for g in range(groups):
            s_s[g] = jnp.where(ok, dot(keys(g), qs[g], 0, 0), NEG_FILL)
        alphas = []
        for g in range(groups):
            s = s_s[g]
            m_old = m_s[g]
            m_new = jnp.maximum(m_old, jnp.max(s, axis=0, keepdims=True))
            w = jnp.exp(s - m_new)
            alpha = jnp.exp(m_old - m_new)
            l_s[g] = l_s[g] * alpha + jnp.sum(w, axis=0, keepdims=True)
            m_s[g] = m_new
            w_s[g] = w.astype(BF16)
            alphas.append(alpha)
        for g in range(groups):
            acc[g] = acc[g] * alphas[g] + dot(keys(groups + g), w_s[g], 1, 0)
        return carry

    lax.fori_loop(0, (b - lo + STEP) // STEP, step, 0)
    for g in range(groups):
        total = l_s[g]
        out = (acc[g] / total).astype(BF16)
        for h in range(share):
            at = (g * share + h) * HDIM
            o_ref[at : at + HDIM, :] = out[:, h * BLOCK : (h + 1) * BLOCK]
        lse_ref[0, g : g + 1, :] = m_s[g] + jnp.log(total)


def attention_fwd(info, kvat, q_t, start, kv):
    width = q_t.shape[0]
    n, micro, nq, kvw, _ = kv.shape
    groups = kvw // HDIM // 2
    share = width // HDIM // groups
    lanes = share * BLOCK
    tok = lambda rows: pl.BlockSpec((rows, BLOCK), lambda m, i, *_: (0, m * nq + i))
    return pl.pallas_call(
        functools.partial(fwd_kernel, groups, share),
        grid_spec=pltpu.PrefetchScalarGridSpec(
            num_scalar_prefetch=2,
            grid=(micro, nq),
            in_specs=[
                tok(width),
                tok(1),
                pl.BlockSpec((n, 1, nq, kvw, BLOCK), lambda m, i, *_: (0, m, 0, 0, 0)),
            ],
            out_specs=[
                tok(width),
                pl.BlockSpec((1, groups, lanes), lambda m, i, *_: (m * nq + i, 0, 0)),
            ],
            scratch_shapes=[
                pltpu.VMEM((groups, HDIM, lanes), BF16),
                pltpu.VMEM((groups, 1, lanes), F32),
                pltpu.VMEM((groups, 1, lanes), F32),
                pltpu.VMEM((groups, HDIM, lanes), F32),
                pltpu.VMEM((groups, STEP * BLOCK, lanes), F32),
                pltpu.VMEM((groups, STEP * BLOCK, lanes), BF16),
            ],
        ),
        out_shape=[
            jax.ShapeDtypeStruct(q_t.shape, BF16),
            jax.ShapeDtypeStruct((micro * nq, groups, lanes), F32),
        ],
        compiler_params=pltpu.CompilerParams(vmem_limit_bytes=VMEM_LIMIT),
        cost_estimate=pl.CostEstimate(
            flops=int(1e10), bytes_accessed=int(8e6), transcendentals=int(8e6)
        ),
        name="attention_fwd",
    )(info, kvat, q_t, start, kv)


def bwd_kernel(
    groups, share, info, kvat, q_ref, do_ref, o_ref, lse_ref, start_ref, cos_ref, sin_ref, kv_ref,
    dq_ref, dkv_ref, qs, dos, delta, dq, dkv, s_s, d_s, w_s, ds_s,
):
    mb, i = pl.program_id(0), pl.program_id(1)
    lo, b = info[mb, 0, i], info[mb, 1, i]
    nq = kv_ref.shape[2]

    @pl.when(i == 0)
    def _():
        dkv[...] = jnp.zeros_like(dkv)

    for g in range(groups):
        for h in range(share):
            at = (g * share + h) * HDIM
            cols = slice(h * BLOCK, (h + 1) * BLOCK)
            d_out = do_ref[at : at + HDIM, :]
            qs[g, :, cols] = q_ref[at : at + HDIM, :]
            dos[g, :, cols] = d_out
            delta[g, :, cols] = jnp.sum(
                d_out.astype(F32) * o_ref[at : at + HDIM, :].astype(F32), axis=0, keepdims=True
            )
    dq[...] = jnp.zeros_like(dq)
    qpos = b * BLOCK + lax.broadcasted_iota(jnp.int32, (1, BLOCK), 1)
    start = start_ref[...]

    def step(t, carry):
        keys, at, ok = pick(kv_ref, kvat, mb, qpos, start, b, t, share)
        for g in range(groups):
            s_s[g] = jnp.where(ok, dot(keys(g), qs[g], 0, 0), NEG_FILL)
            d_s[g] = dot(keys(groups + g), dos[g], 0, 0)
        for g in range(groups):
            w = jnp.exp(s_s[g] - lse_ref[0, g : g + 1, :])
            w_s[g] = w.astype(BF16)
            ds_s[g] = (w * (d_s[g] - delta[g])).astype(BF16)
        for g in range(groups):
            dq[g] += dot(keys(g), ds_s[g], 1, 0)
            dk = dot(qs[g], ds_s[g], 1, 1)
            dv = dot(dos[g], w_s[g], 1, 1)
            krows = slice(g * HDIM, (g + 1) * HDIM)
            vrows = slice((groups + g) * HDIM, (groups + g + 1) * HDIM)
            for i in range(STEP):
                cols = slice(i * BLOCK, (i + 1) * BLOCK)
                dkv[at[i][0], at[i][1], krows, :] += dk[:, cols]
                dkv[at[i][0], at[i][1], vrows, :] += dv[:, cols]
        return carry

    lax.fori_loop(0, (b - lo + STEP) // STEP, step, 0)
    cos, sin = cos_ref[...], sin_ref[...]
    half = HDIM // 2
    for g in range(groups):
        for h in range(share):
            at = (g * share + h) * HDIM
            one = dq[g, :half, h * BLOCK : (h + 1) * BLOCK] * HDIM**-0.5
            two = dq[g, half:, h * BLOCK : (h + 1) * BLOCK] * HDIM**-0.5
            dq_ref[at : at + half, :] = (one * cos + two * sin).astype(BF16)
            dq_ref[at + half : at + HDIM, :] = (two * cos - one * sin).astype(BF16)

    @pl.when(i == nq - 1)
    def _():
        dkv_ref[:, 0] = dkv[...].astype(BF16)


def attention_bwd(info, kvat, q_t, do_t, o_t, lse, start, cos_t, sin_t, kv):
    width = q_t.shape[0]
    n, micro, nq, kvw, _ = kv.shape
    groups = kvw // HDIM // 2
    share = width // HDIM // groups
    lanes = share * BLOCK
    tok = lambda rows: pl.BlockSpec((rows, BLOCK), lambda m, i, *_: (0, m * nq + i))
    keys = pl.BlockSpec((n, 1, nq, kvw, BLOCK), lambda m, i, *_: (0, m, 0, 0, 0))
    return pl.pallas_call(
        functools.partial(bwd_kernel, groups, share),
        grid_spec=pltpu.PrefetchScalarGridSpec(
            num_scalar_prefetch=2,
            grid=(micro, nq),
            in_specs=[
                tok(width),
                tok(width),
                tok(width),
                pl.BlockSpec((1, groups, lanes), lambda m, i, *_: (m * nq + i, 0, 0)),
                tok(1),
                tok(HDIM // 2),
                tok(HDIM // 2),
                keys,
            ],
            out_specs=[tok(width), keys],
            scratch_shapes=[
                pltpu.VMEM((groups, HDIM, lanes), BF16),
                pltpu.VMEM((groups, HDIM, lanes), BF16),
                pltpu.VMEM((groups, 1, lanes), F32),
                pltpu.VMEM((groups, HDIM, lanes), F32),
                pltpu.VMEM((n, nq, kvw, BLOCK), F32),
                pltpu.VMEM((groups, STEP * BLOCK, lanes), F32),
                pltpu.VMEM((groups, STEP * BLOCK, lanes), F32),
                pltpu.VMEM((groups, STEP * BLOCK, lanes), BF16),
                pltpu.VMEM((groups, STEP * BLOCK, lanes), BF16),
            ],
        ),
        out_shape=[
            jax.ShapeDtypeStruct(q_t.shape, BF16),
            jax.ShapeDtypeStruct(kv.shape, BF16),
        ],
        compiler_params=pltpu.CompilerParams(vmem_limit_bytes=VMEM_LIMIT),
        cost_estimate=pl.CostEstimate(
            flops=int(2e10), bytes_accessed=int(16e6), transcendentals=int(8e6)
        ),
        name="attention_bwd",
    )(info, kvat, q_t, do_t, o_t, lse, start, cos_t, sin_t, kv)


CORE, ALONG_X, ALONG_Y = 1, 2, 4
FAR = ALONG_X + ALONG_Y
CUBE = 8
LAG = 2
LAGS = 2
SEM = pltpu.SemaphoreType.DMA


def meet(peers):
    barrier = pltpu.get_barrier_semaphore()
    for peer in peers:
        pl.semaphore_signal(barrier, inc=1, device_id=peer, device_id_type=pl.DeviceIdType.MESH)
    pl.semaphore_wait(barrier, len(peers))


def weight_chunks(shapes, most=160 * 1024):
    chunks = []
    for a, (rows, cols) in enumerate(shapes):
        n = 1
        while rows * cols // n > most and rows % (32 * n) == 0:
            n *= 2
        k = 1
        while rows // n * cols // k > most and cols % (256 * k) == 0:
            k *= 2
        for i in range(n):
            lo, hi = rows // n * i, rows // n * (i + 1)
            mid = lo + -(-(hi - lo) // 32) * 16
            for j in range(k):
                c = pl.ds(cols // k * j, cols // k)
                chunks.append((a, (pl.ds(lo, mid - lo), c), (pl.ds(mid, hi - mid), c)))
    return chunks


def pieces_of(total, size):
    return [(lo, min(size, total - lo)) for lo in range(0, total, size)]


def start_kernel(chunks, micro, *refs):
    refs = list(refs)
    take_refs = lambda n: [refs.pop(0) for _ in range(n)]
    ins = take_refs(6)
    far_x, far_ct, gain_ref, cos_ref, sin_ref = take_refs(5)
    outs = take_refs(6)
    far_q, far_xn, far_kv, far_x_tok, far_ct_tok = take_refs(5)
    near_w = take_refs(2)
    x, ct, x_tok, ct_tok, xn, q_s, own_kv, sent, came, local = take_refs(10)
    at, row = lax.axis_index("wide"), lax.axis_index("narrow")
    peer = {bit: (at ^ bit, row) for bit in (CORE, ALONG_X, ALONG_Y)}
    peer["row"] = (at, row ^ 1)
    keys = len(ins)
    source = [*ins, own_kv]
    land = [*near_w, *outs[2:], far_kv]
    n = len(chunks)
    kd = own_kv.shape[2] // 2
    nq = own_kv.shape[1]
    width, half = q_s.shape[0], HDIM // 2

    mine_in = [pltpu.make_async_copy(ins[i], near_w[i].at[at], local.at[i]) for i in range(2)]
    give = [pltpu.make_async_copy(near_w[i], outs[i], local.at[2 + i]) for i in range(2)]
    give_q = pltpu.make_async_copy(q_s, far_q, local.at[4])
    give_xn = pltpu.make_async_copy(xn, far_xn, local.at[5])
    give_kv = pltpu.make_async_copy(own_kv, far_kv.at[at], local.at[6])
    give_x = pltpu.make_async_copy(x_tok, far_x_tok, local.at[7])
    give_ct = pltpu.make_async_copy(ct_tok, far_ct_tok, local.at[8])
    each = x.shape[2] // micro
    halves_of = lambda far, near, first: [
        pltpu.make_async_copy(far.at[m], near.at[:, :, pl.ds(m * each, each)], local.at[first + m])
        for m in range(micro)
    ]
    x_in, ct_in = halves_of(far_x, x, 9), halves_of(far_ct, ct, 9 + micro)

    def norm():
        for r in x_in:
            r.wait()
        count, high, tokens = x.shape
        square = jnp.zeros((1, tokens), F32)
        for j in range(count):
            v = x[j].astype(F32)
            square += jnp.sum(v * v, axis=0, keepdims=True)
        rr = lax.rsqrt(square / width + EPS)
        gain = jnp.broadcast_to(gain_ref[...], (BLOCK, width)).T
        for j in range(count):
            xn[j] = (x[j].astype(F32) * rr * gain[j * high : (j + 1) * high, 0:1]).astype(BF16)
        give_xn.start()

    def by_token(near, tok, copies, out):
        for r in copies:
            r.wait()
        for lo in range(0, tok.shape[0], BLOCK):
            tok[lo : lo + BLOCK, :] = near[:, :, lo : lo + BLOCK].astype(F32).reshape(width, BLOCK).T.astype(BF16)
        out.start()

    def turned(w, lo, size):
        return sum(dot(w[j, :, lo : lo + size], xn[j], 0, 0) for j in range(w.shape[0]))

    def heads(got):
        cos, sin = cos_ref[...], sin_ref[...]
        for h in range(0, got.shape[0], HDIM):
            one, two = got[h : h + half], got[h + half : h + HDIM]
            yield h, one * cos - two * sin
            yield h + half, two * cos + one * sin

    def to_keys(at_row, value):
        value = value.astype(BF16)
        for m in range(micro):
            for i in range(nq):
                lanes = slice((m * nq + i) * BLOCK, (m * nq + i + 1) * BLOCK)
                own_kv[m, i, at_row : at_row + value.shape[0], :] = value[:, lanes]

    def key_tile(lo, size):
        got = turned(near_w[1], lo, size)
        turn_to = max(0, min(kd - lo, size))
        for h, v in heads(got[:turn_to]):
            to_keys(lo + h, v)
        if turn_to < size:
            to_keys(lo + turn_to, got[turn_to:])

    def query_tile(lo, size):
        for h, v in heads(turned(near_w[0], lo, size)):
            q_s[lo + h : lo + h + half, :] = v.astype(BF16) * HDIM**-0.5

    def run(mine):
        other = 1 - mine
        used = [0] * n
        begun = []

        def part(ref, c, which):
            return ref.at[chunks[c][1 + which]]

        def copy(c, m, which, way, slot):
            a = chunks[c][0]
            there = part(land[a].at[at ^ m], c, which)
            return pltpu.make_async_remote_copy(
                src_ref=there if m else part(source[a], c, which),
                dst_ref=there,
                send_sem=sent.at[c, slot],
                recv_sem=came.at[c, m if way == "row" else m ^ way, which],
                device_id=peer[way],
                device_id_type=pl.DeviceIdType.MESH,
            )

        def push(c, m, which, way):
            r = copy(c, m, which, way, used[c])
            used[c] += 1
            r.start()
            begun.append(r)

        def take(c, m, which, *ways):
            copy(c, m ^ CORE, which, CORE, 0).wait_recv()
            for way in ways:
                push(c, m, which, way)

        planes = [c[0] != keys for c in chunks]
        bounced = [1 < c[0] < keys for c in chunks]

        def first(c):
            push(c, 0, mine, ALONG_X)
            push(c, 0, mine, ALONG_Y)
            if not planes[c]:
                push(c, 0, other, ALONG_X)
                push(c, 0, other, ALONG_Y)

        def second(c):
            if planes[c]:
                take(c, ALONG_Y, mine, ALONG_X, CORE)
                push(c, 0, other, ALONG_Y)
                take(c, ALONG_X, mine, "row", CORE)
            else:
                take(c, ALONG_X, mine, ALONG_Y, CORE)
                take(c, ALONG_Y, other, ALONG_X, CORE)
                take(c, ALONG_Y, mine, CORE)
                take(c, ALONG_X, other, CORE)
            push(c, 0, 0, CORE)
            push(c, 0, 1, CORE)

        def third(c):
            take(c, FAR, mine, *(("row", CORE) if planes[c] else (CORE,)))
            if planes[c]:
                take(c, ALONG_Y, other, CORE)
                take(c, ALONG_X, other, CORE)
            else:
                take(c, FAR, other, CORE)

        def fourth(c):
            if planes[c]:
                take(c, FAR, other, CORE)

        def fifth(c):
            for which in range(2):
                take(c, CORE, which, *((CORE,) if bounced[c] else ()))
            for m in (ALONG_X, ALONG_Y, FAR):
                for which in range(2):
                    take(c, m + CORE, which)

        def sixth(c):
            if bounced[c]:
                for which in range(2):
                    take(c, 0, which)

        steps = (first, second, third, fourth, fifth, sixth)
        begins, ready = [], 0
        for c in range(n):
            begins.append(c)
            if chunks[c][0] < 2:
                ready = c + LAG * 4
            if chunks[c][0] == keys:
                begins[c] = max(begins[c - 1] + 1, ready + 1)
        work = {1: [norm], ready: []}
        work[2] = [functools.partial(by_token, x, x_tok, (), give_x)]
        work[3] = [functools.partial(by_token, ct, ct_tok, ct_in, give_ct)]
        for lo, size in pieces_of(2 * kd, 256):
            work[ready].append(functools.partial(key_tile, lo, size))
        work[ready].append(give_kv.start)
        for i, (lo, size) in enumerate(pieces_of(width, 256)):
            work[ready + 2 + i] = [functools.partial(query_tile, lo, size)]
        for t in range(begins[-1] + LAG * (len(steps) - 1) + 1):
            for s, step in enumerate(steps):
                for c in range(n):
                    if begins[c] + LAG * s == t:
                        step(c)
            if t == ready:
                for r in mine_in:
                    r.wait()
                for r in give:
                    r.start()
            for job in work.get(t, ()):
                job()
        for r in begun:
            r.wait_send()

    for r in (*x_in, *mine_in, *ct_in):
        r.start()
    meet(list(peer.values()))
    for mine in range(2):
        pl.when(row % 2 == mine)(functools.partial(run, mine))
    give_q.start()
    for r in (*give, give_q, give_xn, give_kv, give_x, give_ct):
        r.wait()


def start_of(weights, x, ct, gain, cos, sin, collective_id):
    micro, count, high, each = x.shape
    tokens, width = micro * each, count * high
    kd = weights[1].shape[1] // 2
    nq = each // BLOCK
    chunks = weight_chunks([a.shape for a in weights])
    keys = len(weights)
    for m in range(micro):
        for i in range(2):
            rows = pl.ds(kd * i, kd)
            halves = [(m, pl.ds(nq // 2 * h, nq // 2), rows) for h in range(2)]
            chunks.append((keys, *halves))
    anywhere = pl.BlockSpec(memory_space=pl.ANY)
    vmem = pl.BlockSpec(memory_space=pltpu.VMEM)
    shape = jax.ShapeDtypeStruct
    kv = (micro, nq, 2 * kd, BLOCK)
    split = pltpu.VMEM((count, high, tokens), BF16)
    by_token = pltpu.VMEM((tokens, width), BF16)
    got = pl.pallas_call(
        functools.partial(start_kernel, chunks, micro),
        in_specs=[anywhere] * (keys + 2) + [vmem] * 3,
        out_specs=[anywhere] * (keys + 5),
        out_shape=[shape((count,) + a.shape, BF16) for a in weights]
        + [shape((width, tokens), BF16), shape((count, high, tokens), BF16), shape((count,) + kv, BF16)]
        + [shape((tokens, width), BF16)] * 2,
        scratch_shapes=[pltpu.VMEM((count,) + a.shape, BF16) for a in weights[:2]]
        + [split, split, by_token, by_token, split, pltpu.VMEM((width, tokens), BF16), pltpu.VMEM(kv, BF16)]
        + [SEM((len(chunks), 16)), SEM((len(chunks), 8, 2)), SEM((9 + 2 * micro,))],
        compiler_params=pltpu.CompilerParams(
            collective_id=collective_id, has_side_effects=True, vmem_limit_bytes=VMEM_LIMIT
        ),
        name="gather_and_project",
    )(*weights, x, ct, gain, cos, sin)
    return got[:keys], *got[keys:]


class Unit:
    def __init__(self, source, target, out, rows, cols, first):
        self.source, self.target, self.out = source, target, out
        self.rows, self.cols, self.first = rows, cols, first

    @property
    def shape(self):
        return (self.rows[1], self.cols[1])


def weight_units(sizes, most, units=()):
    units = list(units)
    for source, target, out, rows, cols in sizes:
        k = 1
        while cols % (256 * k) == 0 and rows * cols // k > most:
            k *= 2
        high = -(-rows // max(1, round(rows * cols / k / most)) // 16) * 16
        cols_cuts = pieces_of(cols, cols // k)
        if out == sizes[-1][2] and cols % BLOCK == 0:
            lo, size = cols_cuts.pop()
            while size > BLOCK:
                part = -(-size // (2 * BLOCK)) * BLOCK
                cols_cuts.append((lo, part))
                lo, size = lo + part, size - part
            cols_cuts.append((lo, size))
        for rows_cut in pieces_of(rows, high):
            for cols_cut in cols_cuts:
                first = (ALONG_X, ALONG_Y)[len(units) % 2]
                units.append(Unit(source, target, out, rows_cut, cols_cut, first))
    return units


RING = 3


def ring_sizes(units):
    shapes = [u.shape for u in units if u.source is not None]
    return {a: min(RING, shapes.count(a)) for a in shapes}


def sum_scratch(units, tokens):
    n = len(units)
    room = lambda *lead: [pltpu.VMEM(lead + u.shape, BF16) for u in units]
    line = [pltpu.VMEM((2,) + u.shape if u.source is not None else (8, BLOCK), BF16) for u in units]
    rows = max(u.shape[0] for u in units if u.source is not None)
    scratch = room(4) + room(4) + room(2) + room() + line
    scratch += [pltpu.VMEM((4 * rows, tokens), BF16)]
    scratch += [pltpu.VMEM((d, 4) + a, BF16) for a, d in ring_sizes(units).items()]
    return scratch + [SEM((n, 5)), SEM((n, 5)), SEM((n,)), SEM((n, 4)), SEM((n, 4)), SEM((n, 4))]


class Sums:
    def __init__(self, units, take, outs, source, product, far_keys=None, keys_done=None):
        n = len(units)
        self.units, self.outs, self.source, self.product = units, outs, source, product
        self.far_keys, self.keys_done = far_keys, keys_done
        self.held, self.core_in, self.one_in, self.two_in, self.line_in = (take(n) for _ in range(5))
        self.lhs = take(1)[0]
        self.depth = ring_sizes(units)
        self.rings = dict(zip(self.depth, take(len(self.depth))))
        self.sent, self.came, self.stored, self.key_load, self.key_sent, self.key_came = take(6)
        self.at, self.row = lax.axis_index("wide"), lax.axis_index("narrow")
        self.way = {bit: (self.at ^ bit, self.row) for bit in (CORE, ALONG_X, ALONG_Y)}
        self.near, self.across = (self.at, self.row ^ 1), (self.at, self.row ^ 3)
        self.middle = (self.row == 1) | (self.row == 2)
        self.is_keys = [u.source is None for u in units]
        self.steps = (self.s0, self.s1, self.s2, self.s3, self.s4, self.s5, self.s6)

    def meet(self):
        meet([*self.way.values(), self.near, self.across])

    def send(self, c, slot, a, b, to):
        return pltpu.make_async_remote_copy(
            src_ref=a, dst_ref=b, send_sem=self.sent.at[c, slot], recv_sem=self.came.at[c, slot],
            device_id=to, device_id_type=pl.DeviceIdType.MESH,
        )

    @staticmethod
    def add(dst, other):
        rows = dst.shape[-2]
        most = rows // 16
        step = 16 * max(k for k in (1, 2, 3, 4) if most % k == 0)

        def body(i, carry):
            cut = pl.ds(pl.multiple_of(i * step, 16), step)
            dst[cut, :] = dst[cut, :] + other[cut, :]
            return carry

        lax.fori_loop(0, most * 16 // step, body, 0)
        if rows % 16:
            cut = slice(most * 16, rows)
            dst[cut, :] = dst[cut, :] + other[cut, :]

    def order(self, c):
        first = self.units[c].first
        return (0, FAR - first, first, FAR)

    def slot_of(self, c):
        shape = self.units[c].shape
        alike = [i for i, u in enumerate(self.units) if u.source is not None and u.shape == shape]
        return alike.index(c) % self.depth[shape]

    def same_slot(self, i, c):
        if self.is_keys[i] or self.is_keys[c] or self.units[i].shape != self.units[c].shape:
            return False
        return self.slot_of(i) == self.slot_of(c)

    def core_copies(self, c):
        u = self.units[c]
        if not self.is_keys[c]:
            return [self.send(c, 0, self.rings[u.shape].at[self.slot_of(c)], self.core_in[c], self.way[CORE])]
        return [
            pltpu.make_async_remote_copy(
                src_ref=self.far_keys.at[self.at ^ CORE ^ m, pl.ds(*u.rows)], dst_ref=self.core_in[c].at[i],
                send_sem=self.key_sent.at[c, i], recv_sem=self.key_came.at[c, i],
                device_id=self.way[CORE], device_id_type=pl.DeviceIdType.MESH,
            )
            for i, m in enumerate(self.order(c))
        ]

    def key_loads(self, c):
        rows = pl.ds(*self.units[c].rows)
        return [
            pltpu.make_async_copy(self.far_keys.at[self.at ^ m, rows], self.held[c].at[i], self.key_load.at[c, i])
            for i, m in enumerate(self.order(c))
        ]

    def first_copy(self, c):
        return self.send(c, 1, self.held[c].at[pl.ds(2, 2)], self.one_in[c], self.way[self.units[c].first])

    def second_copy(self, c):
        return self.send(c, 2, self.held[c].at[1], self.two_in[c], self.way[FAR - self.units[c].first])

    def inward(self, c):
        return self.send(c, 3, self.held[c].at[0], self.line_in[c].at[0], self.near)

    def over(self, c):
        return self.send(c, 4, self.held[c].at[0], self.line_in[c].at[1], self.across)

    def outward(self, c):
        return self.send(c, 3, self.line_in[c].at[1], self.line_in[c].at[0], self.near)

    def store(self, c, slot):
        u = self.units[c]
        cut = (pl.ds(*u.rows), pl.ds(*u.cols))
        return pltpu.make_async_copy(self.line_in[c].at[slot], self.outs[u.out].at[cut], self.stored.at[c])

    def products(self, c, mine):
        u = self.units[c]
        rows, cols = u.shape
        for i, m in enumerate(self.order(c)):
            self.lhs[pl.ds(i * rows, rows), :] = self.source(u, self.at ^ m ^ mine)
        a = self.lhs[pl.ds(0, 4 * rows), :]
        for lo, size in pieces_of(cols, 256):
            got = self.product(u, a, u.cols[0] + lo, size).astype(BF16).reshape(4, rows, size)
            if mine:
                self.rings[u.shape][self.slot_of(c), :, :, lo : lo + size] = got
            else:
                self.held[c][:, :, lo : lo + size] = got

    def s0(self, c):
        if self.is_keys[c]:
            for r in self.core_copies(c) + self.key_loads(c):
                r.start()
            return
        before = [i for i in range(c) if self.same_slot(i, c)]
        if before:
            self.core_copies(before[-1])[0].wait_send()
        self.products(c, CORE)
        self.core_copies(c)[0].start()
        self.products(c, 0)

    def s1(self, c):
        if self.is_keys[c]:
            for r in self.key_loads(c):
                r.wait()
        for r in self.core_copies(c):
            r.wait_recv()
        for i in (2, 3, 0, 1):
            self.add(self.held[c].at[i], self.core_in[c].at[i])
            if i == 3:
                self.first_copy(c).start()

    def s2(self, c):
        self.first_copy(c).wait_recv()
        self.add(self.held[c].at[1], self.one_in[c].at[1])
        self.second_copy(c).start()
        self.add(self.held[c].at[0], self.one_in[c].at[0])

    def s3(self, c):
        self.second_copy(c).wait_recv()
        self.add(self.held[c].at[0], self.two_in[c])
        if self.is_keys[c]:
            self.keys_done(c, self.held[c].at[0])
        else:
            pl.when(~self.middle)(lambda: self.inward(c).start())

    def s4(self, c):
        @pl.when(self.middle)
        def _():
            self.inward(c).wait_recv()
            self.add(self.held[c].at[0], self.line_in[c].at[0])
            self.over(c).start()

    def s5(self, c):
        @pl.when(self.middle)
        def _():
            self.over(c).wait_recv()
            self.add(self.line_in[c].at[1], self.held[c].at[0])
            self.outward(c).start()
            self.store(c, 1).start()

    def s6(self, c):
        @pl.when(~self.middle)
        def _():
            self.outward(c).wait_recv()
            self.store(c, 0).start()

    def finish(self):
        n = len(self.units)
        for c in range(n):
            if not any(self.same_slot(c, i) for i in range(c + 1, n)):
                for r in self.core_copies(c):
                    r.wait_send()
            self.first_copy(c).wait_send()
            self.second_copy(c).wait_send()
            if not self.is_keys[c]:
                self.inward(c).wait_send()
                pl.when(self.middle)(lambda: self.over(c).wait_send())
                self.store(c, 0).wait()

    def run(self, begins, work):
        last = max(b + LAGS * (len(self.steps) - 1) for b in begins)
        for t in range(max([last, *work]) + 1):
            for s, step in enumerate(self.steps):
                for c, b in enumerate(begins):
                    if b + LAGS * s == t and not (self.is_keys[c] and s > 3):
                        step(c)
            for job in work.get(t, ()):
                job()


TILE = 256


def ffn_kernel(units, *refs):
    refs = list(refs)
    take = lambda n: [refs.pop(0) for _ in range(n)]
    far_att, far_x, far_ct, far_out_w, far_gate_w, far_up_w, far_down_w, gain_ref = take(8)
    far_out, far_res, far_do, far_hn, far_d_up, far_d_attn, gain_sum = take(7)
    outs = take(2)
    att, x, ct, out_w, wg, wu, wd, res, hn, hn_t, hid_t, d_gate, d_up, out_acc, hn_acc = take(15)
    load, give = take(2)
    do, d_attn = att, hn
    width, tokens = att.shape
    ff = hid_t.shape[0]
    tiles = ff // TILE
    slots = range(0, tokens, BLOCK)
    loads = [
        pltpu.make_async_copy(a, b, load.at[i])
        for i, (a, b) in enumerate(
            zip(
                (far_att, far_out_w, far_x, far_gate_w, far_up_w, far_down_w, far_ct),
                (att, out_w, x, wg, wu, wd, ct),
            )
        )
    ]
    gives = [
        pltpu.make_async_copy(a, b, give.at[i])
        for i, (a, b) in enumerate(
            ((x, far_out), (res, far_res), (do, far_do), (hn_t, far_hn), (d_up, far_d_up), (d_attn, far_d_attn))
        )
    ]

    def attend():
        for r in loads[:3]:
            r.wait()
        for lo in slots:
            cut = slice(lo, lo + BLOCK)
            r = x[cut, :].astype(F32) + dot(att[:, cut], out_w[...], 0, 0)
            res[cut, :] = r
            rr = lax.rsqrt(jnp.mean(r * r, axis=1, keepdims=True) + EPS)
            h = r * rr * gain_ref[...]
            hn[cut, :] = h.astype(BF16)
            h = h.T
            high = hn_t.shape[1]
            for j in range(hn_t.shape[0]):
                hn_t[j, :, cut] = h[j * high : (j + 1) * high].astype(BF16)
        gives[3].start()

    def hidden_tile(i):
        cut = slice(i * TILE, (i + 1) * TILE)
        gate, up = dot(hn[...], wg[:, cut], 1, 0), dot(hn[...], wu[:, cut], 1, 0)
        hidden = (gate / (1.0 + jnp.exp(-gate)) * up).astype(BF16)
        hid_t[cut, :] = hidden.T

    def back_tile(i):
        cut = slice(i * TILE, (i + 1) * TILE)
        gate, up = dot(hn[...], wg[:, cut], 1, 0), dot(hn[...], wu[:, cut], 1, 0)
        sg = 1.0 / (1.0 + jnp.exp(-gate))
        act = gate * sg
        hidden = (act * up).astype(BF16)
        d_hidden = dot(ct[...], wd[cut, :], 1, 1)
        d_gate[:, cut] = (d_hidden * up * sg * (1.0 + gate * (1.0 - sg))).astype(BF16)
        d_up[:, cut] = (d_hidden * act).astype(BF16)
        forward = dot(hidden, wd[cut, :], 1, 0)
        back = dot(d_gate[:, cut], wg[:, cut], 1, 1) + dot(d_up[:, cut], wu[:, cut], 1, 1)
        if i == 0:
            out_acc[...] = forward
            hn_acc[...] = back
        else:
            out_acc[...] += forward
            hn_acc[...] += back

    def residual():
        gives[4].start()
        total = jnp.zeros(gain_sum.shape, F32)
        for lo in slots:
            cut = slice(lo, lo + BLOCK)
            r, d = res[cut, :], hn_acc[cut, :]
            rr = lax.rsqrt(jnp.mean(r * r, axis=1, keepdims=True) + EPS)
            total += jnp.sum(d * r * rr, axis=0, keepdims=True)
            u = d * gain_ref[...]
            x[cut, :] = (r + out_acc[cut, :]).astype(BF16)
            mean = jnp.mean(u * r, axis=1, keepdims=True)
            d = ct[cut, :].astype(F32) + rr * u - r * (rr * rr * rr * mean)
            res[cut, :] = d
            d_attn[cut, :] = d.astype(BF16)
            do[:, cut] = dot(out_w[...], d_attn[cut, :], 1, 1).astype(BF16)
        gain_sum[...] = total
        for i in (0, 1, 2, 5):
            gives[i].start()

    def source(u, device):
        lo, size = u.rows
        if u.source == 0:
            per = ff // CUBE
            return hid_t[pl.ds(pl.multiple_of(device * per + lo, 16), size), :]
        return hn_t[device, pl.ds(lo, size), :]

    def product(u, a, lo, size):
        b = ct if u.target == 0 else d_gate
        return dot(a, b[:, pl.ds(lo, size)], 1, 0)

    sums = Sums(units, take, outs, source, product)
    for r in loads:
        r.start()
    sums.meet()
    attend()
    for r in loads[3:5]:
        r.wait()
    for i in range(tiles):
        hidden_tile(i)
    for r in loads[5:]:
        r.wait()
    downs = sum(u.source == 0 for u in units)
    spread = max(1, downs)
    work = {}
    for i in range(tiles):
        work.setdefault(i * spread // tiles, []).append(functools.partial(back_tile, i))
    work.setdefault(spread + 1, []).append(residual)
    begins = [c if c < downs else c for c in range(len(units))]
    sums.run(begins, work)
    sums.finish()
    for r in gives:
        r.wait()


def ffn(att_t, x, ct, g_out, g_gate, g_up, g_down, gain, collective_id, most):
    width, tokens = att_t.shape
    ff = g_gate.shape[1]
    high = width // CUBE
    units = weight_units([(0, 0, 0, ff // CUBE, width), (1, 1, 1, high, ff)], most)
    anywhere = pl.BlockSpec(memory_space=pl.ANY)
    vmem = pl.BlockSpec(memory_space=pltpu.VMEM)
    shape = jax.ShapeDtypeStruct
    by_token, by_width = (tokens, width), (width, tokens)
    return pl.pallas_call(
        functools.partial(ffn_kernel, units),
        in_specs=[anywhere] * 7 + [vmem],
        out_specs=[anywhere] * 6 + [vmem] + [anywhere] * 2,
        out_shape=[
            shape(by_token, BF16), shape(by_token, F32), shape(by_width, BF16),
            shape((CUBE, high, tokens), BF16), shape((tokens, ff), BF16), shape(by_token, BF16),
            shape((1, width), F32), shape((ff // CUBE, width), BF16), shape((high, ff), BF16),
        ],
        scratch_shapes=[
            pltpu.VMEM(by_width, BF16), pltpu.VMEM(by_token, BF16), pltpu.VMEM(by_token, BF16),
            pltpu.VMEM((width, width), BF16), pltpu.VMEM((width, ff), BF16),
            pltpu.VMEM((width, ff), BF16), pltpu.VMEM((ff, width), BF16),
            pltpu.VMEM(by_token, F32), pltpu.VMEM(by_token, BF16),
            pltpu.VMEM((CUBE, high, tokens), BF16), pltpu.VMEM((ff, tokens), BF16),
            pltpu.VMEM((tokens, ff), BF16), pltpu.VMEM((tokens, ff), BF16),
            pltpu.VMEM(by_token, F32), pltpu.VMEM(by_token, F32), SEM((7,)), SEM((6,)),
        ] + sum_scratch(units, tokens),
        compiler_params=pltpu.CompilerParams(
            collective_id=collective_id, has_side_effects=True, vmem_limit_bytes=62 * 1024 * 1024
        ),
        name="feed_forward",
    )(att_t, x, ct, g_out, g_gate, g_up, g_down, gain)


def last_kernel(units, *refs):
    refs = list(refs)
    take = lambda n: [refs.pop(0) for _ in range(n)]
    far = take(6)
    far_keys, far_w, far_x, far_res = *take(1), take(2), *take(2)
    cos_ref, sin_ref, gain_ref, gain_two = take(4)
    outs = take(4)
    far_grad, total = take(2)
    near = take(6)
    xn_t, hn_t, att, dq, d_up, d_attn = near
    dkv, w, x, res, gain_buf = *take(1), take(2), *take(3)
    load, tail_load, gain_sent, gain_came = take(4)
    kd, tokens = dkv.shape[0] // 2, dkv.shape[1]
    loads = [pltpu.make_async_copy(a, b, load.at[i]) for i, (a, b) in enumerate(zip(far, near))]
    tail_loads = [
        pltpu.make_async_copy(a, b, tail_load.at[i])
        for i, (a, b) in enumerate(zip([*far_w, far_x, far_res], [*w, x, res]))
    ]
    give = pltpu.make_async_copy(res, far_grad, tail_load.at[len(tail_loads)])
    ready = set()

    def need(copies, i):
        if (copies is loads, i) not in ready:
            ready.add((copies is loads, i))
            copies[i].wait()

    def source(u, device):
        need(loads, u.source)
        return near[u.source][device, pl.ds(*u.rows), :]

    def product(u, a, lo, size):
        if u.target is None:
            return dot(a, dkv[pl.ds(lo, size), :], 1, 1)
        need(loads, u.target)
        if u.target == 3:
            return dot(a, dq[pl.ds(lo, size), :], 1, 1)
        return dot(a, near[u.target][:, pl.ds(lo, size)], 1, 0)

    def keys_done(c, got):
        lanes = slice(c * BLOCK, (c + 1) * BLOCK)
        cs, sn = cos_ref[:, lanes], sin_ref[:, lanes]
        half = HDIM // 2
        for h in range(0, kd, HDIM):
            one = got[h : h + half, :].astype(F32)
            two = got[h + half : h + HDIM, :].astype(F32)
            dkv[h : h + half, lanes] = (one * cs + two * sn).astype(BF16)
            dkv[h + half : h + HDIM, lanes] = (two * cs - one * sn).astype(BF16)
        dkv[kd:, lanes] = got[kd:, :]

    def input_grad():
        need(loads, 3)
        for i in range(len(tail_loads)):
            need(tail_loads, i)
        sum_one = jnp.zeros(gain_two.shape, F32)
        for lo in range(0, tokens, BLOCK):
            cut = slice(lo, lo + BLOCK)
            d = dot(dq[:, cut], w[0][...], 0, 1)
            d += dot(dkv[:, cut], w[1][...], 0, 1)
            v = x[cut, :].astype(F32)
            rr = lax.rsqrt(jnp.mean(v * v, axis=1, keepdims=True) + EPS)
            sum_one += jnp.sum(d * v * rr, axis=0, keepdims=True)
            u = d * gain_ref[...]
            mean = jnp.mean(u * v, axis=1, keepdims=True)
            res[cut, :] = res[cut, :] + rr * u - v * (rr * rr * rr * mean)
        gain_buf[0, 0:1, :] = sum_one
        gain_buf[0, 1:2, :] = gain_two[...]
        give.start()

    sums = Sums(units, take, outs, source, product, far_keys, keys_done)
    gain_ways = [*sums.way.values(), sums.near, sums.across]

    def gain_copy(i):
        return pltpu.make_async_remote_copy(
            src_ref=gain_buf.at[2 * i], dst_ref=gain_buf.at[2 * i + 1], send_sem=gain_sent.at[i],
            recv_sem=gain_came.at[i], device_id=gain_ways[i], device_id_type=pl.DeviceIdType.MESH,
        )

    def gain_step(i):
        if i:
            gain_copy(i - 1).wait_recv()
            gain_buf[2 * i] = gain_buf[2 * i - 2] + gain_buf[2 * i - 1]
        if i < len(gain_ways):
            gain_copy(i).start()

    for r in loads + tail_loads:
        r.start()
    sums.meet()
    begins, after = [], 0
    for c, u in enumerate(units):
        begins.append(c if not begins else begins[-1] + 1)
        if u.source is None:
            after = begins[-1] + 3 * LAGS + 1
        elif u.target is None:
            begins[-1] = max(begins[-1], after)
    work = {after: [input_grad]}
    for i in range(len(gain_ways) + 1):
        work.setdefault(after + i, []).append(functools.partial(gain_step, i))
    sums.run(begins, work)
    total[...] = gain_buf[2 * len(gain_ways)]
    sums.finish()
    for i in range(len(gain_ways)):
        gain_copy(i).wait_send()
    give.wait()


def last_sums(xn_t, hn_t, att_t, dq, d_up, d_attn, keys, weights, x, d_res, cos, sin, gain, gain_two, collective_id, most):
    count, high, tokens = xn_t.shape
    width, ff = count * high, d_up.shape[1]
    rows = keys.shape[1] * BLOCK // tokens
    units = [
        Unit(None, None, None, (rows * i, rows), (0, BLOCK), (ALONG_X, ALONG_Y)[i % 2])
        for i in range(tokens // BLOCK)
    ]
    units = weight_units(
        [(1, 4, 2, high, ff), (2, 5, 3, high, width), (0, 3, 0, high, width), (0, None, 1, high, rows)], most, units
    )
    anywhere = pl.BlockSpec(memory_space=pl.ANY)
    vmem = pl.BlockSpec(memory_space=pltpu.VMEM)
    shape = jax.ShapeDtypeStruct
    near = (xn_t, hn_t, att_t, dq, d_up, d_attn)
    return pl.pallas_call(
        functools.partial(last_kernel, units),
        in_specs=[anywhere] * 11 + [vmem] * 4,
        out_specs=[anywhere] * 5 + [vmem],
        out_shape=[
            shape((high, width), BF16), shape((high, rows), BF16), shape((high, ff), BF16),
            shape((high, width), BF16), shape((tokens, width), F32), shape((2, width), F32),
        ],
        scratch_shapes=[pltpu.VMEM(a.shape, a.dtype) for a in near]
        + [pltpu.VMEM((rows, tokens), BF16)]
        + [pltpu.VMEM(a.shape, a.dtype) for a in (*weights, x, d_res)]
        + [pltpu.VMEM((11, 2, width), F32), SEM((6,)), SEM((6,)), SEM((5,)), SEM((5,))]
        + sum_scratch(units, tokens),
        compiler_params=pltpu.CompilerParams(
            collective_id=collective_id, has_side_effects=True, vmem_limit_bytes=62 * 1024 * 1024
        ),
        name="last_sums",
    )(*near, keys, *weights, x, d_res, cos, sin, gain, gain_two)


def row_sum(part, size):
    if size != 4:
        return lax.psum(part, "narrow")
    add = lambda a, b: (a.astype(F32) + b.astype(F32)).astype(BF16)
    part = add(part, lax.ppermute(part, "narrow", [(0, 1), (3, 2)]))
    part = add(part, lax.ppermute(part, "narrow", [(1, 2), (2, 1)]))
    back = lax.ppermute(part, "narrow", [(1, 0), (2, 3)])
    at = lax.axis_index("narrow")
    return jnp.where((at == 1) | (at == 2), part, back)


def turn(v, cos, sin):
    heads = v.reshape(-1, 2, HDIM // 2, v.shape[1])
    one, two = heads[:, 0], heads[:, 1]
    return jnp.stack([one * cos - two * sin, two * cos + one * sin], axis=1).reshape(v.shape)


def turn_back(v, cos, sin):
    return turn(v, cos, -sin)


def shards(sizes, tokens, lengths, block_plan, attn_gain, w_query, w_key, w_value, w_out, ffn_gain,
           w_gate, w_up, w_down, cotangent):
    n = sizes["wide"]
    at = lax.axis_index("wide")
    micro, _, slots, width = tokens.shape
    total = micro * slots
    kd = w_key.shape[1]
    ff = w_gate.shape[1]
    nq = slots // BLOCK
    nb = nq * n

    plan = block_plan[:, 0]
    sizes_of = lengths[:, 0]
    docs = sizes_of.shape[1]
    upto = jnp.arange(docs)[:, None] >= jnp.arange(docs)[None, :]
    ends = jnp.sum(jnp.where(upto[None], sizes_of[:, None, :], 0), axis=2)
    own_plan = lax.dynamic_slice_in_dim(plan, at * nq, nq, axis=1)
    position = own_plan[:, :, None] * BLOCK + jnp.arange(BLOCK, dtype=jnp.int32)
    start = jnp.sum(
        jnp.where(position[..., None] >= ends[:, None, None, :], sizes_of[:, None, None, :], 0), axis=3
    )
    info = jnp.stack([start[:, :, 0] // BLOCK, own_plan], axis=1)
    slot_block = jnp.arange(nb, dtype=jnp.int32)
    where_is = jnp.sum(
        jnp.where(plan[:, None, :] == slot_block[None, :, None], slot_block[None, None, :], 0), axis=2
    )
    start = start.reshape(1, total)
    local = position.reshape(1, total) - start
    frequency = ROPE_BASE ** (-2.0 * jnp.arange(HDIM // 2, dtype=F32) / HDIM)
    angles = frequency[:, None] * local.astype(F32)
    cos, sin = jnp.cos(angles), jnp.sin(angles)

    cube = n == CUBE and sizes["narrow"] == 4 and nq % 2 == 0

    x = tokens.reshape(total, width)
    ct = cotangent.reshape(total, width)
    most = 64 * 1024
    high = width // n
    w_kv = jnp.concatenate([w_key, w_value], axis=1)
    weights = (w_query, w_kv, w_out, w_gate, w_up, w_down)
    by_device = lambda a: a.reshape(n, -1, a.shape[1])
    gain_one_row, gain_two_row = attn_gain[None], ffn_gain[None]
    if cube:
        by_width = lambda a: a[:, 0].transpose(0, 2, 1).reshape(micro, n, high, slots)
        got, q_t, xn, kv, x, ct = start_of(
            weights, by_width(tokens), by_width(cotangent), gain_one_row, cos, sin, 2
        )
        g_query, g_kv, g_out, g_gate, g_up, g_down = [a.reshape(-1, a.shape[2]) for a in got]
        att_t, lse = attention_fwd(info, where_is, q_t, start, kv)
        out, d_res, do_t, hn_t, d_up, d_attn, gain_two, s_down, s_gate = ffn(
            att_t, x, ct, g_out, g_gate, g_up, g_down, gain_two_row, 3, most
        )
        dq, dkv = attention_bwd(info, where_is, q_t, do_t, att_t, lse, start, cos, sin, kv)
        s_query, s_kv, s_up, s_out, grad_x, gains = last_sums(
            xn, hn_t, by_device(att_t), dq, d_up, d_attn, dkv.reshape(n, -1, BLOCK),
            (g_query, g_kv), x, d_res, cos, sin, gain_one_row, gain_two, 4, most,
        )
        s_key, s_value = s_kv[:, :kd], s_kv[:, kd:]
    else:
        got = [lax.all_gather(a, "wide", axis=0, tiled=True) for a in weights]
        g_query, g_kv, g_out, g_gate, g_up, g_down = got
        g_key, g_value = g_kv[:, :kd], g_kv[:, kd:]
        x = x.astype(F32)
        rr1 = lax.rsqrt(jnp.mean(x * x, axis=1, keepdims=True) + EPS)
        xn = (x * rr1 * attn_gain).astype(BF16)
        key_t = turn(dot(g_key, xn, 0, 1), cos, sin).astype(BF16)
        value_t = dot(g_value, xn, 0, 1).astype(BF16)
        own_kv = jnp.concatenate([key_t, value_t]).reshape(2 * kd, micro, nq, BLOCK).transpose(1, 2, 0, 3)
        q_t = (turn(dot(g_query, xn, 0, 1), cos, sin).astype(BF16) * HDIM**-0.5).astype(BF16)
        kv = lax.all_gather(own_kv, "wide", axis=0)
        att_t, lse = attention_fwd(info, where_is, q_t, start, kv)

        res = x + dot(att_t, g_out, 0, 0)
        rr2 = lax.rsqrt(jnp.mean(res * res, axis=1, keepdims=True) + EPS)
        hn = (res * rr2 * ffn_gain).astype(BF16)
        gate, up = dot(hn, g_gate, 1, 0), dot(hn, g_up, 1, 0)
        sg = 1.0 / (1.0 + jnp.exp(-gate))
        hidden = (gate * sg * up).astype(BF16)
        out = (res + dot(hidden, g_down, 1, 0)).astype(BF16)
        d_hidden = dot(ct, g_down, 1, 1)
        d_gate = (d_hidden * up * sg * (1.0 + gate * (1.0 - sg))).astype(BF16)
        d_up = (d_hidden * gate * sg).astype(BF16)
        d_hn = dot(d_gate, g_gate, 1, 1) + dot(d_up, g_up, 1, 1)
        u = d_hn * ffn_gain
        mean = jnp.mean(u * res, axis=1, keepdims=True)
        d_res = ct.astype(F32) + rr2 * u - res * rr2**3 * mean
        gain_two = jnp.sum(d_hn * res * rr2, axis=0)
        d_attn = d_res.astype(BF16)
        do_t = dot(g_out, d_attn, 1, 1).astype(BF16)

        dq, dkv = attention_bwd(info, where_is, q_t, do_t, att_t, lse, start, cos, sin, kv)
        dkv = lax.psum_scatter(dkv, "wide", scatter_dimension=0).transpose(2, 0, 1, 3).reshape(2 * kd, total)
        dk = turn_back(dkv[:kd].astype(F32), cos, sin).astype(BF16)
        dv = dkv[kd:]
        d_xn = dot(dq, g_query, 0, 1) + dot(dk, g_key, 0, 1) + dot(dv, g_value, 0, 1)
        u = d_xn * attn_gain
        grad_x = d_res + rr1 * u - x * rr1**3 * jnp.mean(u * x, axis=1, keepdims=True)
        gain_one = jnp.sum(d_xn * x * rr1, axis=0)
        gains = lax.psum(jnp.stack([gain_one, gain_two]), ("wide", "narrow"))

        def row_part(source, target, ca, cb):
            part = dot(source, target, ca, cb).astype(BF16)
            own = lax.psum_scatter(part, "wide", scatter_dimension=0, tiled=True)
            return row_sum(own, sizes["narrow"])

        s_query, s_key, s_value = row_part(xn, dq, 0, 1), row_part(xn, dk, 0, 1), row_part(xn, dv, 0, 1)
        s_out, s_down = row_part(att_t, d_attn, 1, 0), row_part(hidden, ct, 0, 0)
        s_gate, s_up = row_part(hn, d_gate, 0, 0), row_part(hn, d_up, 0, 0)

    shape = (micro, 1, slots, width)
    wide_out = lambda a: a.astype(F32)
    return (
        out.reshape(shape),
        grad_x.reshape(shape),
        gains[0],
        wide_out(s_query),
        wide_out(s_key),
        wide_out(s_value),
        wide_out(s_out),
        gains[1],
        wide_out(s_gate),
        wide_out(s_up),
        wide_out(s_down),
    )


def solution(mesh):
    by_slot = P(None, "narrow", "wide", None)
    by_row = P(None, "narrow", None)
    split = P("wide", None)
    in_specs = (
        by_slot, by_row, by_row, P(), split, split, split, split, P(), split, split, split, by_slot,
    )
    out_specs = (
        by_slot, by_slot, P(), split, split, split, split, P(), split, split, split,
    )
    return jax.shard_map(
        functools.partial(shards, dict(mesh.shape)),
        mesh=mesh,
        in_specs=in_specs,
        out_specs=out_specs,
        check_vma=False,
    )
```

```python
import functools

import jax
import jax.numpy as jnp
from jax import lax
from jax.experimental import pallas as pl
from jax.experimental.pallas import tpu as pltpu
from jax.sharding import PartitionSpec as P

HDIM = 64
BLOCK = 128
EPS = 1e-05
ROPE_BASE = 100000.0
NEG_FILL = -1e30
F32 = jnp.float32
BF16 = jnp.bfloat16
VMEM_LIMIT = 56 * 1024 * 1024


def dot(a, b, ca, cb):
    return lax.dot_general(a, b, (((ca,), (cb,)), ((), ())), preferred_element_type=F32)


def live_mask(qpos, start, p):
    kpos = p * BLOCK + lax.broadcasted_iota(jnp.int32, (BLOCK, BLOCK), 0)
    return (kpos <= qpos) & (kpos >= start)


STEP = 2


def pick(kv_ref, kvat, mb, qpos, start, b, t, share):
    nq = kv_ref.shape[2]
    blocks = [b - STEP * t - i for i in range(STEP)]
    slots = [kvat[mb, jnp.maximum(p, 0)] for p in blocks]
    at = [(lax.div(s, nq), lax.rem(s, nq)) for s in slots]
    ok = jnp.concatenate([live_mask(qpos, start, p) for p in blocks], axis=0)

    def keys(g):
        rows = slice(g * HDIM, (g + 1) * HDIM)
        return jnp.concatenate([kv_ref[d, 0, s, rows, :] for d, s in at], axis=1)

    return keys, at, jnp.concatenate([ok] * share, axis=1)


def fwd_kernel(groups, share, info, kvat, q_ref, start_ref, kv_ref, o_ref, lse_ref, qs, m_s, l_s, acc, s_s, w_s):
    mb, i = pl.program_id(0), pl.program_id(1)
    lo, b = info[mb, 0, i], info[mb, 1, i]
    nq = kv_ref.shape[2]
    lanes = share * BLOCK
    for g in range(groups):
        for h in range(share):
            at = (g * share + h) * HDIM
            qs[g, :, h * BLOCK : (h + 1) * BLOCK] = q_ref[at : at + HDIM, :]
    m_s[...] = jnp.full_like(m_s, NEG_FILL)
    l_s[...] = jnp.zeros_like(l_s)
    acc[...] = jnp.zeros_like(acc)
    qpos = b * BLOCK + lax.broadcasted_iota(jnp.int32, (1, BLOCK), 1)
    start = start_ref[...]

    def step(t, carry):
        keys, at, ok = pick(kv_ref, kvat, mb, qpos, start, b, t, share)
        for g in range(groups):
            s_s[g] = jnp.where(ok, dot(keys(g), qs[g], 0, 0), NEG_FILL)
        alphas = []
        for g in range(groups):
            s = s_s[g]
            m_old = m_s[g]
            m_new = jnp.maximum(m_old, jnp.max(s, axis=0, keepdims=True))
            w = jnp.exp(s - m_new)
            alpha = jnp.exp(m_old - m_new)
            l_s[g] = l_s[g] * alpha + jnp.sum(w, axis=0, keepdims=True)
            m_s[g] = m_new
            w_s[g] = w.astype(BF16)
            alphas.append(alpha)
        for g in range(groups):
            acc[g] = acc[g] * alphas[g] + dot(keys(groups + g), w_s[g], 1, 0)
        return carry

    lax.fori_loop(0, (b - lo + STEP) // STEP, step, 0)
    for g in range(groups):
        total = l_s[g]
        out = (acc[g] / total).astype(BF16)
        for h in range(share):
            at = (g * share + h) * HDIM
            o_ref[at : at + HDIM, :] = out[:, h * BLOCK : (h + 1) * BLOCK]
        lse_ref[0, g : g + 1, :] = m_s[g] + jnp.log(total)


def attention_fwd(info, kvat, q_t, start, kv):
    width = q_t.shape[0]
    n, micro, nq, kvw, _ = kv.shape
    groups = kvw // HDIM // 2
    share = width // HDIM // groups
    lanes = share * BLOCK
    tok = lambda rows: pl.BlockSpec((rows, BLOCK), lambda m, i, *_: (0, m * nq + i))
    return pl.pallas_call(
        functools.partial(fwd_kernel, groups, share),
        grid_spec=pltpu.PrefetchScalarGridSpec(
            num_scalar_prefetch=2,
            grid=(micro, nq),
            in_specs=[
                tok(width),
                tok(1),
                pl.BlockSpec((n, 1, nq, kvw, BLOCK), lambda m, i, *_: (0, m, 0, 0, 0)),
            ],
            out_specs=[
                tok(width),
                pl.BlockSpec((1, groups, lanes), lambda m, i, *_: (m * nq + i, 0, 0)),
            ],
            scratch_shapes=[
                pltpu.VMEM((groups, HDIM, lanes), BF16),
                pltpu.VMEM((groups, 1, lanes), F32),
                pltpu.VMEM((groups, 1, lanes), F32),
                pltpu.VMEM((groups, HDIM, lanes), F32),
                pltpu.VMEM((groups, STEP * BLOCK, lanes), F32),
                pltpu.VMEM((groups, STEP * BLOCK, lanes), BF16),
            ],
        ),
        out_shape=[
            jax.ShapeDtypeStruct(q_t.shape, BF16),
            jax.ShapeDtypeStruct((micro * nq, groups, lanes), F32),
        ],
        compiler_params=pltpu.CompilerParams(vmem_limit_bytes=VMEM_LIMIT),
        cost_estimate=pl.CostEstimate(
            flops=int(1e10), bytes_accessed=int(8e6), transcendentals=int(8e6)
        ),
        name="attention_fwd",
    )(info, kvat, q_t, start, kv)


def bwd_kernel(
    groups, share, info, kvat, q_ref, do_ref, o_ref, lse_ref, start_ref, cos_ref, sin_ref, kv_ref,
    dq_ref, dkv_ref, qs, dos, delta, dq, dkv, s_s, d_s, w_s, ds_s,
):
    mb, i = pl.program_id(0), pl.program_id(1)
    lo, b = info[mb, 0, i], info[mb, 1, i]
    nq = kv_ref.shape[2]

    @pl.when(i == 0)
    def _():
        dkv[...] = jnp.zeros_like(dkv)

    for g in range(groups):
        for h in range(share):
            at = (g * share + h) * HDIM
            cols = slice(h * BLOCK, (h + 1) * BLOCK)
            d_out = do_ref[at : at + HDIM, :]
            qs[g, :, cols] = q_ref[at : at + HDIM, :]
            dos[g, :, cols] = d_out
            delta[g, :, cols] = jnp.sum(
                d_out.astype(F32) * o_ref[at : at + HDIM, :].astype(F32), axis=0, keepdims=True
            )
    dq[...] = jnp.zeros_like(dq)
    qpos = b * BLOCK + lax.broadcasted_iota(jnp.int32, (1, BLOCK), 1)
    start = start_ref[...]

    def step(t, carry):
        keys, at, ok = pick(kv_ref, kvat, mb, qpos, start, b, t, share)
        for g in range(groups):
            s_s[g] = jnp.where(ok, dot(keys(g), qs[g], 0, 0), NEG_FILL)
            d_s[g] = dot(keys(groups + g), dos[g], 0, 0)
        for g in range(groups):
            w = jnp.exp(s_s[g] - lse_ref[0, g : g + 1, :])
            w_s[g] = w.astype(BF16)
            ds_s[g] = (w * (d_s[g] - delta[g])).astype(BF16)
        for g in range(groups):
            dq[g] += dot(keys(g), ds_s[g], 1, 0)
            dk = dot(qs[g], ds_s[g], 1, 1)
            dv = dot(dos[g], w_s[g], 1, 1)
            krows = slice(g * HDIM, (g + 1) * HDIM)
            vrows = slice((groups + g) * HDIM, (groups + g + 1) * HDIM)
            for i in range(STEP):
                cols = slice(i * BLOCK, (i + 1) * BLOCK)
                dkv[at[i][0], at[i][1], krows, :] += dk[:, cols]
                dkv[at[i][0], at[i][1], vrows, :] += dv[:, cols]
        return carry

    lax.fori_loop(0, (b - lo + STEP) // STEP, step, 0)
    cos, sin = cos_ref[...], sin_ref[...]
    half = HDIM // 2
    for g in range(groups):
        for h in range(share):
            at = (g * share + h) * HDIM
            one = dq[g, :half, h * BLOCK : (h + 1) * BLOCK] * HDIM**-0.5
            two = dq[g, half:, h * BLOCK : (h + 1) * BLOCK] * HDIM**-0.5
            dq_ref[at : at + half, :] = (one * cos + two * sin).astype(BF16)
            dq_ref[at + half : at + HDIM, :] = (two * cos - one * sin).astype(BF16)

    @pl.when(i == nq - 1)
    def _():
        dkv_ref[:, 0] = dkv[...].astype(BF16)


def attention_bwd(info, kvat, q_t, do_t, o_t, lse, start, cos_t, sin_t, kv):
    width = q_t.shape[0]
    n, micro, nq, kvw, _ = kv.shape
    groups = kvw // HDIM // 2
    share = width // HDIM // groups
    lanes = share * BLOCK
    tok = lambda rows: pl.BlockSpec((rows, BLOCK), lambda m, i, *_: (0, m * nq + i))
    keys = pl.BlockSpec((n, 1, nq, kvw, BLOCK), lambda m, i, *_: (0, m, 0, 0, 0))
    return pl.pallas_call(
        functools.partial(bwd_kernel, groups, share),
        grid_spec=pltpu.PrefetchScalarGridSpec(
            num_scalar_prefetch=2,
            grid=(micro, nq),
            in_specs=[
                tok(width),
                tok(width),
                tok(width),
                pl.BlockSpec((1, groups, lanes), lambda m, i, *_: (m * nq + i, 0, 0)),
                tok(1),
                tok(HDIM // 2),
                tok(HDIM // 2),
                keys,
            ],
            out_specs=[tok(width), keys],
            scratch_shapes=[
                pltpu.VMEM((groups, HDIM, lanes), BF16),
                pltpu.VMEM((groups, HDIM, lanes), BF16),
                pltpu.VMEM((groups, 1, lanes), F32),
                pltpu.VMEM((groups, HDIM, lanes), F32),
                pltpu.VMEM((n, nq, kvw, BLOCK), F32),
                pltpu.VMEM((groups, STEP * BLOCK, lanes), F32),
                pltpu.VMEM((groups, STEP * BLOCK, lanes), F32),
                pltpu.VMEM((groups, STEP * BLOCK, lanes), BF16),
                pltpu.VMEM((groups, STEP * BLOCK, lanes), BF16),
            ],
        ),
        out_shape=[
            jax.ShapeDtypeStruct(q_t.shape, BF16),
            jax.ShapeDtypeStruct(kv.shape, BF16),
        ],
        compiler_params=pltpu.CompilerParams(vmem_limit_bytes=VMEM_LIMIT),
        cost_estimate=pl.CostEstimate(
            flops=int(2e10), bytes_accessed=int(16e6), transcendentals=int(8e6)
        ),
        name="attention_bwd",
    )(info, kvat, q_t, do_t, o_t, lse, start, cos_t, sin_t, kv)


CORE, ALONG_X, ALONG_Y = 1, 2, 4
FAR = ALONG_X + ALONG_Y
CUBE = 8
LAG = 2
LAGS = 2
SEM = pltpu.SemaphoreType.DMA


def meet(peers):
    barrier = pltpu.get_barrier_semaphore()
    for peer in peers:
        pl.semaphore_signal(barrier, inc=1, device_id=peer, device_id_type=pl.DeviceIdType.MESH)
    pl.semaphore_wait(barrier, len(peers))


def weight_chunks(shapes, most=160 * 1024):
    chunks = []
    for a, (rows, cols) in enumerate(shapes):
        n = 1
        while rows * cols // n > most and rows % (32 * n) == 0:
            n *= 2
        k = 1
        while rows // n * cols // k > most and cols % (256 * k) == 0:
            k *= 2
        for i in range(n):
            lo, hi = rows // n * i, rows // n * (i + 1)
            mid = lo + -(-(hi - lo) // 32) * 16
            for j in range(k):
                c = pl.ds(cols // k * j, cols // k)
                chunks.append((a, (pl.ds(lo, mid - lo), c), (pl.ds(mid, hi - mid), c)))
    return chunks


def pieces_of(total, size):
    return [(lo, min(size, total - lo)) for lo in range(0, total, size)]


def start_kernel(chunks, micro, *refs):
    refs = list(refs)
    take_refs = lambda n: [refs.pop(0) for _ in range(n)]
    ins = take_refs(6)
    far_x, far_ct, gain_ref, cos_ref, sin_ref = take_refs(5)
    outs = take_refs(6)
    far_q, far_xn, far_kv, far_x_tok, far_ct_tok = take_refs(5)
    near_w = take_refs(2)
    x, ct, x_tok, ct_tok, xn, q_s, own_kv, sent, came, local = take_refs(10)
    at, row = lax.axis_index("wide"), lax.axis_index("narrow")
    peer = {bit: (at ^ bit, row) for bit in (CORE, ALONG_X, ALONG_Y)}
    peer["row"] = (at, row ^ 1)
    keys = len(ins)
    source = [*ins, own_kv]
    land = [*near_w, *outs[2:], far_kv]
    n = len(chunks)
    kd = own_kv.shape[2] // 2
    nq = own_kv.shape[1]
    width, half = q_s.shape[0], HDIM // 2

    mine_in = [pltpu.make_async_copy(ins[i], near_w[i].at[at], local.at[i]) for i in range(2)]
    give = [pltpu.make_async_copy(near_w[i], outs[i], local.at[2 + i]) for i in range(2)]
    give_q = pltpu.make_async_copy(q_s, far_q, local.at[4])
    give_xn = pltpu.make_async_copy(xn, far_xn, local.at[5])
    give_kv = pltpu.make_async_copy(own_kv, far_kv.at[at], local.at[6])
    give_x = pltpu.make_async_copy(x_tok, far_x_tok, local.at[7])
    give_ct = pltpu.make_async_copy(ct_tok, far_ct_tok, local.at[8])
    each = x.shape[2] // micro
    halves_of = lambda far, near, first: [
        pltpu.make_async_copy(far.at[m], near.at[:, :, pl.ds(m * each, each)], local.at[first + m])
        for m in range(micro)
    ]
    x_in, ct_in = halves_of(far_x, x, 9), halves_of(far_ct, ct, 9 + micro)

    def norm():
        for r in x_in:
            r.wait()
        count, high, tokens = x.shape
        square = jnp.zeros((1, tokens), F32)
        for j in range(count):
            v = x[j].astype(F32)
            square += jnp.sum(v * v, axis=0, keepdims=True)
        rr = lax.rsqrt(square / width + EPS)
        gain = jnp.broadcast_to(gain_ref[...], (BLOCK, width)).T
        for j in range(count):
            xn[j] = (x[j].astype(F32) * rr * gain[j * high : (j + 1) * high, 0:1]).astype(BF16)
        give_xn.start()

    def by_token(near, tok, copies, out):
        for r in copies:
            r.wait()
        for lo in range(0, tok.shape[0], BLOCK):
            tok[lo : lo + BLOCK, :] = near[:, :, lo : lo + BLOCK].astype(F32).reshape(width, BLOCK).T.astype(BF16)
        out.start()

    def turned(w, lo, size):
        return sum(dot(w[j, :, lo : lo + size], xn[j], 0, 0) for j in range(w.shape[0]))

    def heads(got):
        cos, sin = cos_ref[...], sin_ref[...]
        for h in range(0, got.shape[0], HDIM):
            one, two = got[h : h + half], got[h + half : h + HDIM]
            yield h, one * cos - two * sin
            yield h + half, two * cos + one * sin

    def to_keys(at_row, value):
        value = value.astype(BF16)
        for m in range(micro):
            for i in range(nq):
                lanes = slice((m * nq + i) * BLOCK, (m * nq + i + 1) * BLOCK)
                own_kv[m, i, at_row : at_row + value.shape[0], :] = value[:, lanes]

    def key_tile(lo, size):
        got = turned(near_w[1], lo, size)
        turn_to = max(0, min(kd - lo, size))
        for h, v in heads(got[:turn_to]):
            to_keys(lo + h, v)
        if turn_to < size:
            to_keys(lo + turn_to, got[turn_to:])

    def query_tile(lo, size):
        for h, v in heads(turned(near_w[0], lo, size)):
            q_s[lo + h : lo + h + half, :] = v.astype(BF16) * HDIM**-0.5

    def run(mine):
        other = 1 - mine
        used = [0] * n
        begun = []

        def part(ref, c, which):
            return ref.at[chunks[c][1 + which]]

        def copy(c, m, which, way, slot):
            a = chunks[c][0]
            there = part(land[a].at[at ^ m], c, which)
            return pltpu.make_async_remote_copy(
                src_ref=there if m else part(source[a], c, which),
                dst_ref=there,
                send_sem=sent.at[c, slot],
                recv_sem=came.at[c, m if way == "row" else m ^ way, which],
                device_id=peer[way],
                device_id_type=pl.DeviceIdType.MESH,
            )

        def push(c, m, which, way):
            r = copy(c, m, which, way, used[c])
            used[c] += 1
            r.start()
            begun.append(r)

        def take(c, m, which, *ways):
            copy(c, m ^ CORE, which, CORE, 0).wait_recv()
            for way in ways:
                push(c, m, which, way)

        planes = [c[0] != keys for c in chunks]
        bounced = [1 < c[0] < keys for c in chunks]
        lean = [planes[c] and c % 2 == 1 for c in range(n)]

        def first(c):
            push(c, 0, mine, ALONG_X)
            push(c, 0, mine, ALONG_Y)
            if not planes[c]:
                push(c, 0, other, ALONG_X)
                push(c, 0, other, ALONG_Y)

        def second(c):
            if lean[c]:
                over_x = c % 4 == 1
                take(c, ALONG_Y, mine, *((ALONG_X,) if over_x else ()), "row", CORE)
                take(c, ALONG_X, mine, *(() if over_x else (ALONG_Y,)), "row", CORE)
            elif planes[c]:
                take(c, ALONG_Y, mine, ALONG_X, CORE)
                push(c, 0, other, ALONG_Y)
                take(c, ALONG_X, mine, "row", CORE)
            else:
                take(c, ALONG_X, mine, ALONG_Y, CORE)
                take(c, ALONG_Y, other, ALONG_X, CORE)
                take(c, ALONG_Y, mine, CORE)
                take(c, ALONG_X, other, CORE)
            push(c, 0, 0, CORE)
            push(c, 0, 1, CORE)

        def third(c):
            take(c, FAR, mine, *(("row", CORE) if planes[c] else (CORE,)))
            if planes[c]:
                take(c, ALONG_Y, other, CORE)
                take(c, ALONG_X, other, CORE)
            else:
                take(c, FAR, other, CORE)

        def fourth(c):
            if planes[c]:
                take(c, FAR, other, CORE)

        def fifth(c):
            for which in range(2):
                take(c, CORE, which, *((CORE,) if bounced[c] else ()))
            for m in (ALONG_X, ALONG_Y, FAR):
                for which in range(2):
                    take(c, m + CORE, which)

        def sixth(c):
            if bounced[c]:
                for which in range(2):
                    take(c, 0, which)

        steps = (first, second, third, fourth, fifth, sixth)
        begins, ready = [], 0
        for c in range(n):
            begins.append(c)
            if chunks[c][0] < 2:
                ready = c + LAG * 4
            if chunks[c][0] == keys:
                begins[c] = max(begins[c - 1] + 1, ready + 1)
        work = {1: [norm], ready: []}
        work[2] = [functools.partial(by_token, x, x_tok, (), give_x)]
        work[3] = [functools.partial(by_token, ct, ct_tok, ct_in, give_ct)]
        for lo, size in pieces_of(2 * kd, 256):
            work[ready].append(functools.partial(key_tile, lo, size))
        work[ready].append(give_kv.start)
        for i, (lo, size) in enumerate(pieces_of(width, 256)):
            work[ready + 2 + i] = [functools.partial(query_tile, lo, size)]
        for t in range(begins[-1] + LAG * (len(steps) - 1) + 1):
            for s, step in enumerate(steps):
                for c in range(n):
                    if begins[c] + LAG * s == t:
                        step(c)
            if t == ready:
                for r in mine_in:
                    r.wait()
                for r in give:
                    r.start()
            for job in work.get(t, ()):
                job()
        for r in begun:
            r.wait_send()

    for r in (*x_in, *mine_in, *ct_in):
        r.start()
    meet(list(peer.values()))
    for mine in range(2):
        pl.when(row % 2 == mine)(functools.partial(run, mine))
    give_q.start()
    for r in (*give, give_q, give_xn, give_kv, give_x, give_ct):
        r.wait()


def start_of(weights, x, ct, gain, cos, sin, collective_id):
    micro, count, high, each = x.shape
    tokens, width = micro * each, count * high
    kd = weights[1].shape[1] // 2
    nq = each // BLOCK
    chunks = weight_chunks([a.shape for a in weights])
    keys = len(weights)
    for m in range(micro):
        for i in range(2):
            rows = pl.ds(kd * i, kd)
            halves = [(m, pl.ds(nq // 2 * h, nq // 2), rows) for h in range(2)]
            chunks.append((keys, *halves))
    anywhere = pl.BlockSpec(memory_space=pl.ANY)
    vmem = pl.BlockSpec(memory_space=pltpu.VMEM)
    shape = jax.ShapeDtypeStruct
    kv = (micro, nq, 2 * kd, BLOCK)
    split = pltpu.VMEM((count, high, tokens), BF16)
    by_token = pltpu.VMEM((tokens, width), BF16)
    got = pl.pallas_call(
        functools.partial(start_kernel, chunks, micro),
        in_specs=[anywhere] * (keys + 2) + [vmem] * 3,
        out_specs=[anywhere] * (keys + 5),
        out_shape=[shape((count,) + a.shape, BF16) for a in weights]
        + [shape((width, tokens), BF16), shape((count, high, tokens), BF16), shape((count,) + kv, BF16)]
        + [shape((tokens, width), BF16)] * 2,
        scratch_shapes=[pltpu.VMEM((count,) + a.shape, BF16) for a in weights[:2]]
        + [split, split, by_token, by_token, split, pltpu.VMEM((width, tokens), BF16), pltpu.VMEM(kv, BF16)]
        + [SEM((len(chunks), 16)), SEM((len(chunks), 8, 2)), SEM((9 + 2 * micro,))],
        compiler_params=pltpu.CompilerParams(
            collective_id=collective_id, has_side_effects=True, vmem_limit_bytes=VMEM_LIMIT
        ),
        name="gather_and_project",
    )(*weights, x, ct, gain, cos, sin)
    return got[:keys], *got[keys:]


class Unit:
    def __init__(self, source, target, out, rows, cols, first):
        self.source, self.target, self.out = source, target, out
        self.rows, self.cols, self.first = rows, cols, first

    @property
    def shape(self):
        return (self.rows[1], self.cols[1])


def weight_units(sizes, most, units=()):
    units = list(units)
    for source, target, out, rows, cols in sizes:
        k = 1
        while cols % (256 * k) == 0 and rows * cols // k > most:
            k *= 2
        high = -(-rows // max(1, round(rows * cols / k / most)) // 16) * 16
        cols_cuts = pieces_of(cols, cols // k)
        if out == sizes[-1][2] and cols % BLOCK == 0:
            lo, size = cols_cuts.pop()
            while size > BLOCK:
                part = -(-size // (2 * BLOCK)) * BLOCK
                cols_cuts.append((lo, part))
                lo, size = lo + part, size - part
            cols_cuts.append((lo, size))
        for rows_cut in pieces_of(rows, high):
            for cols_cut in cols_cuts:
                first = (ALONG_X, ALONG_Y)[len(units) % 2]
                units.append(Unit(source, target, out, rows_cut, cols_cut, first))
    return units


RING = 3


def ring_sizes(units):
    shapes = [u.shape for u in units if u.source is not None]
    return {a: min(RING, shapes.count(a)) for a in shapes}


def sum_scratch(units, tokens):
    n = len(units)
    room = lambda *lead: [pltpu.VMEM(lead + u.shape, BF16) for u in units]
    line = [pltpu.VMEM((2,) + u.shape if u.source is not None else (8, BLOCK), BF16) for u in units]
    rows = max(u.shape[0] for u in units if u.source is not None)
    scratch = room(4) + room(4) + room(2) + room() + line
    scratch += [pltpu.VMEM((8 * rows, tokens), BF16)]
    scratch += [pltpu.VMEM((d, 4) + a, BF16) for a, d in ring_sizes(units).items()]
    return scratch + [SEM((n, 5)), SEM((n, 5)), SEM((n,)), SEM((n, 4)), SEM((n, 4)), SEM((n, 4))]


class Sums:
    def __init__(self, units, take, outs, source, product, far_keys=None, keys_done=None):
        n = len(units)
        self.units, self.outs, self.source, self.product = units, outs, source, product
        self.far_keys, self.keys_done = far_keys, keys_done
        self.held, self.core_in, self.one_in, self.two_in, self.line_in = (take(n) for _ in range(5))
        self.lhs = take(1)[0]
        self.depth = ring_sizes(units)
        self.rings = dict(zip(self.depth, take(len(self.depth))))
        self.sent, self.came, self.stored, self.key_load, self.key_sent, self.key_came = take(6)
        self.at, self.row = lax.axis_index("wide"), lax.axis_index("narrow")
        self.way = {bit: (self.at ^ bit, self.row) for bit in (CORE, ALONG_X, ALONG_Y)}
        self.near, self.across = (self.at, self.row ^ 1), (self.at, self.row ^ 3)
        self.middle = (self.row == 1) | (self.row == 2)
        self.is_keys = [u.source is None for u in units]
        self.steps = (self.s0, self.s1, self.s2, self.s3, self.s4, self.s5, self.s6)

    def meet(self):
        meet([*self.way.values(), self.near, self.across])

    def send(self, c, slot, a, b, to):
        return pltpu.make_async_remote_copy(
            src_ref=a, dst_ref=b, send_sem=self.sent.at[c, slot], recv_sem=self.came.at[c, slot],
            device_id=to, device_id_type=pl.DeviceIdType.MESH,
        )

    @staticmethod
    def add(dst, other):
        dst[...] = dst[...] + other[...]

    def order(self, c):
        first = self.units[c].first
        return (0, FAR - first, first, FAR)

    def slot_of(self, c):
        shape = self.units[c].shape
        alike = [i for i, u in enumerate(self.units) if u.source is not None and u.shape == shape]
        return alike.index(c) % self.depth[shape]

    def same_slot(self, i, c):
        if self.is_keys[i] or self.is_keys[c] or self.units[i].shape != self.units[c].shape:
            return False
        return self.slot_of(i) == self.slot_of(c)

    def core_copies(self, c):
        u = self.units[c]
        if not self.is_keys[c]:
            return [self.send(c, 0, self.rings[u.shape].at[self.slot_of(c)], self.core_in[c], self.way[CORE])]
        return [
            pltpu.make_async_remote_copy(
                src_ref=self.far_keys.at[self.at ^ CORE ^ m, pl.ds(*u.rows)], dst_ref=self.core_in[c].at[i],
                send_sem=self.key_sent.at[c, i], recv_sem=self.key_came.at[c, i],
                device_id=self.way[CORE], device_id_type=pl.DeviceIdType.MESH,
            )
            for i, m in enumerate(self.order(c))
        ]

    def key_loads(self, c):
        rows = pl.ds(*self.units[c].rows)
        return [
            pltpu.make_async_copy(self.far_keys.at[self.at ^ m, rows], self.held[c].at[i], self.key_load.at[c, i])
            for i, m in enumerate(self.order(c))
        ]

    def first_copy(self, c):
        return self.send(c, 1, self.held[c].at[pl.ds(2, 2)], self.one_in[c], self.way[self.units[c].first])

    def second_copy(self, c):
        return self.send(c, 2, self.held[c].at[1], self.two_in[c], self.way[FAR - self.units[c].first])

    def inward(self, c):
        return self.send(c, 3, self.held[c].at[0], self.line_in[c].at[0], self.near)

    def over(self, c):
        return self.send(c, 4, self.held[c].at[0], self.line_in[c].at[1], self.across)

    def outward(self, c):
        return self.send(c, 3, self.line_in[c].at[1], self.line_in[c].at[0], self.near)

    def store(self, c, slot):
        u = self.units[c]
        cut = (pl.ds(*u.rows), pl.ds(*u.cols))
        return pltpu.make_async_copy(self.line_in[c].at[slot], self.outs[u.out].at[cut], self.stored.at[c])

    def products(self, c):
        u = self.units[c]
        rows, cols = u.shape
        for i, core in enumerate((CORE, 0)):
            for k, m in enumerate(self.order(c)):
                self.lhs[pl.ds((4 * i + k) * rows, rows), :] = self.source(u, self.at ^ m ^ core)
        a = self.lhs[pl.ds(0, 8 * rows), :]
        for lo, size in pieces_of(cols, 256):
            got = self.product(u, a, u.cols[0] + lo, size).astype(BF16).reshape(8, rows, size)
            self.rings[u.shape][self.slot_of(c), :, :, lo : lo + size] = got[:4]
            self.held[c][:, :, lo : lo + size] = got[4:]

    def s0(self, c):
        if self.is_keys[c]:
            for r in self.core_copies(c) + self.key_loads(c):
                r.start()
            return
        before = [i for i in range(c) if self.same_slot(i, c)]
        if before:
            self.core_copies(before[-1])[0].wait_send()
        self.products(c)
        self.core_copies(c)[0].start()

    def s1(self, c):
        if self.is_keys[c]:
            for r in self.key_loads(c):
                r.wait()
        for r in self.core_copies(c):
            r.wait_recv()
        for i in (2, 3, 0, 1):
            self.add(self.held[c].at[i], self.core_in[c].at[i])
            if i == 3:
                self.first_copy(c).start()

    def s2(self, c):
        self.first_copy(c).wait_recv()
        self.add(self.held[c].at[1], self.one_in[c].at[1])
        self.second_copy(c).start()
        self.add(self.held[c].at[0], self.one_in[c].at[0])

    def s3(self, c):
        self.second_copy(c).wait_recv()
        self.add(self.held[c].at[0], self.two_in[c])
        if self.is_keys[c]:
            self.keys_done(c, self.held[c].at[0])
        else:
            pl.when(~self.middle)(lambda: self.inward(c).start())

    def s4(self, c):
        @pl.when(self.middle)
        def _():
            self.inward(c).wait_recv()
            self.add(self.held[c].at[0], self.line_in[c].at[0])
            self.over(c).start()

    def s5(self, c):
        @pl.when(self.middle)
        def _():
            self.over(c).wait_recv()
            self.add(self.line_in[c].at[1], self.held[c].at[0])
            self.outward(c).start()
            self.store(c, 1).start()

    def s6(self, c):
        @pl.when(~self.middle)
        def _():
            self.outward(c).wait_recv()
            self.store(c, 0).start()

    def finish(self):
        n = len(self.units)
        for c in range(n):
            if not any(self.same_slot(c, i) for i in range(c + 1, n)):
                for r in self.core_copies(c):
                    r.wait_send()
            self.first_copy(c).wait_send()
            self.second_copy(c).wait_send()
            if not self.is_keys[c]:
                self.inward(c).wait_send()
                pl.when(self.middle)(lambda: self.over(c).wait_send())
                self.store(c, 0).wait()

    def run(self, begins, work):
        last = max(b + LAGS * (len(self.steps) - 1) for b in begins)
        for t in range(max([last, *work]) + 1):
            for s, step in enumerate(self.steps):
                for c, b in enumerate(begins):
                    if b + LAGS * s == t and not (self.is_keys[c] and s > 3):
                        step(c)
            for job in work.get(t, ()):
                job()


TILE = 256


def ffn_kernel(units, *refs):
    refs = list(refs)
    take = lambda n: [refs.pop(0) for _ in range(n)]
    far_att, far_x, far_ct, far_out_w, far_gate_w, far_up_w, far_down_w, gain_ref = take(8)
    far_out, far_res, far_do, far_hn, far_d_up, far_d_attn, gain_sum = take(7)
    outs = take(2)
    att, x, ct, out_w, wg, wu, wd, res, hn, hn_t, hid_t, d_gate, d_up, out_acc, hn_acc = take(15)
    load, give = take(2)
    do, d_attn = att, hn
    width, tokens = att.shape
    ff = hid_t.shape[0]
    tiles = ff // TILE
    slots = range(0, tokens, BLOCK)
    loads = [
        pltpu.make_async_copy(a, b, load.at[i])
        for i, (a, b) in enumerate(
            zip(
                (far_att, far_out_w, far_x, far_gate_w, far_up_w, far_down_w, far_ct),
                (att, out_w, x, wg, wu, wd, ct),
            )
        )
    ]
    gives = [
        pltpu.make_async_copy(a, b, give.at[i])
        for i, (a, b) in enumerate(
            ((x, far_out), (res, far_res), (do, far_do), (hn_t, far_hn), (d_up, far_d_up), (d_attn, far_d_attn))
        )
    ]

    def attend():
        for r in loads[:3]:
            r.wait()
        for lo in slots:
            cut = slice(lo, lo + BLOCK)
            r = x[cut, :].astype(F32) + dot(att[:, cut], out_w[...], 0, 0)
            res[cut, :] = r
            rr = lax.rsqrt(jnp.mean(r * r, axis=1, keepdims=True) + EPS)
            h = r * rr * gain_ref[...]
            hn[cut, :] = h.astype(BF16)
            h = h.T
            high = hn_t.shape[1]
            for j in range(hn_t.shape[0]):
                hn_t[j, :, cut] = h[j * high : (j + 1) * high].astype(BF16)
        gives[3].start()

    def hidden_tile(i):
        cut = slice(i * TILE, (i + 1) * TILE)
        gate, up = dot(hn[...], wg[:, cut], 1, 0), dot(hn[...], wu[:, cut], 1, 0)
        hidden = (gate / (1.0 + jnp.exp(-gate)) * up).astype(BF16)
        hid_t[cut, :] = hidden.T

    def back_tile(i):
        cut = slice(i * TILE, (i + 1) * TILE)
        gate, up = dot(hn[...], wg[:, cut], 1, 0), dot(hn[...], wu[:, cut], 1, 0)
        sg = 1.0 / (1.0 + jnp.exp(-gate))
        act = gate * sg
        hidden = (act * up).astype(BF16)
        d_hidden = dot(ct[...], wd[cut, :], 1, 1)
        d_gate[:, cut] = (d_hidden * up * sg * (1.0 + gate * (1.0 - sg))).astype(BF16)
        d_up[:, cut] = (d_hidden * act).astype(BF16)
        forward = dot(hidden, wd[cut, :], 1, 0)
        back = dot(d_gate[:, cut], wg[:, cut], 1, 1) + dot(d_up[:, cut], wu[:, cut], 1, 1)
        if i == 0:
            out_acc[...] = forward
            hn_acc[...] = back
        else:
            out_acc[...] += forward
            hn_acc[...] += back

    def residual():
        gives[4].start()
        total = jnp.zeros(gain_sum.shape, F32)
        for lo in slots:
            cut = slice(lo, lo + BLOCK)
            r, d = res[cut, :], hn_acc[cut, :]
            rr = lax.rsqrt(jnp.mean(r * r, axis=1, keepdims=True) + EPS)
            total += jnp.sum(d * r * rr, axis=0, keepdims=True)
            u = d * gain_ref[...]
            x[cut, :] = (r + out_acc[cut, :]).astype(BF16)
            mean = jnp.mean(u * r, axis=1, keepdims=True)
            d = ct[cut, :].astype(F32) + rr * u - r * (rr * rr * rr * mean)
            res[cut, :] = d
            d_attn[cut, :] = d.astype(BF16)
            do[:, cut] = dot(out_w[...], d_attn[cut, :], 1, 1).astype(BF16)
        gain_sum[...] = total
        for i in (0, 1, 2, 5):
            gives[i].start()

    def source(u, device):
        lo, size = u.rows
        if u.source == 0:
            per = ff // CUBE
            return hid_t[pl.ds(pl.multiple_of(device * per + lo, 16), size), :]
        return hn_t[device, pl.ds(lo, size), :]

    def product(u, a, lo, size):
        b = ct if u.target == 0 else d_gate
        return dot(a, b[:, pl.ds(lo, size)], 1, 0)

    sums = Sums(units, take, outs, source, product)
    for r in loads:
        r.start()
    sums.meet()
    attend()
    for r in loads[3:5]:
        r.wait()
    for i in range(tiles):
        hidden_tile(i)
    for r in loads[5:]:
        r.wait()
    downs = sum(u.source == 0 for u in units)
    spread = max(1, downs)
    work = {}
    for i in range(tiles):
        work.setdefault(i * spread // tiles, []).append(functools.partial(back_tile, i))
    work.setdefault(spread + 1, []).append(residual)
    begins = [c if c < downs else c for c in range(len(units))]
    sums.run(begins, work)
    sums.finish()
    for r in gives:
        r.wait()


def ffn(att_t, x, ct, g_out, g_gate, g_up, g_down, gain, collective_id, most):
    width, tokens = att_t.shape
    ff = g_gate.shape[1]
    high = width // CUBE
    units = weight_units([(0, 0, 0, ff // CUBE, width), (1, 1, 1, high, ff)], most)
    anywhere = pl.BlockSpec(memory_space=pl.ANY)
    vmem = pl.BlockSpec(memory_space=pltpu.VMEM)
    shape = jax.ShapeDtypeStruct
    by_token, by_width = (tokens, width), (width, tokens)
    return pl.pallas_call(
        functools.partial(ffn_kernel, units),
        in_specs=[anywhere] * 7 + [vmem],
        out_specs=[anywhere] * 6 + [vmem] + [anywhere] * 2,
        out_shape=[
            shape(by_token, BF16), shape(by_token, F32), shape(by_width, BF16),
            shape((CUBE, high, tokens), BF16), shape((tokens, ff), BF16), shape(by_token, BF16),
            shape((1, width), F32), shape((ff // CUBE, width), BF16), shape((high, ff), BF16),
        ],
        scratch_shapes=[
            pltpu.VMEM(by_width, BF16), pltpu.VMEM(by_token, BF16), pltpu.VMEM(by_token, BF16),
            pltpu.VMEM((width, width), BF16), pltpu.VMEM((width, ff), BF16),
            pltpu.VMEM((width, ff), BF16), pltpu.VMEM((ff, width), BF16),
            pltpu.VMEM(by_token, F32), pltpu.VMEM(by_token, BF16),
            pltpu.VMEM((CUBE, high, tokens), BF16), pltpu.VMEM((ff, tokens), BF16),
            pltpu.VMEM((tokens, ff), BF16), pltpu.VMEM((tokens, ff), BF16),
            pltpu.VMEM(by_token, F32), pltpu.VMEM(by_token, F32), SEM((7,)), SEM((6,)),
        ] + sum_scratch(units, tokens),
        compiler_params=pltpu.CompilerParams(
            collective_id=collective_id, has_side_effects=True, vmem_limit_bytes=62 * 1024 * 1024
        ),
        name="feed_forward",
    )(att_t, x, ct, g_out, g_gate, g_up, g_down, gain)


def last_kernel(units, *refs):
    refs = list(refs)
    take = lambda n: [refs.pop(0) for _ in range(n)]
    far = take(6)
    far_keys, far_w, far_x, far_res = *take(1), take(2), *take(2)
    cos_ref, sin_ref, gain_ref, gain_two = take(4)
    outs = take(4)
    far_grad, total = take(2)
    near = take(6)
    xn_t, hn_t, att, dq, d_up, d_attn = near
    dkv, w, x, res, gain_buf = *take(1), take(2), *take(3)
    load, tail_load, gain_sent, gain_came = take(4)
    kd, tokens = dkv.shape[0] // 2, dkv.shape[1]
    loads = [pltpu.make_async_copy(a, b, load.at[i]) for i, (a, b) in enumerate(zip(far, near))]
    tail_loads = [
        pltpu.make_async_copy(a, b, tail_load.at[i])
        for i, (a, b) in enumerate(zip([*far_w, far_x, far_res], [*w, x, res]))
    ]
    give = pltpu.make_async_copy(res, far_grad, tail_load.at[len(tail_loads)])
    ready = set()

    def need(copies, i):
        if (copies is loads, i) not in ready:
            ready.add((copies is loads, i))
            copies[i].wait()

    def source(u, device):
        need(loads, u.source)
        return near[u.source][device, pl.ds(*u.rows), :]

    def product(u, a, lo, size):
        if u.target is None:
            return dot(a, dkv[pl.ds(lo, size), :], 1, 1)
        need(loads, u.target)
        if u.target == 3:
            return dot(a, dq[pl.ds(lo, size), :], 1, 1)
        return dot(a, near[u.target][:, pl.ds(lo, size)], 1, 0)

    def keys_done(c, got):
        lanes = slice(c * BLOCK, (c + 1) * BLOCK)
        cs, sn = cos_ref[:, lanes], sin_ref[:, lanes]
        half = HDIM // 2
        for h in range(0, kd, HDIM):
            one = got[h : h + half, :].astype(F32)
            two = got[h + half : h + HDIM, :].astype(F32)
            dkv[h : h + half, lanes] = (one * cs + two * sn).astype(BF16)
            dkv[h + half : h + HDIM, lanes] = (two * cs - one * sn).astype(BF16)
        dkv[kd:, lanes] = got[kd:, :]

    def input_grad():
        need(loads, 3)
        for i in range(len(tail_loads)):
            need(tail_loads, i)
        sum_one = jnp.zeros(gain_two.shape, F32)
        for lo in range(0, tokens, BLOCK):
            cut = slice(lo, lo + BLOCK)
            d = dot(dq[:, cut], w[0][...], 0, 1)
            d += dot(dkv[:, cut], w[1][...], 0, 1)
            v = x[cut, :].astype(F32)
            rr = lax.rsqrt(jnp.mean(v * v, axis=1, keepdims=True) + EPS)
            sum_one += jnp.sum(d * v * rr, axis=0, keepdims=True)
            u = d * gain_ref[...]
            mean = jnp.mean(u * v, axis=1, keepdims=True)
            res[cut, :] = res[cut, :] + rr * u - v * (rr * rr * rr * mean)
        gain_buf[0, 0:1, :] = sum_one
        gain_buf[0, 1:2, :] = gain_two[...]
        give.start()

    sums = Sums(units, take, outs, source, product, far_keys, keys_done)
    gain_ways = [*sums.way.values(), sums.near, sums.across]

    def gain_copy(i):
        return pltpu.make_async_remote_copy(
            src_ref=gain_buf.at[2 * i], dst_ref=gain_buf.at[2 * i + 1], send_sem=gain_sent.at[i],
            recv_sem=gain_came.at[i], device_id=gain_ways[i], device_id_type=pl.DeviceIdType.MESH,
        )

    def gain_step(i):
        if i:
            gain_copy(i - 1).wait_recv()
            gain_buf[2 * i] = gain_buf[2 * i - 2] + gain_buf[2 * i - 1]
        if i < len(gain_ways):
            gain_copy(i).start()

    for r in loads + tail_loads:
        r.start()
    sums.meet()
    begins, after = [], 0
    for c, u in enumerate(units):
        begins.append(c if not begins else begins[-1] + 1)
        if u.source is None:
            after = begins[-1] + 3 * LAGS + 1
        elif u.target is None:
            begins[-1] = max(begins[-1], after)
    work = {after: [input_grad]}
    for i in range(len(gain_ways) + 1):
        work.setdefault(after + i, []).append(functools.partial(gain_step, i))
    sums.run(begins, work)
    total[...] = gain_buf[2 * len(gain_ways)]
    sums.finish()
    for i in range(len(gain_ways)):
        gain_copy(i).wait_send()
    give.wait()


def last_sums(xn_t, hn_t, att_t, dq, d_up, d_attn, keys, weights, x, d_res, cos, sin, gain, gain_two, collective_id, most):
    count, high, tokens = xn_t.shape
    width, ff = count * high, d_up.shape[1]
    rows = keys.shape[1] * BLOCK // tokens
    units = [
        Unit(None, None, None, (rows * i, rows), (0, BLOCK), (ALONG_X, ALONG_Y)[i % 2])
        for i in range(tokens // BLOCK)
    ]
    units = weight_units(
        [(1, 4, 2, high, ff), (2, 5, 3, high, width), (0, 3, 0, high, width), (0, None, 1, high, rows)], most, units
    )
    anywhere = pl.BlockSpec(memory_space=pl.ANY)
    vmem = pl.BlockSpec(memory_space=pltpu.VMEM)
    shape = jax.ShapeDtypeStruct
    near = (xn_t, hn_t, att_t, dq, d_up, d_attn)
    return pl.pallas_call(
        functools.partial(last_kernel, units),
        in_specs=[anywhere] * 11 + [vmem] * 4,
        out_specs=[anywhere] * 5 + [vmem],
        out_shape=[
            shape((high, width), BF16), shape((high, rows), BF16), shape((high, ff), BF16),
            shape((high, width), BF16), shape((tokens, width), F32), shape((2, width), F32),
        ],
        scratch_shapes=[pltpu.VMEM(a.shape, a.dtype) for a in near]
        + [pltpu.VMEM((rows, tokens), BF16)]
        + [pltpu.VMEM(a.shape, a.dtype) for a in (*weights, x, d_res)]
        + [pltpu.VMEM((11, 2, width), F32), SEM((6,)), SEM((6,)), SEM((5,)), SEM((5,))]
        + sum_scratch(units, tokens),
        compiler_params=pltpu.CompilerParams(
            collective_id=collective_id, has_side_effects=True, vmem_limit_bytes=62 * 1024 * 1024
        ),
        name="last_sums",
    )(*near, keys, *weights, x, d_res, cos, sin, gain, gain_two)


def row_sum(part, size):
    if size != 4:
        return lax.psum(part, "narrow")
    add = lambda a, b: (a.astype(F32) + b.astype(F32)).astype(BF16)
    part = add(part, lax.ppermute(part, "narrow", [(0, 1), (3, 2)]))
    part = add(part, lax.ppermute(part, "narrow", [(1, 2), (2, 1)]))
    back = lax.ppermute(part, "narrow", [(1, 0), (2, 3)])
    at = lax.axis_index("narrow")
    return jnp.where((at == 1) | (at == 2), part, back)


def turn(v, cos, sin):
    heads = v.reshape(-1, 2, HDIM // 2, v.shape[1])
    one, two = heads[:, 0], heads[:, 1]
    return jnp.stack([one * cos - two * sin, two * cos + one * sin], axis=1).reshape(v.shape)


def turn_back(v, cos, sin):
    return turn(v, cos, -sin)


def shards(sizes, tokens, lengths, block_plan, attn_gain, w_query, w_key, w_value, w_out, ffn_gain,
           w_gate, w_up, w_down, cotangent):
    n = sizes["wide"]
    at = lax.axis_index("wide")
    micro, _, slots, width = tokens.shape
    total = micro * slots
    kd = w_key.shape[1]
    ff = w_gate.shape[1]
    nq = slots // BLOCK
    nb = nq * n

    plan = block_plan[:, 0]
    sizes_of = lengths[:, 0]
    docs = sizes_of.shape[1]
    upto = jnp.arange(docs)[:, None] >= jnp.arange(docs)[None, :]
    ends = jnp.sum(jnp.where(upto[None], sizes_of[:, None, :], 0), axis=2)
    own_plan = lax.dynamic_slice_in_dim(plan, at * nq, nq, axis=1)
    position = own_plan[:, :, None] * BLOCK + jnp.arange(BLOCK, dtype=jnp.int32)
    start = jnp.sum(
        jnp.where(position[..., None] >= ends[:, None, None, :], sizes_of[:, None, None, :], 0), axis=3
    )
    info = jnp.stack([start[:, :, 0] // BLOCK, own_plan], axis=1)
    slot_block = jnp.arange(nb, dtype=jnp.int32)
    where_is = jnp.sum(
        jnp.where(plan[:, None, :] == slot_block[None, :, None], slot_block[None, None, :], 0), axis=2
    )
    start = start.reshape(1, total)
    local = position.reshape(1, total) - start
    frequency = ROPE_BASE ** (-2.0 * jnp.arange(HDIM // 2, dtype=F32) / HDIM)
    angles = frequency[:, None] * local.astype(F32)
    cos, sin = jnp.cos(angles), jnp.sin(angles)

    cube = n == CUBE and sizes["narrow"] == 4 and nq % 2 == 0

    x = tokens.reshape(total, width)
    ct = cotangent.reshape(total, width)
    most = 64 * 1024
    high = width // n
    w_kv = jnp.concatenate([w_key, w_value], axis=1)
    weights = (w_query, w_kv, w_out, w_gate, w_up, w_down)
    by_device = lambda a: a.reshape(n, -1, a.shape[1])
    gain_one_row, gain_two_row = attn_gain[None], ffn_gain[None]
    if cube:
        by_width = lambda a: a[:, 0].transpose(0, 2, 1).reshape(micro, n, high, slots)
        got, q_t, xn, kv, x, ct = start_of(
            weights, by_width(tokens), by_width(cotangent), gain_one_row, cos, sin, 2
        )
        g_query, g_kv, g_out, g_gate, g_up, g_down = [a.reshape(-1, a.shape[2]) for a in got]
        att_t, lse = attention_fwd(info, where_is, q_t, start, kv)
        out, d_res, do_t, hn_t, d_up, d_attn, gain_two, s_down, s_gate = ffn(
            att_t, x, ct, g_out, g_gate, g_up, g_down, gain_two_row, 3, 44 * 1024
        )
        dq, dkv = attention_bwd(info, where_is, q_t, do_t, att_t, lse, start, cos, sin, kv)
        s_query, s_kv, s_up, s_out, grad_x, gains = last_sums(
            xn, hn_t, by_device(att_t), dq, d_up, d_attn, dkv.reshape(n, -1, BLOCK),
            (g_query, g_kv), x, d_res, cos, sin, gain_one_row, gain_two, 4, most,
        )
        s_key, s_value = s_kv[:, :kd], s_kv[:, kd:]
    else:
        got = [lax.all_gather(a, "wide", axis=0, tiled=True) for a in weights]
        g_query, g_kv, g_out, g_gate, g_up, g_down = got
        g_key, g_value = g_kv[:, :kd], g_kv[:, kd:]
        x = x.astype(F32)
        rr1 = lax.rsqrt(jnp.mean(x * x, axis=1, keepdims=True) + EPS)
        xn = (x * rr1 * attn_gain).astype(BF16)
        key_t = turn(dot(g_key, xn, 0, 1), cos, sin).astype(BF16)
        value_t = dot(g_value, xn, 0, 1).astype(BF16)
        own_kv = jnp.concatenate([key_t, value_t]).reshape(2 * kd, micro, nq, BLOCK).transpose(1, 2, 0, 3)
        q_t = (turn(dot(g_query, xn, 0, 1), cos, sin).astype(BF16) * HDIM**-0.5).astype(BF16)
        kv = lax.all_gather(own_kv, "wide", axis=0)
        att_t, lse = attention_fwd(info, where_is, q_t, start, kv)

        res = x + dot(att_t, g_out, 0, 0)
        rr2 = lax.rsqrt(jnp.mean(res * res, axis=1, keepdims=True) + EPS)
        hn = (res * rr2 * ffn_gain).astype(BF16)
        gate, up = dot(hn, g_gate, 1, 0), dot(hn, g_up, 1, 0)
        sg = 1.0 / (1.0 + jnp.exp(-gate))
        hidden = (gate * sg * up).astype(BF16)
        out = (res + dot(hidden, g_down, 1, 0)).astype(BF16)
        d_hidden = dot(ct, g_down, 1, 1)
        d_gate = (d_hidden * up * sg * (1.0 + gate * (1.0 - sg))).astype(BF16)
        d_up = (d_hidden * gate * sg).astype(BF16)
        d_hn = dot(d_gate, g_gate, 1, 1) + dot(d_up, g_up, 1, 1)
        u = d_hn * ffn_gain
        mean = jnp.mean(u * res, axis=1, keepdims=True)
        d_res = ct.astype(F32) + rr2 * u - res * rr2**3 * mean
        gain_two = jnp.sum(d_hn * res * rr2, axis=0)
        d_attn = d_res.astype(BF16)
        do_t = dot(g_out, d_attn, 1, 1).astype(BF16)

        dq, dkv = attention_bwd(info, where_is, q_t, do_t, att_t, lse, start, cos, sin, kv)
        dkv = lax.psum_scatter(dkv, "wide", scatter_dimension=0).transpose(2, 0, 1, 3).reshape(2 * kd, total)
        dk = turn_back(dkv[:kd].astype(F32), cos, sin).astype(BF16)
        dv = dkv[kd:]
        d_xn = dot(dq, g_query, 0, 1) + dot(dk, g_key, 0, 1) + dot(dv, g_value, 0, 1)
        u = d_xn * attn_gain
        grad_x = d_res + rr1 * u - x * rr1**3 * jnp.mean(u * x, axis=1, keepdims=True)
        gain_one = jnp.sum(d_xn * x * rr1, axis=0)
        gains = lax.psum(jnp.stack([gain_one, gain_two]), ("wide", "narrow"))

        def row_part(source, target, ca, cb):
            part = dot(source, target, ca, cb).astype(BF16)
            own = lax.psum_scatter(part, "wide", scatter_dimension=0, tiled=True)
            return row_sum(own, sizes["narrow"])

        s_query, s_key, s_value = row_part(xn, dq, 0, 1), row_part(xn, dk, 0, 1), row_part(xn, dv, 0, 1)
        s_out, s_down = row_part(att_t, d_attn, 1, 0), row_part(hidden, ct, 0, 0)
        s_gate, s_up = row_part(hn, d_gate, 0, 0), row_part(hn, d_up, 0, 0)

    shape = (micro, 1, slots, width)
    wide_out = lambda a: a.astype(F32)
    return (
        out.reshape(shape),
        grad_x.reshape(shape),
        gains[0],
        wide_out(s_query),
        wide_out(s_key),
        wide_out(s_value),
        wide_out(s_out),
        gains[1],
        wide_out(s_gate),
        wide_out(s_up),
        wide_out(s_down),
    )


def solution(mesh):
    by_slot = P(None, "narrow", "wide", None)
    by_row = P(None, "narrow", None)
    split = P("wide", None)
    in_specs = (
        by_slot, by_row, by_row, P(), split, split, split, split, P(), split, split, split, by_slot,
    )
    out_specs = (
        by_slot, by_slot, P(), split, split, split, split, P(), split, split, split,
    )
    return jax.shard_map(
        functools.partial(shards, dict(mesh.shape)),
        mesh=mesh,
        in_specs=in_specs,
        out_specs=out_specs,
        check_vma=False,
    )
```

```python
import functools

import jax
import jax.numpy as jnp
from jax import lax
from jax.experimental import pallas as pl
from jax.experimental.pallas import tpu as pltpu
from jax.sharding import PartitionSpec as P

HDIM = 64
BLOCK = 128
EPS = 1e-05
ROPE_BASE = 100000.0
NEG_FILL = -1e30
F32 = jnp.float32
BF16 = jnp.bfloat16
VMEM_LIMIT = 56 * 1024 * 1024


def dot(a, b, ca, cb):
    return lax.dot_general(a, b, (((ca,), (cb,)), ((), ())), preferred_element_type=F32)


def live_mask(qpos, start, p):
    kpos = p * BLOCK + lax.broadcasted_iota(jnp.int32, (BLOCK, BLOCK), 0)
    return (kpos <= qpos) & (kpos >= start)


STEP = 2
FWD_STEP = 3


def pick(kv_ref, kvat, mb, qpos, start, b, t, share, size):
    nq = kv_ref.shape[2]
    blocks = [b - size * t - i for i in range(size)]
    slots = [kvat[mb, jnp.maximum(p, 0)] for p in blocks]
    at = [(lax.div(s, nq), lax.rem(s, nq)) for s in slots]
    ok = jnp.concatenate([live_mask(qpos, start, p) for p in blocks], axis=0)

    def keys(g):
        rows = slice(g * HDIM, (g + 1) * HDIM)
        return jnp.concatenate([kv_ref[d, 0, s, rows, :] for d, s in at], axis=1)

    return keys, at, jnp.concatenate([ok] * share, axis=1)


def fwd_kernel(groups, share, info, kvat, q_ref, start_ref, kv_ref, o_ref, lse_ref, qs, m_s, l_s, acc, s_s, w_s):
    mb, i = pl.program_id(0), pl.program_id(1)
    lo, b = info[mb, 0, i], info[mb, 1, i]
    nq = kv_ref.shape[2]
    lanes = share * BLOCK
    for g in range(groups):
        for h in range(share):
            at = (g * share + h) * HDIM
            qs[g, :, h * BLOCK : (h + 1) * BLOCK] = q_ref[at : at + HDIM, :]
    m_s[...] = jnp.full_like(m_s, NEG_FILL)
    l_s[...] = jnp.zeros_like(l_s)
    acc[...] = jnp.zeros_like(acc)
    qpos = b * BLOCK + lax.broadcasted_iota(jnp.int32, (1, BLOCK), 1)
    start = start_ref[...]

    def step(t, carry):
        keys, at, ok = pick(kv_ref, kvat, mb, qpos, start, b, t, share, FWD_STEP)
        for g in range(groups):
            s_s[g] = jnp.where(ok, dot(keys(g), qs[g], 0, 0), NEG_FILL)
        alphas = []
        for g in range(groups):
            s = s_s[g]
            m_old = m_s[g]
            m_new = jnp.maximum(m_old, jnp.max(s, axis=0, keepdims=True))
            w = jnp.exp(s - m_new)
            alpha = jnp.exp(m_old - m_new)
            l_s[g] = l_s[g] * alpha + jnp.sum(w, axis=0, keepdims=True)
            m_s[g] = m_new
            w_s[g] = w.astype(BF16)
            alphas.append(alpha)
        for g in range(groups):
            acc[g] = acc[g] * alphas[g] + dot(keys(groups + g), w_s[g], 1, 0)
        return carry

    lax.fori_loop(0, (b - lo + FWD_STEP) // FWD_STEP, step, 0)
    for g in range(groups):
        total = l_s[g]
        out = (acc[g] / total).astype(BF16)
        for h in range(share):
            at = (g * share + h) * HDIM
            o_ref[at : at + HDIM, :] = out[:, h * BLOCK : (h + 1) * BLOCK]
        lse_ref[0, g : g + 1, :] = m_s[g] + jnp.log(total)


def attention_fwd(info, kvat, q_t, start, kv):
    width = q_t.shape[0]
    n, micro, nq, kvw, _ = kv.shape
    groups = kvw // HDIM // 2
    share = width // HDIM // groups
    lanes = share * BLOCK
    tok = lambda rows: pl.BlockSpec((rows, BLOCK), lambda m, i, *_: (0, m * nq + i))
    return pl.pallas_call(
        functools.partial(fwd_kernel, groups, share),
        grid_spec=pltpu.PrefetchScalarGridSpec(
            num_scalar_prefetch=2,
            grid=(micro, nq),
            in_specs=[
                tok(width),
                tok(1),
                pl.BlockSpec((n, 1, nq, kvw, BLOCK), lambda m, i, *_: (0, m, 0, 0, 0)),
            ],
            out_specs=[
                tok(width),
                pl.BlockSpec((1, groups, lanes), lambda m, i, *_: (m * nq + i, 0, 0)),
            ],
            scratch_shapes=[
                pltpu.VMEM((groups, HDIM, lanes), BF16),
                pltpu.VMEM((groups, 1, lanes), F32),
                pltpu.VMEM((groups, 1, lanes), F32),
                pltpu.VMEM((groups, HDIM, lanes), F32),
                pltpu.VMEM((groups, FWD_STEP * BLOCK, lanes), F32),
                pltpu.VMEM((groups, FWD_STEP * BLOCK, lanes), BF16),
            ],
        ),
        out_shape=[
            jax.ShapeDtypeStruct(q_t.shape, BF16),
            jax.ShapeDtypeStruct((micro * nq, groups, lanes), F32),
        ],
        compiler_params=pltpu.CompilerParams(vmem_limit_bytes=VMEM_LIMIT),
        cost_estimate=pl.CostEstimate(
            flops=int(1e10), bytes_accessed=int(8e6), transcendentals=int(8e6)
        ),
        name="attention_fwd",
    )(info, kvat, q_t, start, kv)


def bwd_kernel(
    groups, share, info, kvat, q_ref, do_ref, o_ref, lse_ref, start_ref, cos_ref, sin_ref, kv_ref,
    dq_ref, dkv_ref, qs, dos, delta, dq, dkv, s_s, d_s, w_s, ds_s,
):
    mb, i = pl.program_id(0), pl.program_id(1)
    lo, b = info[mb, 0, i], info[mb, 1, i]
    nq = kv_ref.shape[2]

    @pl.when(i == 0)
    def _():
        dkv[...] = jnp.zeros_like(dkv)

    for g in range(groups):
        for h in range(share):
            at = (g * share + h) * HDIM
            cols = slice(h * BLOCK, (h + 1) * BLOCK)
            d_out = do_ref[at : at + HDIM, :]
            qs[g, :, cols] = q_ref[at : at + HDIM, :]
            dos[g, :, cols] = d_out
            delta[g, :, cols] = jnp.sum(
                d_out.astype(F32) * o_ref[at : at + HDIM, :].astype(F32), axis=0, keepdims=True
            )
    dq[...] = jnp.zeros_like(dq)
    qpos = b * BLOCK + lax.broadcasted_iota(jnp.int32, (1, BLOCK), 1)
    start = start_ref[...]

    def step(t, carry):
        keys, at, ok = pick(kv_ref, kvat, mb, qpos, start, b, t, share, STEP)
        for g in range(groups):
            s_s[g] = jnp.where(ok, dot(keys(g), qs[g], 0, 0), NEG_FILL)
            d_s[g] = dot(keys(groups + g), dos[g], 0, 0)
        for g in range(groups):
            w = jnp.exp(s_s[g] - lse_ref[0, g : g + 1, :])
            w_s[g] = w.astype(BF16)
            ds_s[g] = (w * (d_s[g] - delta[g])).astype(BF16)
        for g in range(groups):
            dq[g] += dot(keys(g), ds_s[g], 1, 0)
            dk = dot(qs[g], ds_s[g], 1, 1)
            dv = dot(dos[g], w_s[g], 1, 1)
            krows = slice(g * HDIM, (g + 1) * HDIM)
            vrows = slice((groups + g) * HDIM, (groups + g + 1) * HDIM)
            for i in range(STEP):
                cols = slice(i * BLOCK, (i + 1) * BLOCK)
                dkv[at[i][0], at[i][1], krows, :] += dk[:, cols]
                dkv[at[i][0], at[i][1], vrows, :] += dv[:, cols]
        return carry

    lax.fori_loop(0, (b - lo + STEP) // STEP, step, 0)
    cos, sin = cos_ref[...], sin_ref[...]
    half = HDIM // 2
    for g in range(groups):
        for h in range(share):
            at = (g * share + h) * HDIM
            one = dq[g, :half, h * BLOCK : (h + 1) * BLOCK] * HDIM**-0.5
            two = dq[g, half:, h * BLOCK : (h + 1) * BLOCK] * HDIM**-0.5
            dq_ref[at : at + half, :] = (one * cos + two * sin).astype(BF16)
            dq_ref[at + half : at + HDIM, :] = (two * cos - one * sin).astype(BF16)

    @pl.when(i == nq - 1)
    def _():
        dkv_ref[:, 0] = dkv[...].astype(BF16)


def attention_bwd(info, kvat, q_t, do_t, o_t, lse, start, cos_t, sin_t, kv):
    width = q_t.shape[0]
    n, micro, nq, kvw, _ = kv.shape
    groups = kvw // HDIM // 2
    share = width // HDIM // groups
    lanes = share * BLOCK
    tok = lambda rows: pl.BlockSpec((rows, BLOCK), lambda m, i, *_: (0, m * nq + i))
    keys = pl.BlockSpec((n, 1, nq, kvw, BLOCK), lambda m, i, *_: (0, m, 0, 0, 0))
    return pl.pallas_call(
        functools.partial(bwd_kernel, groups, share),
        grid_spec=pltpu.PrefetchScalarGridSpec(
            num_scalar_prefetch=2,
            grid=(micro, nq),
            in_specs=[
                tok(width),
                tok(width),
                tok(width),
                pl.BlockSpec((1, groups, lanes), lambda m, i, *_: (m * nq + i, 0, 0)),
                tok(1),
                tok(HDIM // 2),
                tok(HDIM // 2),
                keys,
            ],
            out_specs=[tok(width), keys],
            scratch_shapes=[
                pltpu.VMEM((groups, HDIM, lanes), BF16),
                pltpu.VMEM((groups, HDIM, lanes), BF16),
                pltpu.VMEM((groups, 1, lanes), F32),
                pltpu.VMEM((groups, HDIM, lanes), F32),
                pltpu.VMEM((n, nq, kvw, BLOCK), F32),
                pltpu.VMEM((groups, STEP * BLOCK, lanes), F32),
                pltpu.VMEM((groups, STEP * BLOCK, lanes), F32),
                pltpu.VMEM((groups, STEP * BLOCK, lanes), BF16),
                pltpu.VMEM((groups, STEP * BLOCK, lanes), BF16),
            ],
        ),
        out_shape=[
            jax.ShapeDtypeStruct(q_t.shape, BF16),
            jax.ShapeDtypeStruct(kv.shape, BF16),
        ],
        compiler_params=pltpu.CompilerParams(vmem_limit_bytes=VMEM_LIMIT),
        cost_estimate=pl.CostEstimate(
            flops=int(2e10), bytes_accessed=int(16e6), transcendentals=int(8e6)
        ),
        name="attention_bwd",
    )(info, kvat, q_t, do_t, o_t, lse, start, cos_t, sin_t, kv)


CORE, ALONG_X, ALONG_Y = 1, 2, 4
FAR = ALONG_X + ALONG_Y
CUBE = 8
LAG = 2
LAGS = 2
SEM = pltpu.SemaphoreType.DMA


def meet(peers):
    barrier = pltpu.get_barrier_semaphore()
    for peer in peers:
        pl.semaphore_signal(barrier, inc=1, device_id=peer, device_id_type=pl.DeviceIdType.MESH)
    pl.semaphore_wait(barrier, len(peers))


def weight_chunks(shapes, most=160 * 1024):
    chunks = []
    for a, (rows, cols) in enumerate(shapes):
        n = 1
        while rows * cols // n > most and rows % (32 * n) == 0:
            n *= 2
        k = 1
        while rows // n * cols // k > most and cols % (256 * k) == 0:
            k *= 2
        for i in range(n):
            lo, hi = rows // n * i, rows // n * (i + 1)
            mid = lo + -(-(hi - lo) // 32) * 16
            for j in range(k):
                c = pl.ds(cols // k * j, cols // k)
                chunks.append((a, (pl.ds(lo, mid - lo), c), (pl.ds(mid, hi - mid), c)))
    return chunks


def pieces_of(total, size):
    return [(lo, min(size, total - lo)) for lo in range(0, total, size)]


def start_kernel(chunks, micro, *refs):
    refs = list(refs)
    take_refs = lambda n: [refs.pop(0) for _ in range(n)]
    ins = take_refs(6)
    far_x, far_ct, gain_ref, cos_ref, sin_ref = take_refs(5)
    outs = take_refs(6)
    far_q, far_xn, far_kv, far_x_tok, far_ct_tok = take_refs(5)
    near_w = take_refs(2)
    x, ct, x_tok, ct_tok, xn, q_s, own_kv, sent, came, local = take_refs(10)
    at, row = lax.axis_index("wide"), lax.axis_index("narrow")
    peer = {bit: (at ^ bit, row) for bit in (CORE, ALONG_X, ALONG_Y)}
    peer["row"] = (at, row ^ 1)
    keys = len(ins)
    source = [*ins, own_kv]
    land = [*near_w, *outs[2:], far_kv]
    n = len(chunks)
    kd = own_kv.shape[2] // 2
    nq = own_kv.shape[1]
    width, half = q_s.shape[0], HDIM // 2

    mine_in = [pltpu.make_async_copy(ins[i], near_w[i].at[at], local.at[i]) for i in range(2)]
    give = [pltpu.make_async_copy(near_w[i], outs[i], local.at[2 + i]) for i in range(2)]
    give_q = pltpu.make_async_copy(q_s, far_q, local.at[4])
    give_xn = pltpu.make_async_copy(xn, far_xn, local.at[5])
    give_kv = pltpu.make_async_copy(own_kv, far_kv.at[at], local.at[6])
    give_x = pltpu.make_async_copy(x_tok, far_x_tok, local.at[7])
    give_ct = pltpu.make_async_copy(ct_tok, far_ct_tok, local.at[8])
    each = x.shape[2] // micro
    halves_of = lambda far, near, first: [
        pltpu.make_async_copy(far.at[m], near.at[:, :, pl.ds(m * each, each)], local.at[first + m])
        for m in range(micro)
    ]
    x_in, ct_in = halves_of(far_x, x, 9), halves_of(far_ct, ct, 9 + micro)

    def norm():
        for r in x_in:
            r.wait()
        count, high, tokens = x.shape
        square = jnp.zeros((1, tokens), F32)
        for j in range(count):
            v = x[j].astype(F32)
            square += jnp.sum(v * v, axis=0, keepdims=True)
        rr = lax.rsqrt(square / width + EPS)
        gain = jnp.broadcast_to(gain_ref[...], (BLOCK, width)).T
        for j in range(count):
            xn[j] = (x[j].astype(F32) * rr * gain[j * high : (j + 1) * high, 0:1]).astype(BF16)
        give_xn.start()

    def by_token(near, tok, copies, out):
        for r in copies:
            r.wait()
        for lo in range(0, tok.shape[0], BLOCK):
            tok[lo : lo + BLOCK, :] = near[:, :, lo : lo + BLOCK].astype(F32).reshape(width, BLOCK).T.astype(BF16)
        out.start()

    def turned(w, lo, size):
        return sum(dot(w[j, :, lo : lo + size], xn[j], 0, 0) for j in range(w.shape[0]))

    def heads(got):
        cos, sin = cos_ref[...], sin_ref[...]
        for h in range(0, got.shape[0], HDIM):
            one, two = got[h : h + half], got[h + half : h + HDIM]
            yield h, one * cos - two * sin
            yield h + half, two * cos + one * sin

    def to_keys(at_row, value):
        value = value.astype(BF16)
        for m in range(micro):
            for i in range(nq):
                lanes = slice((m * nq + i) * BLOCK, (m * nq + i + 1) * BLOCK)
                own_kv[m, i, at_row : at_row + value.shape[0], :] = value[:, lanes]

    def key_tile(lo, size):
        got = turned(near_w[1], lo, size)
        turn_to = max(0, min(kd - lo, size))
        for h, v in heads(got[:turn_to]):
            to_keys(lo + h, v)
        if turn_to < size:
            to_keys(lo + turn_to, got[turn_to:])

    def query_tile(lo, size):
        for h, v in heads(turned(near_w[0], lo, size)):
            q_s[lo + h : lo + h + half, :] = v.astype(BF16) * HDIM**-0.5

    def run(mine):
        other = 1 - mine
        used = [0] * n
        begun = []

        def part(ref, c, which):
            return ref.at[chunks[c][1 + which]]

        def copy(c, m, which, way, slot):
            a = chunks[c][0]
            there = part(land[a].at[at ^ m], c, which)
            return pltpu.make_async_remote_copy(
                src_ref=there if m else part(source[a], c, which),
                dst_ref=there,
                send_sem=sent.at[c, slot],
                recv_sem=came.at[c, m if way == "row" else m ^ way, which],
                device_id=peer[way],
                device_id_type=pl.DeviceIdType.MESH,
            )

        def push(c, m, which, way):
            r = copy(c, m, which, way, used[c])
            used[c] += 1
            r.start()
            begun.append(r)

        def take(c, m, which, *ways):
            copy(c, m ^ CORE, which, CORE, 0).wait_recv()
            for way in ways:
                push(c, m, which, way)

        planes = [c[0] != keys for c in chunks]
        bounced = [1 < c[0] < keys for c in chunks]
        lean = [planes[c] and c % 2 == 1 for c in range(n)]

        def first(c):
            push(c, 0, mine, ALONG_X)
            push(c, 0, mine, ALONG_Y)
            if not planes[c]:
                push(c, 0, other, ALONG_X)
                push(c, 0, other, ALONG_Y)

        def second(c):
            if lean[c]:
                over_x = c % 4 == 1
                take(c, ALONG_Y, mine, *((ALONG_X,) if over_x else ()), "row", CORE)
                take(c, ALONG_X, mine, *(() if over_x else (ALONG_Y,)), "row", CORE)
            elif planes[c]:
                take(c, ALONG_Y, mine, ALONG_X, CORE)
                push(c, 0, other, ALONG_Y)
                take(c, ALONG_X, mine, "row", CORE)
            else:
                take(c, ALONG_X, mine, ALONG_Y, CORE)
                take(c, ALONG_Y, other, ALONG_X, CORE)
                take(c, ALONG_Y, mine, CORE)
                take(c, ALONG_X, other, CORE)
            push(c, 0, 0, CORE)
            push(c, 0, 1, CORE)

        def third(c):
            take(c, FAR, mine, *(("row", CORE) if planes[c] else (CORE,)))
            if planes[c]:
                take(c, ALONG_Y, other, CORE)
                take(c, ALONG_X, other, CORE)
            else:
                take(c, FAR, other, CORE)

        def fourth(c):
            if planes[c]:
                take(c, FAR, other, CORE)

        def fifth(c):
            for which in range(2):
                take(c, CORE, which, *((CORE,) if bounced[c] else ()))
            for m in (ALONG_X, ALONG_Y, FAR):
                for which in range(2):
                    take(c, m + CORE, which)

        def sixth(c):
            if bounced[c]:
                for which in range(2):
                    take(c, 0, which)

        steps = (first, second, third, fourth, fifth, sixth)
        begins, ready = [], 0
        for c in range(n):
            begins.append(c)
            if chunks[c][0] < 2:
                ready = c + LAG * 4
            if chunks[c][0] == keys:
                begins[c] = max(begins[c - 1] + 1, ready + 1)
        work = {1: [norm], ready: []}
        work[2] = [functools.partial(by_token, x, x_tok, (), give_x)]
        work[3] = [functools.partial(by_token, ct, ct_tok, ct_in, give_ct)]
        for lo, size in pieces_of(2 * kd, 256):
            work[ready].append(functools.partial(key_tile, lo, size))
        work[ready].append(give_kv.start)
        for i, (lo, size) in enumerate(pieces_of(width, 256)):
            work[ready + 2 + i] = [functools.partial(query_tile, lo, size)]
        for t in range(begins[-1] + LAG * (len(steps) - 1) + 1):
            for s, step in enumerate(steps):
                for c in range(n):
                    if begins[c] + LAG * s == t:
                        step(c)
            if t == ready:
                for r in mine_in:
                    r.wait()
                for r in give:
                    r.start()
            for job in work.get(t, ()):
                job()
        for r in begun:
            r.wait_send()

    for r in (*x_in, *mine_in, *ct_in):
        r.start()
    meet(list(peer.values()))
    for mine in range(2):
        pl.when(row % 2 == mine)(functools.partial(run, mine))
    give_q.start()
    for r in (*give, give_q, give_xn, give_kv, give_x, give_ct):
        r.wait()


def start_of(weights, x, ct, gain, cos, sin, collective_id):
    micro, count, high, each = x.shape
    tokens, width = micro * each, count * high
    kd = weights[1].shape[1] // 2
    nq = each // BLOCK
    chunks = weight_chunks([a.shape for a in weights])
    keys = len(weights)
    for m in range(micro):
        for i in range(2):
            rows = pl.ds(kd * i, kd)
            halves = [(m, pl.ds(nq // 2 * h, nq // 2), rows) for h in range(2)]
            chunks.append((keys, *halves))
    anywhere = pl.BlockSpec(memory_space=pl.ANY)
    vmem = pl.BlockSpec(memory_space=pltpu.VMEM)
    shape = jax.ShapeDtypeStruct
    kv = (micro, nq, 2 * kd, BLOCK)
    split = pltpu.VMEM((count, high, tokens), BF16)
    by_token = pltpu.VMEM((tokens, width), BF16)
    got = pl.pallas_call(
        functools.partial(start_kernel, chunks, micro),
        in_specs=[anywhere] * (keys + 2) + [vmem] * 3,
        out_specs=[anywhere] * (keys + 5),
        out_shape=[shape((count,) + a.shape, BF16) for a in weights]
        + [shape((width, tokens), BF16), shape((count, high, tokens), BF16), shape((count,) + kv, BF16)]
        + [shape((tokens, width), BF16)] * 2,
        scratch_shapes=[pltpu.VMEM((count,) + a.shape, BF16) for a in weights[:2]]
        + [split, split, by_token, by_token, split, pltpu.VMEM((width, tokens), BF16), pltpu.VMEM(kv, BF16)]
        + [SEM((len(chunks), 16)), SEM((len(chunks), 8, 2)), SEM((9 + 2 * micro,))],
        compiler_params=pltpu.CompilerParams(
            collective_id=collective_id, has_side_effects=True, vmem_limit_bytes=VMEM_LIMIT
        ),
        name="gather_and_project",
    )(*weights, x, ct, gain, cos, sin)
    return got[:keys], *got[keys:]


class Unit:
    def __init__(self, source, target, out, rows, cols, first):
        self.source, self.target, self.out = source, target, out
        self.rows, self.cols, self.first = rows, cols, first

    @property
    def shape(self):
        return (self.rows[1], self.cols[1])


def weight_units(sizes, most, units=()):
    units = list(units)
    for source, target, out, rows, cols in sizes:
        k = 1
        while cols % (256 * k) == 0 and rows * cols // k > most:
            k *= 2
        high = -(-rows // max(1, round(rows * cols / k / most)) // 16) * 16
        cols_cuts = pieces_of(cols, cols // k)
        if out == sizes[-1][2] and cols % BLOCK == 0:
            lo, size = cols_cuts.pop()
            while size > BLOCK:
                part = -(-size // (2 * BLOCK)) * BLOCK
                cols_cuts.append((lo, part))
                lo, size = lo + part, size - part
            cols_cuts.append((lo, size))
        for rows_cut in pieces_of(rows, high):
            for cols_cut in cols_cuts:
                first = (ALONG_X, ALONG_Y)[len(units) % 2]
                units.append(Unit(source, target, out, rows_cut, cols_cut, first))
    return units


RING = 3


def ring_sizes(units):
    shapes = [u.shape for u in units if u.source is not None]
    return {a: min(RING, shapes.count(a)) for a in shapes}


def sum_scratch(units, tokens):
    n = len(units)
    room = lambda *lead: [pltpu.VMEM(lead + u.shape, BF16) for u in units]
    line = [pltpu.VMEM((2,) + u.shape if u.source is not None else (8, BLOCK), BF16) for u in units]
    rows = max(u.shape[0] for u in units if u.source is not None)
    scratch = room(4) + room(4) + room(2) + room() + line
    scratch += [pltpu.VMEM((8 * rows, tokens), BF16)]
    scratch += [pltpu.VMEM((d, 4) + a, BF16) for a, d in ring_sizes(units).items()]
    return scratch + [SEM((n, 5)), SEM((n, 5)), SEM((n,)), SEM((n, 4)), SEM((n, 4)), SEM((n, 4))]


class Sums:
    def __init__(self, units, take, outs, source, product, far_keys=None, keys_done=None):
        n = len(units)
        self.units, self.outs, self.source, self.product = units, outs, source, product
        self.far_keys, self.keys_done = far_keys, keys_done
        self.held, self.core_in, self.one_in, self.two_in, self.line_in = (take(n) for _ in range(5))
        self.lhs = take(1)[0]
        self.depth = ring_sizes(units)
        self.rings = dict(zip(self.depth, take(len(self.depth))))
        self.sent, self.came, self.stored, self.key_load, self.key_sent, self.key_came = take(6)
        self.at, self.row = lax.axis_index("wide"), lax.axis_index("narrow")
        self.way = {bit: (self.at ^ bit, self.row) for bit in (CORE, ALONG_X, ALONG_Y)}
        self.near, self.across = (self.at, self.row ^ 1), (self.at, self.row ^ 3)
        self.middle = (self.row == 1) | (self.row == 2)
        self.is_keys = [u.source is None for u in units]
        self.steps = (self.s0, self.s1, self.s2, self.s3, self.s4, self.s5, self.s6)

    def meet(self):
        meet([*self.way.values(), self.near, self.across])

    def send(self, c, slot, a, b, to):
        return pltpu.make_async_remote_copy(
            src_ref=a, dst_ref=b, send_sem=self.sent.at[c, slot], recv_sem=self.came.at[c, slot],
            device_id=to, device_id_type=pl.DeviceIdType.MESH,
        )

    @staticmethod
    def add(dst, other):
        dst[...] = dst[...] + other[...]

    def order(self, c):
        first = self.units[c].first
        return (0, FAR - first, first, FAR)

    def slot_of(self, c):
        shape = self.units[c].shape
        alike = [i for i, u in enumerate(self.units) if u.source is not None and u.shape == shape]
        return alike.index(c) % self.depth[shape]

    def same_slot(self, i, c):
        if self.is_keys[i] or self.is_keys[c] or self.units[i].shape != self.units[c].shape:
            return False
        return self.slot_of(i) == self.slot_of(c)

    def core_copies(self, c):
        u = self.units[c]
        if not self.is_keys[c]:
            return [self.send(c, 0, self.rings[u.shape].at[self.slot_of(c)], self.core_in[c], self.way[CORE])]
        return [
            pltpu.make_async_remote_copy(
                src_ref=self.far_keys.at[self.at ^ CORE ^ m, pl.ds(*u.rows)], dst_ref=self.core_in[c].at[i],
                send_sem=self.key_sent.at[c, i], recv_sem=self.key_came.at[c, i],
                device_id=self.way[CORE], device_id_type=pl.DeviceIdType.MESH,
            )
            for i, m in enumerate(self.order(c))
        ]

    def key_loads(self, c):
        rows = pl.ds(*self.units[c].rows)
        return [
            pltpu.make_async_copy(self.far_keys.at[self.at ^ m, rows], self.held[c].at[i], self.key_load.at[c, i])
            for i, m in enumerate(self.order(c))
        ]

    def first_copy(self, c):
        return self.send(c, 1, self.held[c].at[pl.ds(2, 2)], self.one_in[c], self.way[self.units[c].first])

    def second_copy(self, c):
        return self.send(c, 2, self.held[c].at[1], self.two_in[c], self.way[FAR - self.units[c].first])

    def inward(self, c):
        return self.send(c, 3, self.held[c].at[0], self.line_in[c].at[0], self.near)

    def over(self, c):
        return self.send(c, 4, self.held[c].at[0], self.line_in[c].at[1], self.across)

    def outward(self, c):
        return self.send(c, 3, self.line_in[c].at[1], self.line_in[c].at[0], self.near)

    def store(self, c, slot):
        u = self.units[c]
        cut = (pl.ds(*u.rows), pl.ds(*u.cols))
        return pltpu.make_async_copy(self.line_in[c].at[slot], self.outs[u.out].at[cut], self.stored.at[c])

    def products(self, c):
        u = self.units[c]
        rows, cols = u.shape
        for i, core in enumerate((CORE, 0)):
            for k, m in enumerate(self.order(c)):
                self.lhs[pl.ds((4 * i + k) * rows, rows), :] = self.source(u, self.at ^ m ^ core)
        a = self.lhs[pl.ds(0, 8 * rows), :]
        for lo, size in pieces_of(cols, 256):
            got = self.product(u, a, u.cols[0] + lo, size).astype(BF16).reshape(8, rows, size)
            self.rings[u.shape][self.slot_of(c), :, :, lo : lo + size] = got[:4]
            self.held[c][:, :, lo : lo + size] = got[4:]

    def s0(self, c):
        if self.is_keys[c]:
            for r in self.core_copies(c) + self.key_loads(c):
                r.start()
            return
        before = [i for i in range(c) if self.same_slot(i, c)]
        if before:
            self.core_copies(before[-1])[0].wait_send()
        self.products(c)
        self.core_copies(c)[0].start()

    def s1(self, c):
        if self.is_keys[c]:
            for r in self.key_loads(c):
                r.wait()
        for r in self.core_copies(c):
            r.wait_recv()
        for i in (2, 3, 0, 1):
            self.add(self.held[c].at[i], self.core_in[c].at[i])
            if i == 3:
                self.first_copy(c).start()

    def s2(self, c):
        self.first_copy(c).wait_recv()
        self.add(self.held[c].at[1], self.one_in[c].at[1])
        self.second_copy(c).start()
        self.add(self.held[c].at[0], self.one_in[c].at[0])

    def s3(self, c):
        self.second_copy(c).wait_recv()
        self.add(self.held[c].at[0], self.two_in[c])
        if self.is_keys[c]:
            self.keys_done(c, self.held[c].at[0])
        else:
            pl.when(~self.middle)(lambda: self.inward(c).start())

    def s4(self, c):
        @pl.when(self.middle)
        def _():
            self.inward(c).wait_recv()
            self.add(self.held[c].at[0], self.line_in[c].at[0])
            self.over(c).start()

    def s5(self, c):
        @pl.when(self.middle)
        def _():
            self.over(c).wait_recv()
            self.add(self.line_in[c].at[1], self.held[c].at[0])
            self.outward(c).start()
            self.store(c, 1).start()

    def s6(self, c):
        @pl.when(~self.middle)
        def _():
            self.outward(c).wait_recv()
            self.store(c, 0).start()

    def finish(self):
        n = len(self.units)
        for c in range(n):
            if not any(self.same_slot(c, i) for i in range(c + 1, n)):
                for r in self.core_copies(c):
                    r.wait_send()
            self.first_copy(c).wait_send()
            self.second_copy(c).wait_send()
            if not self.is_keys[c]:
                self.inward(c).wait_send()
                pl.when(self.middle)(lambda: self.over(c).wait_send())
                self.store(c, 0).wait()

    def run(self, begins, work):
        last = max(b + LAGS * (len(self.steps) - 1) for b in begins)
        for t in range(max([last, *work]) + 1):
            for s, step in enumerate(self.steps):
                for c, b in enumerate(begins):
                    if b + LAGS * s == t and not (self.is_keys[c] and s > 3):
                        step(c)
            for job in work.get(t, ()):
                job()


TILE = 256


def ffn_kernel(units, *refs):
    refs = list(refs)
    take = lambda n: [refs.pop(0) for _ in range(n)]
    far_att, far_x, far_ct, far_out_w, far_gate_w, far_up_w, far_down_w, gain_ref = take(8)
    far_out, far_res, far_do, far_hn, far_d_up, far_d_attn, gain_sum = take(7)
    outs = take(2)
    att, x, ct, out_w, wg, wu, wd, res, hn, hn_t, hid_t, d_gate, d_up, out_acc, hn_acc = take(15)
    load, give = take(2)
    do, d_attn = att, hn
    width, tokens = att.shape
    ff = hid_t.shape[0]
    tiles = ff // TILE
    slots = range(0, tokens, BLOCK)
    loads = [
        pltpu.make_async_copy(a, b, load.at[i])
        for i, (a, b) in enumerate(
            zip(
                (far_att, far_out_w, far_x, far_gate_w, far_up_w, far_down_w, far_ct),
                (att, out_w, x, wg, wu, wd, ct),
            )
        )
    ]
    gives = [
        pltpu.make_async_copy(a, b, give.at[i])
        for i, (a, b) in enumerate(
            ((x, far_out), (res, far_res), (do, far_do), (hn_t, far_hn), (d_up, far_d_up), (d_attn, far_d_attn))
        )
    ]

    def attend():
        for r in loads[:3]:
            r.wait()
        for lo in slots:
            cut = slice(lo, lo + BLOCK)
            r = x[cut, :].astype(F32) + dot(att[:, cut], out_w[...], 0, 0)
            res[cut, :] = r
            rr = lax.rsqrt(jnp.mean(r * r, axis=1, keepdims=True) + EPS)
            h = r * rr * gain_ref[...]
            hn[cut, :] = h.astype(BF16)
            h = h.T
            high = hn_t.shape[1]
            for j in range(hn_t.shape[0]):
                hn_t[j, :, cut] = h[j * high : (j + 1) * high].astype(BF16)
        gives[3].start()

    def hidden_tile(i):
        cut = slice(i * TILE, (i + 1) * TILE)
        gate, up = dot(hn[...], wg[:, cut], 1, 0), dot(hn[...], wu[:, cut], 1, 0)
        hidden = (gate / (1.0 + jnp.exp(-gate)) * up).astype(BF16)
        hid_t[cut, :] = hidden.T

    def back_tile(i):
        cut = slice(i * TILE, (i + 1) * TILE)
        gate, up = dot(hn[...], wg[:, cut], 1, 0), dot(hn[...], wu[:, cut], 1, 0)
        sg = 1.0 / (1.0 + jnp.exp(-gate))
        act = gate * sg
        hidden = (act * up).astype(BF16)
        d_hidden = dot(ct[...], wd[cut, :], 1, 1)
        d_gate[:, cut] = (d_hidden * up * sg * (1.0 + gate * (1.0 - sg))).astype(BF16)
        d_up[:, cut] = (d_hidden * act).astype(BF16)
        forward = dot(hidden, wd[cut, :], 1, 0)
        back = dot(d_gate[:, cut], wg[:, cut], 1, 1) + dot(d_up[:, cut], wu[:, cut], 1, 1)
        if i == 0:
            out_acc[...] = forward
            hn_acc[...] = back
        else:
            out_acc[...] += forward
            hn_acc[...] += back

    def residual():
        gives[4].start()
        total = jnp.zeros(gain_sum.shape, F32)
        for lo in slots:
            cut = slice(lo, lo + BLOCK)
            r, d = res[cut, :], hn_acc[cut, :]
            rr = lax.rsqrt(jnp.mean(r * r, axis=1, keepdims=True) + EPS)
            total += jnp.sum(d * r * rr, axis=0, keepdims=True)
            u = d * gain_ref[...]
            x[cut, :] = (r + out_acc[cut, :]).astype(BF16)
            mean = jnp.mean(u * r, axis=1, keepdims=True)
            d = ct[cut, :].astype(F32) + rr * u - r * (rr * rr * rr * mean)
            res[cut, :] = d
            d_attn[cut, :] = d.astype(BF16)
            do[:, cut] = dot(out_w[...], d_attn[cut, :], 1, 1).astype(BF16)
        gain_sum[...] = total
        for i in (0, 1, 2, 5):
            gives[i].start()

    def source(u, device):
        lo, size = u.rows
        if u.source == 0:
            per = ff // CUBE
            return hid_t[pl.ds(pl.multiple_of(device * per + lo, 16), size), :]
        return hn_t[device, pl.ds(lo, size), :]

    def product(u, a, lo, size):
        b = ct if u.target == 0 else d_gate
        return dot(a, b[:, pl.ds(lo, size)], 1, 0)

    sums = Sums(units, take, outs, source, product)
    for r in loads:
        r.start()
    sums.meet()
    attend()
    for r in loads[3:5]:
        r.wait()
    for i in range(tiles):
        hidden_tile(i)
    for r in loads[5:]:
        r.wait()
    downs = sum(u.source == 0 for u in units)
    spread = max(1, downs)
    work = {}
    for i in range(tiles):
        work.setdefault(i * spread // tiles, []).append(functools.partial(back_tile, i))
    work.setdefault(spread + 1, []).append(residual)
    begins = [c if c < downs else c for c in range(len(units))]
    sums.run(begins, work)
    sums.finish()
    for r in gives:
        r.wait()


def ffn(att_t, x, ct, g_out, g_gate, g_up, g_down, gain, collective_id, most):
    width, tokens = att_t.shape
    ff = g_gate.shape[1]
    high = width // CUBE
    units = weight_units([(0, 0, 0, ff // CUBE, width), (1, 1, 1, high, ff)], most)
    anywhere = pl.BlockSpec(memory_space=pl.ANY)
    vmem = pl.BlockSpec(memory_space=pltpu.VMEM)
    shape = jax.ShapeDtypeStruct
    by_token, by_width = (tokens, width), (width, tokens)
    return pl.pallas_call(
        functools.partial(ffn_kernel, units),
        in_specs=[anywhere] * 7 + [vmem],
        out_specs=[anywhere] * 6 + [vmem] + [anywhere] * 2,
        out_shape=[
            shape(by_token, BF16), shape(by_token, F32), shape(by_width, BF16),
            shape((CUBE, high, tokens), BF16), shape((tokens, ff), BF16), shape(by_token, BF16),
            shape((1, width), F32), shape((ff // CUBE, width), BF16), shape((high, ff), BF16),
        ],
        scratch_shapes=[
            pltpu.VMEM(by_width, BF16), pltpu.VMEM(by_token, BF16), pltpu.VMEM(by_token, BF16),
            pltpu.VMEM((width, width), BF16), pltpu.VMEM((width, ff), BF16),
            pltpu.VMEM((width, ff), BF16), pltpu.VMEM((ff, width), BF16),
            pltpu.VMEM(by_token, F32), pltpu.VMEM(by_token, BF16),
            pltpu.VMEM((CUBE, high, tokens), BF16), pltpu.VMEM((ff, tokens), BF16),
            pltpu.VMEM((tokens, ff), BF16), pltpu.VMEM((tokens, ff), BF16),
            pltpu.VMEM(by_token, F32), pltpu.VMEM(by_token, F32), SEM((7,)), SEM((6,)),
        ] + sum_scratch(units, tokens),
        compiler_params=pltpu.CompilerParams(
            collective_id=collective_id, has_side_effects=True, vmem_limit_bytes=62 * 1024 * 1024
        ),
        name="feed_forward",
    )(att_t, x, ct, g_out, g_gate, g_up, g_down, gain)


def last_kernel(units, *refs):
    refs = list(refs)
    take = lambda n: [refs.pop(0) for _ in range(n)]
    far = take(6)
    far_keys, far_w, far_x, far_res = *take(1), take(2), *take(2)
    cos_ref, sin_ref, gain_ref, gain_two = take(4)
    outs = take(4)
    far_grad, total = take(2)
    near = take(6)
    xn_t, hn_t, att, dq, d_up, d_attn = near
    dkv, w, x, res, gain_buf = *take(1), take(2), *take(3)
    load, tail_load, gain_sent, gain_came = take(4)
    kd, tokens = dkv.shape[0] // 2, dkv.shape[1]
    loads = [pltpu.make_async_copy(a, b, load.at[i]) for i, (a, b) in enumerate(zip(far, near))]
    tail_loads = [
        pltpu.make_async_copy(a, b, tail_load.at[i])
        for i, (a, b) in enumerate(zip([*far_w, far_x, far_res], [*w, x, res]))
    ]
    give = pltpu.make_async_copy(res, far_grad, tail_load.at[len(tail_loads)])
    ready = set()

    def need(copies, i):
        if (copies is loads, i) not in ready:
            ready.add((copies is loads, i))
            copies[i].wait()

    def source(u, device):
        need(loads, u.source)
        return near[u.source][device, pl.ds(*u.rows), :]

    def product(u, a, lo, size):
        if u.target is None:
            return dot(a, dkv[pl.ds(lo, size), :], 1, 1)
        need(loads, u.target)
        if u.target == 3:
            return dot(a, dq[pl.ds(lo, size), :], 1, 1)
        return dot(a, near[u.target][:, pl.ds(lo, size)], 1, 0)

    def keys_done(c, got):
        lanes = slice(c * BLOCK, (c + 1) * BLOCK)
        cs, sn = cos_ref[:, lanes], sin_ref[:, lanes]
        half = HDIM // 2
        for h in range(0, kd, HDIM):
            one = got[h : h + half, :].astype(F32)
            two = got[h + half : h + HDIM, :].astype(F32)
            dkv[h : h + half, lanes] = (one * cs + two * sn).astype(BF16)
            dkv[h + half : h + HDIM, lanes] = (two * cs - one * sn).astype(BF16)
        dkv[kd:, lanes] = got[kd:, :]

    def input_grad():
        need(loads, 3)
        for i in range(len(tail_loads)):
            need(tail_loads, i)
        sum_one = jnp.zeros(gain_two.shape, F32)
        for lo in range(0, tokens, BLOCK):
            cut = slice(lo, lo + BLOCK)
            d = dot(dq[:, cut], w[0][...], 0, 1)
            d += dot(dkv[:, cut], w[1][...], 0, 1)
            v = x[cut, :].astype(F32)
            rr = lax.rsqrt(jnp.mean(v * v, axis=1, keepdims=True) + EPS)
            sum_one += jnp.sum(d * v * rr, axis=0, keepdims=True)
            u = d * gain_ref[...]
            mean = jnp.mean(u * v, axis=1, keepdims=True)
            res[cut, :] = res[cut, :] + rr * u - v * (rr * rr * rr * mean)
        gain_buf[0, 0:1, :] = sum_one
        gain_buf[0, 1:2, :] = gain_two[...]
        give.start()

    sums = Sums(units, take, outs, source, product, far_keys, keys_done)
    gain_ways = [*sums.way.values(), sums.near, sums.across]

    def gain_copy(i):
        return pltpu.make_async_remote_copy(
            src_ref=gain_buf.at[2 * i], dst_ref=gain_buf.at[2 * i + 1], send_sem=gain_sent.at[i],
            recv_sem=gain_came.at[i], device_id=gain_ways[i], device_id_type=pl.DeviceIdType.MESH,
        )

    def gain_step(i):
        if i:
            gain_copy(i - 1).wait_recv()
            gain_buf[2 * i] = gain_buf[2 * i - 2] + gain_buf[2 * i - 1]
        if i < len(gain_ways):
            gain_copy(i).start()

    for r in loads + tail_loads:
        r.start()
    sums.meet()
    begins, after = [], 0
    for c, u in enumerate(units):
        begins.append(c if not begins else begins[-1] + 1)
        if u.source is None:
            after = begins[-1] + 3 * LAGS + 1
        elif u.target is None:
            begins[-1] = max(begins[-1], after)
    work = {after: [input_grad]}
    for i in range(len(gain_ways) + 1):
        work.setdefault(after + i, []).append(functools.partial(gain_step, i))
    sums.run(begins, work)
    total[...] = gain_buf[2 * len(gain_ways)]
    sums.finish()
    for i in range(len(gain_ways)):
        gain_copy(i).wait_send()
    give.wait()


def last_sums(xn_t, hn_t, att_t, dq, d_up, d_attn, keys, weights, x, d_res, cos, sin, gain, gain_two, collective_id, most):
    count, high, tokens = xn_t.shape
    width, ff = count * high, d_up.shape[1]
    rows = keys.shape[1] * BLOCK // tokens
    units = [
        Unit(None, None, None, (rows * i, rows), (0, BLOCK), (ALONG_X, ALONG_Y)[i % 2])
        for i in range(tokens // BLOCK)
    ]
    units = weight_units(
        [(1, 4, 2, high, ff), (2, 5, 3, high, width), (0, 3, 0, high, width), (0, None, 1, high, rows)], most, units
    )
    anywhere = pl.BlockSpec(memory_space=pl.ANY)
    vmem = pl.BlockSpec(memory_space=pltpu.VMEM)
    shape = jax.ShapeDtypeStruct
    near = (xn_t, hn_t, att_t, dq, d_up, d_attn)
    return pl.pallas_call(
        functools.partial(last_kernel, units),
        in_specs=[anywhere] * 11 + [vmem] * 4,
        out_specs=[anywhere] * 5 + [vmem],
        out_shape=[
            shape((high, width), BF16), shape((high, rows), BF16), shape((high, ff), BF16),
            shape((high, width), BF16), shape((tokens, width), F32), shape((2, width), F32),
        ],
        scratch_shapes=[pltpu.VMEM(a.shape, a.dtype) for a in near]
        + [pltpu.VMEM((rows, tokens), BF16)]
        + [pltpu.VMEM(a.shape, a.dtype) for a in (*weights, x, d_res)]
        + [pltpu.VMEM((11, 2, width), F32), SEM((6,)), SEM((6,)), SEM((5,)), SEM((5,))]
        + sum_scratch(units, tokens),
        compiler_params=pltpu.CompilerParams(
            collective_id=collective_id, has_side_effects=True, vmem_limit_bytes=62 * 1024 * 1024
        ),
        name="last_sums",
    )(*near, keys, *weights, x, d_res, cos, sin, gain, gain_two)


def row_sum(part, size):
    if size != 4:
        return lax.psum(part, "narrow")
    add = lambda a, b: (a.astype(F32) + b.astype(F32)).astype(BF16)
    part = add(part, lax.ppermute(part, "narrow", [(0, 1), (3, 2)]))
    part = add(part, lax.ppermute(part, "narrow", [(1, 2), (2, 1)]))
    back = lax.ppermute(part, "narrow", [(1, 0), (2, 3)])
    at = lax.axis_index("narrow")
    return jnp.where((at == 1) | (at == 2), part, back)


def turn(v, cos, sin):
    heads = v.reshape(-1, 2, HDIM // 2, v.shape[1])
    one, two = heads[:, 0], heads[:, 1]
    return jnp.stack([one * cos - two * sin, two * cos + one * sin], axis=1).reshape(v.shape)


def turn_back(v, cos, sin):
    return turn(v, cos, -sin)


def shards(sizes, tokens, lengths, block_plan, attn_gain, w_query, w_key, w_value, w_out, ffn_gain,
           w_gate, w_up, w_down, cotangent):
    n = sizes["wide"]
    at = lax.axis_index("wide")
    micro, _, slots, width = tokens.shape
    total = micro * slots
    kd = w_key.shape[1]
    ff = w_gate.shape[1]
    nq = slots // BLOCK
    nb = nq * n

    plan = block_plan[:, 0]
    sizes_of = lengths[:, 0]
    docs = sizes_of.shape[1]
    upto = jnp.arange(docs)[:, None] >= jnp.arange(docs)[None, :]
    ends = jnp.sum(jnp.where(upto[None], sizes_of[:, None, :], 0), axis=2)
    own_plan = lax.dynamic_slice_in_dim(plan, at * nq, nq, axis=1)
    position = own_plan[:, :, None] * BLOCK + jnp.arange(BLOCK, dtype=jnp.int32)
    start = jnp.sum(
        jnp.where(position[..., None] >= ends[:, None, None, :], sizes_of[:, None, None, :], 0), axis=3
    )
    info = jnp.stack([start[:, :, 0] // BLOCK, own_plan], axis=1)
    slot_block = jnp.arange(nb, dtype=jnp.int32)
    where_is = jnp.sum(
        jnp.where(plan[:, None, :] == slot_block[None, :, None], slot_block[None, None, :], 0), axis=2
    )
    start = start.reshape(1, total)
    local = position.reshape(1, total) - start
    frequency = ROPE_BASE ** (-2.0 * jnp.arange(HDIM // 2, dtype=F32) / HDIM)
    angles = frequency[:, None] * local.astype(F32)
    cos, sin = jnp.cos(angles), jnp.sin(angles)

    cube = n == CUBE and sizes["narrow"] == 4 and nq % 2 == 0

    x = tokens.reshape(total, width)
    ct = cotangent.reshape(total, width)
    most = 64 * 1024
    high = width // n
    w_kv = jnp.concatenate([w_key, w_value], axis=1)
    weights = (w_query, w_kv, w_out, w_gate, w_up, w_down)
    by_device = lambda a: a.reshape(n, -1, a.shape[1])
    gain_one_row, gain_two_row = attn_gain[None], ffn_gain[None]
    if cube:
        by_width = lambda a: a[:, 0].transpose(0, 2, 1).reshape(micro, n, high, slots)
        got, q_t, xn, kv, x, ct = start_of(
            weights, by_width(tokens), by_width(cotangent), gain_one_row, cos, sin, 2
        )
        g_query, g_kv, g_out, g_gate, g_up, g_down = [a.reshape(-1, a.shape[2]) for a in got]
        att_t, lse = attention_fwd(info, where_is, q_t, start, kv)
        out, d_res, do_t, hn_t, d_up, d_attn, gain_two, s_down, s_gate = ffn(
            att_t, x, ct, g_out, g_gate, g_up, g_down, gain_two_row, 3, 44 * 1024
        )
        dq, dkv = attention_bwd(info, where_is, q_t, do_t, att_t, lse, start, cos, sin, kv)
        s_query, s_kv, s_up, s_out, grad_x, gains = last_sums(
            xn, hn_t, by_device(att_t), dq, d_up, d_attn, dkv.reshape(n, -1, BLOCK),
            (g_query, g_kv), x, d_res, cos, sin, gain_one_row, gain_two, 4, most,
        )
        s_key, s_value = s_kv[:, :kd], s_kv[:, kd:]
    else:
        got = [lax.all_gather(a, "wide", axis=0, tiled=True) for a in weights]
        g_query, g_kv, g_out, g_gate, g_up, g_down = got
        g_key, g_value = g_kv[:, :kd], g_kv[:, kd:]
        x = x.astype(F32)
        rr1 = lax.rsqrt(jnp.mean(x * x, axis=1, keepdims=True) + EPS)
        xn = (x * rr1 * attn_gain).astype(BF16)
        key_t = turn(dot(g_key, xn, 0, 1), cos, sin).astype(BF16)
        value_t = dot(g_value, xn, 0, 1).astype(BF16)
        own_kv = jnp.concatenate([key_t, value_t]).reshape(2 * kd, micro, nq, BLOCK).transpose(1, 2, 0, 3)
        q_t = (turn(dot(g_query, xn, 0, 1), cos, sin).astype(BF16) * HDIM**-0.5).astype(BF16)
        kv = lax.all_gather(own_kv, "wide", axis=0)
        att_t, lse = attention_fwd(info, where_is, q_t, start, kv)

        res = x + dot(att_t, g_out, 0, 0)
        rr2 = lax.rsqrt(jnp.mean(res * res, axis=1, keepdims=True) + EPS)
        hn = (res * rr2 * ffn_gain).astype(BF16)
        gate, up = dot(hn, g_gate, 1, 0), dot(hn, g_up, 1, 0)
        sg = 1.0 / (1.0 + jnp.exp(-gate))
        hidden = (gate * sg * up).astype(BF16)
        out = (res + dot(hidden, g_down, 1, 0)).astype(BF16)
        d_hidden = dot(ct, g_down, 1, 1)
        d_gate = (d_hidden * up * sg * (1.0 + gate * (1.0 - sg))).astype(BF16)
        d_up = (d_hidden * gate * sg).astype(BF16)
        d_hn = dot(d_gate, g_gate, 1, 1) + dot(d_up, g_up, 1, 1)
        u = d_hn * ffn_gain
        mean = jnp.mean(u * res, axis=1, keepdims=True)
        d_res = ct.astype(F32) + rr2 * u - res * rr2**3 * mean
        gain_two = jnp.sum(d_hn * res * rr2, axis=0)
        d_attn = d_res.astype(BF16)
        do_t = dot(g_out, d_attn, 1, 1).astype(BF16)

        dq, dkv = attention_bwd(info, where_is, q_t, do_t, att_t, lse, start, cos, sin, kv)
        dkv = lax.psum_scatter(dkv, "wide", scatter_dimension=0).transpose(2, 0, 1, 3).reshape(2 * kd, total)
        dk = turn_back(dkv[:kd].astype(F32), cos, sin).astype(BF16)
        dv = dkv[kd:]
        d_xn = dot(dq, g_query, 0, 1) + dot(dk, g_key, 0, 1) + dot(dv, g_value, 0, 1)
        u = d_xn * attn_gain
        grad_x = d_res + rr1 * u - x * rr1**3 * jnp.mean(u * x, axis=1, keepdims=True)
        gain_one = jnp.sum(d_xn * x * rr1, axis=0)
        gains = lax.psum(jnp.stack([gain_one, gain_two]), ("wide", "narrow"))

        def row_part(source, target, ca, cb):
            part = dot(source, target, ca, cb).astype(BF16)
            own = lax.psum_scatter(part, "wide", scatter_dimension=0, tiled=True)
            return row_sum(own, sizes["narrow"])

        s_query, s_key, s_value = row_part(xn, dq, 0, 1), row_part(xn, dk, 0, 1), row_part(xn, dv, 0, 1)
        s_out, s_down = row_part(att_t, d_attn, 1, 0), row_part(hidden, ct, 0, 0)
        s_gate, s_up = row_part(hn, d_gate, 0, 0), row_part(hn, d_up, 0, 0)

    shape = (micro, 1, slots, width)
    wide_out = lambda a: a.astype(F32)
    return (
        out.reshape(shape),
        grad_x.reshape(shape),
        gains[0],
        wide_out(s_query),
        wide_out(s_key),
        wide_out(s_value),
        wide_out(s_out),
        gains[1],
        wide_out(s_gate),
        wide_out(s_up),
        wide_out(s_down),
    )


def solution(mesh):
    by_slot = P(None, "narrow", "wide", None)
    by_row = P(None, "narrow", None)
    split = P("wide", None)
    in_specs = (
        by_slot, by_row, by_row, P(), split, split, split, split, P(), split, split, split, by_slot,
    )
    out_specs = (
        by_slot, by_slot, P(), split, split, split, split, P(), split, split, split,
    )
    return jax.shard_map(
        functools.partial(shards, dict(mesh.shape)),
        mesh=mesh,
        in_specs=in_specs,
        out_specs=out_specs,
        check_vma=False,
    )
```
